256 devices in a mesh: gx: 8 (over x, z_hi), gy: 32 (over y, z_lo, core).
Axes of the slice: x: 4, y: 4, z: 8 (z_hi: 2, z_lo: 4; z = z_hi * 4 + z_lo), core: 2. Of those that a mesh axis runs over, the one named last changes fastest.
Arguments:
- positions: float32 [48, 32, 3, 128], P('gx', 'gy'), may hold values from 0 to 288, as said below
- species: int32 [48, 32, 128], P('gx', 'gy'), may hold values from 0 to 88
- pair_codes: int32 [8, 32, 26], P('gx', 'gy'), may hold values from 0 to 53, as said below
- pair_count: int32 [8, 32], P('gx', 'gy'), may hold values from 1 to 26, as said below
- embed_table: bfloat16 [89, 128], replicated, may hold values from -6 to 6
- scalar_radial_one: float32 [4, 128], replicated, may hold values from -6 to 6
- vector_radial_one: float32 [4, 128], replicated, may hold values from -6 to 6
- scalar_radial_two: float32 [4, 128], replicated, may hold values from -6 to 6
- vector_radial_two: float32 [4, 128], replicated, may hold values from -6 to 6
- mixing_scalar_one: bfloat16 [128, 128], replicated, may hold values from -0.5 to 0.5
- mixing_vector_one: bfloat16 [128, 128], replicated, may hold values from -0.5 to 0.5
- mixing_two: bfloat16 [128, 128], replicated, may hold values from -0.5 to 0.5
- readout: float32 [128], replicated, may hold values from -0.5 to 0.5
Outputs:
- atom_energy: float32 [48, 32, 128], P('gx', 'gy')
- forces: float32 [48, 32, 3, 128], P('gx', 'gy')
The draws below stay inside these ranges and needn't reach their ends.
Inputs may be any that keep to these rules, and one draw needn't show every extreme that they name: `positions`: each atom lies in its block: x in [6 x_block, 6 x_block + 6), y in [6 y_block, 6 y_block + 6), z in [0, 24). `pair_codes`: the first pair_count entries of a device's list are distinct codes whose far block lies inside the grid of 48 x 32 blocks; entries after them are codes of the same range that take no part. `pair_count`: some device holds 26 pairs in every draw.
All inputs are finite; a program needn't handle non-finite values.
Results may differ from the reference program's by a relative error of at most 0.004.
Values may be sent and summed in bfloat16 or wider, within the bound.
No kernel may reach another device: no remote copies, remote signals or barrier semaphores. Data moves between devices by JAX's collectives and lax.ppermute only.
A program may use at most 64 MiB of HBM per device.

```python
import jax
import jax.numpy as jnp
from jax import lax

D = 128
NBASIS = 4
NSPEC = 89
ATOMS = 128
BX = 6
PMAX = 26
NBX = 48
NBY = 32
N_GX = 8
N_GY = 32


def pair_tables(key):
    key = jax.random.fold_in(key, 11)
    first_key, second_key = jax.random.split(key)
    choices_n = 9 * BX
    codes = jnp.arange(choices_n, dtype=jnp.int32)
    column_dev = jnp.arange(N_GX, dtype=jnp.int32)[:, None, None]
    row_dev = jnp.arange(N_GY, dtype=jnp.int32)[None, :, None]
    block_index = codes // 9
    offset = codes % 9
    far_x = column_dev * BX + block_index + offset // 3 - 1
    far_y = row_dev + offset % 3 - 1
    inside = (far_x >= 0) & (far_x < NBX) & (far_y >= 0) & (far_y < NBY)
    scores = jax.random.randint(first_key, (N_GX, N_GY, choices_n), 0, 4096) * choices_n + codes + jnp.where(inside, 0, 2 ** 22)
    order = jnp.argsort(scores, axis=-1)
    listed = jnp.take_along_axis(jnp.broadcast_to(codes, scores.shape), order, axis=-1)[:, :, :PMAX]
    usable = jnp.sum(inside.astype(jnp.int32), axis=-1)
    sparse = jax.random.randint(second_key, (N_GX, N_GY), 1, PMAX // 2 + 1)
    band_low = 3 * N_GY // 8
    rows_here = jnp.arange(N_GY, dtype=jnp.int32)[None, :]
    dense = (rows_here >= band_low) & (rows_here < band_low + max(N_GY // 4, 1))
    totals = jnp.minimum(jnp.where(dense, PMAX, sparse), usable)
    return (listed.astype(jnp.int32), totals.astype(jnp.int32))


def draw_pair_codes(key, part):
    listed, totals = pair_tables(key)
    return listed


def draw_pair_count(key, part):
    listed, totals = pair_tables(key)
    return totals


def draw_positions(key, part):
    key = jax.random.fold_in(key, 5)
    spread_u = jax.random.uniform(key, (NBX, NBY, 3, ATOMS), jnp.float32)
    column_ids = jnp.arange(NBX, dtype=jnp.float32)[:, None, None]
    row_ids = jnp.arange(NBY, dtype=jnp.float32)[None, :, None]
    coord_x = (column_ids + spread_u[:, :, 0]) * 6.0
    coord_y = (row_ids + spread_u[:, :, 1]) * 6.0
    coord_z = spread_u[:, :, 2] * 24.0
    return jnp.stack([coord_x, coord_y, coord_z], axis=2).astype(jnp.float32)


def plant(array, key, smallest, largest):
    longest = array.shape.index(max(array.shape))
    spots = []
    for shift in (0, 1):
        where = [jax.random.randint(jax.random.fold_in(key, axis), (), 0, length) for axis, length in enumerate(array.shape)]
        where[longest] = (where[longest] + shift) % array.shape[longest]
        spots.append(tuple(where))
    return array.at[spots[0]].set(smallest).at[spots[1]].set(largest)


def gaussian(own_key, extent, scale, reach, held_as=jnp.bfloat16):
    entries = scale * jax.random.normal(own_key, extent, jnp.float32)
    return jnp.clip(entries, min=-reach, max=reach).astype(held_as)


def setup_inputs(seed: int = 0) -> dict:
    key_list = jax.random.split(jax.random.key(seed), 14)
    positions = draw_positions(jax.random.fold_in(key_list[13], 71), 0)
    species = plant(jax.random.randint(key_list[1], (NBX, NBY, ATOMS), 0, NSPEC), jax.random.fold_in(key_list[1], 1), 0, NSPEC - 1).astype(jnp.int32)
    pair_codes = draw_pair_codes(jax.random.fold_in(key_list[13], 71), 0)
    pair_count = draw_pair_count(jax.random.fold_in(key_list[13], 71), 0)
    embed_table = gaussian(key_list[4], (NSPEC, D), 1.0, 6.0)
    scalar_radial_one = gaussian(key_list[5], (NBASIS, D), 1.0, 6.0, jnp.float32)
    vector_radial_one = gaussian(key_list[6], (NBASIS, D), 1.0, 6.0, jnp.float32)
    scalar_radial_two = gaussian(key_list[7], (NBASIS, D), 1.0, 6.0, jnp.float32)
    vector_radial_two = gaussian(key_list[8], (NBASIS, D), 1.0, 6.0, jnp.float32)
    mixing_scalar_one = gaussian(key_list[9], (D, D), D ** -0.5, 0.5)
    mixing_vector_one = gaussian(key_list[10], (D, D), D ** -0.5, 0.5)
    mixing_two = gaussian(key_list[11], (D, D), D ** -0.5, 0.5)
    readout = gaussian(key_list[12], (D,), D ** -0.5, 0.5, jnp.float32)
    return {"positions": positions, "species": species, "pair_codes": pair_codes, "pair_count": pair_count, "embed_table": embed_table, "scalar_radial_one": scalar_radial_one, "vector_radial_one": vector_radial_one, "scalar_radial_two": scalar_radial_two, "vector_radial_two": vector_radial_two, "mixing_scalar_one": mixing_scalar_one, "mixing_vector_one": mixing_vector_one, "mixing_two": mixing_two, "readout": readout}


soften = 0.25
cutoff = 6.0
spread = 1.5
message_scale = 0.125

def geometry(home_pos, other_pos, self_flag, radial_count):
    offset = other_pos[:, None, :] - home_pos[:, :, None]
    squared = lax.optimization_barrier(jnp.sum(offset * offset, axis=0))
    softened = jnp.sqrt(squared + soften)
    tapering = jnp.maximum(1.0 - squared / (cutoff * cutoff), 0.0)
    atoms_here = home_pos.shape[1]
    row_ids = lax.broadcasted_iota(jnp.int32, (atoms_here, atoms_here), 0)
    col_ids = lax.broadcasted_iota(jnp.int32, (atoms_here, atoms_here), 1)
    diagonal = (row_ids == col_ids).astype(jnp.float32)
    envelope = tapering * tapering * (1.0 - self_flag * diagonal)
    centres = cutoff * (jnp.arange(radial_count, dtype=jnp.float32) + 0.5) / radial_count
    radial = envelope[None] * jnp.exp(-jnp.square((softened[None] - centres[:, None, None]) / spread))
    direction = offset / softened[None]
    return (radial, direction)

def tiles(radial, direction):
    plain_tile = radial.astype(jnp.bfloat16)
    tilted = (radial[:, None] * direction[None]).astype(jnp.bfloat16)
    return (plain_tile, tilted)

def layer_one(radial, direction, source, scalar_w, vector_w):
    plain_tile, tilted = tiles(radial, direction)
    scalar_part = jnp.einsum('kab,bc->kac', plain_tile, source, preferred_element_type=jnp.float32)
    vector_part = jnp.einsum('kdab,bc->kdac', tilted, source, preferred_element_type=jnp.float32)
    return (lax.optimization_barrier(jnp.sum(scalar_w[:, None, :] * scalar_part, axis=0)), lax.optimization_barrier(jnp.sum(vector_w[:, None, None, :] * vector_part, axis=0)))

def layer_two(radial, direction, source, scalar_w, vector_w):
    plain_tile, tilted = tiles(radial, direction)
    scalar_part = jnp.einsum('kab,bc->kac', plain_tile, source[0], preferred_element_type=jnp.float32)
    tensor_part = jnp.einsum('kdab,dbc->kac', tilted, source[1:], preferred_element_type=jnp.float32)
    return lax.optimization_barrier(jnp.sum(scalar_w[:, None, :] * scalar_part + vector_w[:, None, :] * tensor_part, axis=0))

def pull_back(pullback, radial, direction, plain_grad, tilted_grad):
    radial_grad = plain_grad + lax.optimization_barrier(jnp.sum(tilted_grad * direction[None], axis=1))
    direction_grad = lax.optimization_barrier(jnp.sum(tilted_grad * radial[:, None], axis=0))
    return pullback((radial_grad, direction_grad))

def back_one(home_pos, other_pos, self_flag, source, scalar_in, vector_in, scalar_w, vector_w):
    radial_count = scalar_w.shape[0]
    (radial, direction), pullback = jax.vjp(lambda home_side, far_side: geometry(home_side, far_side, self_flag, radial_count), home_pos, other_pos)
    scalar_cot = (scalar_w[:, None, :] * scalar_in[None]).astype(jnp.bfloat16)
    vector_cot = (vector_w[:, None, None, :] * vector_in[None]).astype(jnp.bfloat16)
    plain_grad = jnp.einsum('kac,bc->kab', scalar_cot, source, preferred_element_type=jnp.float32)
    tilted_grad = jnp.einsum('kdac,bc->kdab', vector_cot, source, preferred_element_type=jnp.float32)
    return pull_back(pullback, radial, direction, plain_grad, tilted_grad)

def back_two(home_pos, other_pos, self_flag, source, gradient_in, scalar_w, vector_w):
    radial_count = scalar_w.shape[0]
    (radial, direction), pullback = jax.vjp(lambda home_side, far_side: geometry(home_side, far_side, self_flag, radial_count), home_pos, other_pos)
    plain_tile, tilted = tiles(radial, direction)
    scalar_cot = (scalar_w[:, None, :] * gradient_in[None]).astype(jnp.bfloat16)
    tensor_cot = (vector_w[:, None, :] * gradient_in[None]).astype(jnp.bfloat16)
    plain_grad = jnp.einsum('kac,bc->kab', scalar_cot, source[0], preferred_element_type=jnp.float32)
    tilted_grad = jnp.einsum('kac,dbc->kdab', tensor_cot, source[1:], preferred_element_type=jnp.float32)
    scalar_grad = jnp.einsum('kab,kac->bc', plain_tile, scalar_cot, preferred_element_type=jnp.float32)
    vector_grad = jnp.einsum('kdab,kac->dbc', tilted, tensor_cot, preferred_element_type=jnp.float32)
    home_grad, other_grad = pull_back(pullback, radial, direction, plain_grad, tilted_grad)
    return (home_grad, other_grad, jnp.concatenate([scalar_grad[None], vector_grad], axis=0))

def silu_slope(value):
    sigma = jax.nn.sigmoid(value)
    return sigma * (1.0 + value * (1.0 - sigma))

def reference(positions, species, pair_codes, pair_count, embed_table, scalar_radial_one, vector_radial_one, scalar_radial_two, vector_radial_two, mixing_scalar_one, mixing_vector_one, mixing_two, readout):
    radial_count = scalar_radial_one.shape[0]
    atoms_n = positions.shape[3]
    width = embed_table.shape[1]
    slots = N_GX * N_GY * PMAX
    initial = embed_table[species]

    def locate(slot):
        column_dev = slot // (N_GY * PMAX)
        row_dev = slot // PMAX % N_GY
        place = slot % PMAX
        pair_code = pair_codes[column_dev, row_dev, place]
        active = place < pair_count[column_dev, row_dev]
        block_index = pair_code // 9
        offset = pair_code % 9
        home_x = jnp.clip(column_dev * BX + block_index, 0, NBX - 1)
        home_y = row_dev
        far_x = jnp.clip(home_x + offset // 3 - 1, 0, NBX - 1)
        far_y = jnp.clip(home_y + offset % 3 - 1, 0, NBY - 1)
        self_flag = (offset == 4).astype(jnp.float32)
        return (active, (home_x, home_y, far_x, far_y, self_flag))

    def sweep(update, totals):

        def visit(slot, carry):
            active, where_info = locate(slot)
            return lax.cond(active, lambda inner: update(inner, where_info), lambda inner: inner, carry)
        return lax.fori_loop(0, slots, visit, totals)

    def first_forward(totals, where_info):
        home_x, home_y, far_x, far_y, self_flag = where_info
        radial, direction = geometry(positions[home_x, home_y], positions[far_x, far_y], self_flag, radial_count)
        scalar_add, vector_add = layer_one(radial, direction, initial[far_x, far_y], scalar_radial_one, vector_radial_one)
        return (totals[0].at[home_x, home_y].add(scalar_add), totals[1].at[home_x, home_y].add(vector_add))
    scalar_msg, vector_msg = sweep(first_forward, (jnp.zeros((NBX, NBY, atoms_n, width), jnp.float32), jnp.zeros((NBX, NBY, 3, atoms_n, width), jnp.float32)))
    first_pre = jnp.dot((scalar_msg * message_scale).astype(jnp.bfloat16), mixing_scalar_one, preferred_element_type=jnp.float32)
    scalar_one = (initial.astype(jnp.float32) + jax.nn.silu(first_pre)).astype(jnp.bfloat16)
    vector_one = jnp.dot((vector_msg * message_scale).astype(jnp.bfloat16), mixing_vector_one, preferred_element_type=jnp.float32).astype(jnp.bfloat16)
    features = jnp.concatenate([scalar_one[:, :, None], vector_one], axis=2)

    def second_forward(totals, where_info):
        home_x, home_y, far_x, far_y, self_flag = where_info
        radial, direction = geometry(positions[home_x, home_y], positions[far_x, far_y], self_flag, radial_count)
        return totals.at[home_x, home_y].add(layer_two(radial, direction, features[far_x, far_y], scalar_radial_two, vector_radial_two))
    second_msg = sweep(second_forward, jnp.zeros((NBX, NBY, atoms_n, width), jnp.float32))
    second_pre = jnp.dot((second_msg * message_scale).astype(jnp.bfloat16), mixing_two, preferred_element_type=jnp.float32)
    atom_energy = lax.optimization_barrier(jnp.sum((scalar_one.astype(jnp.float32) + jax.nn.silu(second_pre)) * readout, axis=-1))
    second_slope = readout * silu_slope(second_pre)
    second_in = jnp.dot(second_slope.astype(jnp.bfloat16), mixing_two.T, preferred_element_type=jnp.float32) * message_scale

    def second_back(totals, where_info):
        home_x, home_y, far_x, far_y, self_flag = where_info
        home_grad, other_grad, feature_add = back_two(positions[home_x, home_y], positions[far_x, far_y], self_flag, features[far_x, far_y], second_in[home_x, home_y], scalar_radial_two, vector_radial_two)
        position_grad = totals[0].at[home_x, home_y].add(home_grad).at[far_x, far_y].add(other_grad)
        return (position_grad, totals[1].at[far_x, far_y].add(feature_add))
    position_grad, feature_grad = sweep(second_back, (jnp.zeros((NBX, NBY, 3, atoms_n), jnp.float32), jnp.zeros((NBX, NBY, 4, atoms_n, width), jnp.float32)))
    first_slope = (readout + feature_grad[:, :, 0]) * silu_slope(first_pre)
    first_in = jnp.dot(first_slope.astype(jnp.bfloat16), mixing_scalar_one.T, preferred_element_type=jnp.float32) * message_scale
    vector_in = jnp.dot(feature_grad[:, :, 1:].astype(jnp.bfloat16), mixing_vector_one.T, preferred_element_type=jnp.float32) * message_scale

    def first_back(totals, where_info):
        home_x, home_y, far_x, far_y, self_flag = where_info
        home_grad, other_grad = back_one(positions[home_x, home_y], positions[far_x, far_y], self_flag, initial[far_x, far_y], first_in[home_x, home_y], vector_in[home_x, home_y], scalar_radial_one, vector_radial_one)
        return totals.at[home_x, home_y].add(home_grad).at[far_x, far_y].add(other_grad)
    position_grad = sweep(first_back, position_grad)
    return (atom_energy, -position_grad)
```

```python
import jax
import jax.numpy as jnp
from jax import lax
from jax.experimental import pallas as pl
from jax.experimental.pallas import tpu as pltpu
from jax.sharding import PartitionSpec as P

BX = 6
EX = 8
A = 128
C = 128
K = 4
ROWS = 32
F32 = jnp.float32
BF16 = jnp.bfloat16
SIGMA = 1.5
NT = (((1,), (1,)), ((), ()))

HOME_PAIRS = [
    (h, (o % 3) * EX + h + o // 3, EX + 1 + h, o) for h in range(BX) for o in range(9)
]
FAR_PAIRS = [
    (f, (2 - o % 3) * EX + f + 2 - o // 3, (2 - o % 3) * EX + f + 2 - o // 3, o)
    for f in range(BX)
    for o in range(9)
]


def dot(a, b):
    return jnp.dot(a, b, preferred_element_type=F32)


def dot_nt(a, b):
    return lax.dot_general(a, b, NT, preferred_element_type=F32)


def pack_kernel(pos_ref, species_ref, codes_ref, count_ref, out_ref):
    block_id = lax.broadcasted_iota(jnp.int32, (8, 128), 0)
    mask = jnp.zeros((8, 128), jnp.int32)
    for p in range(codes_ref.shape[1]):
        code = codes_ref[0, p]
        block = lax.shift_right_logical(code * 57, 9)
        bit = jnp.where(p < count_ref[0, 0], lax.shift_left(1, code - 9 * block), 0)
        mask = mask + jnp.where(block_id == block, bit, 0)
    mask = mask.astype(F32)
    for h in range(BX):
        out_ref[h, 0:3, :] = pos_ref[h]
        out_ref[h, 3:4, :] = species_ref[h : h + 1, :].astype(F32)
        out_ref[h, 4:5, :] = mask[h : h + 1, :]
        out_ref[h, 5:8, :] = jnp.zeros((3, 128), F32)


def gather_ext(lo_ref, mid_ref, hi_ref, ext_ref):
    for row, ref in enumerate((lo_ref, mid_ref, hi_ref)):
        for x in range(EX):
            ext_ref[row * EX + x] = ref[x]


def send_masks(ext_ref, maskv_ref, masks_ref, sem):
    for e in range(3 * EX):
        maskv_ref[e : e + 1, :] = ext_ref[e, 4:5, :].astype(jnp.int32)
    copy = pltpu.make_async_copy(maskv_ref, masks_ref, sem)
    copy.start()
    return copy


def make_list(pairs, masks_ref, list_ref):
    n = jnp.int32(0)
    for own, other, lister, o in pairs:
        list_ref[n] = own + other * 8 + (256 if o == 4 else 0)
        n = n + (lax.shift_right_logical(masks_ref[lister, 0], o) & 1)
    return n


def entry(list_ref, p):
    code = list_ref[p]
    own = code & 7
    other = lax.shift_right_logical(code, 3) & 31
    bias = jnp.where(code >= 256, 0, 1024)
    return own, other, bias


def columns(ext_ref, col_ref, blocks, parts):
    for i, e in enumerate(blocks):
        turned = ext_ref[e].T
        for d in range(parts):
            col_ref[i, d] = jnp.broadcast_to(turned[:, d : d + 1], (A, 128))


def embed_all(ext_ref, table_ref, init_ref, blocks):
    lanes = lax.broadcasted_iota(jnp.int32, (A, 128), 1).astype(F32)
    for e in blocks:
        kind = jnp.broadcast_to(ext_ref[e].T[:, 3:4], (A, 128))
        hot = (kind == lanes).astype(BF16)
        init_ref[e] = dot(hot, table_ref[...]).astype(BF16)


def geometry(col_ref, i, row, r, sign, bias, rows=ROWS):
    off = [sign * (row[d] - col_ref[i, d, pl.ds(r, rows), :]) for d in range(3)]
    squared = off[0] * off[0] + off[1] * off[1] + off[2] * off[2]
    soft = squared + 0.25
    inv = lax.rsqrt(soft)
    s = soft * inv
    taper = jnp.maximum(1.0 - squared * (1.0 / 36.0), 0.0)
    at = lax.broadcasted_iota(jnp.int32, (rows, 128), 0) + (r + bias)
    lane = lax.broadcasted_iota(jnp.int32, (rows, 128), 1)
    taper = jnp.where(at == lane, 0.0, taper)
    u = jnp.minimum(s, 6.25) * (1.0 / SIGMA) - 0.5
    base = taper * jnp.exp(-u * u)
    step = jnp.exp(2.0 * u - 1.0)
    q = [base]
    for k in range(1, K):
        q.append(q[-1] * (step * EXPS[k]))
    return off, inv, taper, u, q


EXPS = [1.0, 1.0, 0.1353352832366127, 0.01831563888873418]


def store_tiles(put, off, inv, taper, q):
    direction = [o * inv for o in off]
    for k in range(K):
        radial = taper * q[k]
        put(0, k, radial.astype(BF16))
        for d in range(3):
            put(1 + d, k, (radial * direction[d]).astype(BF16))


def pull_back(grads, off, inv, taper, u, q):
    direction = [o * inv for o in off]
    s0 = s1 = turn = None
    dg = [None] * 3
    for k in range(K):
        radial = taper * q[k]
        tilted = [grads(1 + d, k) for d in range(3)]
        along = tilted[0] * direction[0] + tilted[1] * direction[1] + tilted[2] * direction[2]
        p = (grads(0, k) + along) * q[k]
        w = along * radial
        s0 = p if s0 is None else s0 + p
        if k:
            s1 = p * float(k) if s1 is None else s1 + p * float(k)
        turn = w if turn is None else turn + w
        for d in range(3):
            v = tilted[d] * radial
            dg[d] = v if dg[d] is None else dg[d] + v
    bend = (2.0 / SIGMA) * taper * (u * s0 - s1) + turn * inv
    weight = -(s0 * (1.0 / 9.0)) - inv * bend
    return [dg[d] * inv + weight * off[d] for d in range(3)]


def rows_of(ext_ref, e):
    return [ext_ref[e, d : d + 1, :] for d in range(3)]


def scaled(feature, weights_ref, k):
    return (feature.astype(F32) * weights_ref[k : k + 1, :]).astype(BF16)


def forward_kernel(
    lo_ref, mid_ref, hi_ref, table_ref, ws1_ref, wv1_ref, ws2_ref, wv2_ref, ms_ref, mv_ref,
    pre_ref, feat_ref, out_lo_ref, out_mid_ref, out_hi_ref,
    ext_ref, col_ref, init_ref, scaled_s_ref, scaled_v_ref, acc_ref, tile_ref, wide_ref, ready_ref,
    total_ref, maskv_ref, masks_ref, list1_ref, list2_ref, sem,
):
    gather_ext(lo_ref, mid_ref, hi_ref, ext_ref)
    copy = send_masks(ext_ref, maskv_ref, masks_ref, sem)
    columns(ext_ref, col_ref, range(3 * EX), 3)
    embed_all(ext_ref, table_ref, init_ref, range(3 * EX))

    def scale_block(e, carry):
        for k in range(K):
            scaled_s_ref[e, pl.ds(k * A, A), :] = scaled(init_ref[e], ws1_ref, k)
            scaled_v_ref[e, pl.ds(k * A, A), :] = scaled(init_ref[e], wv1_ref, k)
        return carry

    lax.fori_loop(0, 3 * EX, scale_block, 0)
    acc_ref[...] = jnp.zeros_like(acc_ref)
    total_ref[...] = jnp.zeros_like(total_ref)
    copy.wait()
    n1 = make_list(HOME_PAIRS, masks_ref, list1_ref)
    n2 = make_list(FAR_PAIRS, masks_ref, list2_ref)

    def first(p, carry):
        own, other, bias = entry(list1_ref, p)
        row = rows_of(ext_ref, other)
        for r in range(0, A, ROWS):
            off, inv, taper, u, q = geometry(col_ref, own + EX + 1, row, r, 1.0, bias)

            def put(g, k, tile):
                tile_ref[pl.ds(g * A + r, ROWS), pl.ds(k * A, A)] = tile

            store_tiles(put, off, inv, taper, q)
        acc_ref[own, 0:A, :] += dot(tile_ref[0:A, :], scaled_s_ref[other])
        acc_ref[own, A : 4 * A, :] += dot(tile_ref[A : 4 * A, :], scaled_v_ref[other])
        return carry

    lax.fori_loop(0, n1, first, 0)

    def mix(h, carry):
        pre = dot((acc_ref[h, 0:A, :] * 0.125).astype(BF16), ms_ref[...])
        pre_ref[h] = pre
        scalar = (init_ref[h + EX + 1].astype(F32) + pre * jax.nn.sigmoid(pre)).astype(BF16)
        vector = dot((acc_ref[h, A : 4 * A, :] * 0.125).astype(BF16), mv_ref[...]).astype(BF16)
        feat_ref[h, 0:A, :] = scalar
        feat_ref[h, A : 4 * A, :] = vector
        for k in range(K):
            ready_ref[h, pl.ds(k * A, A), :] = scaled(scalar, ws2_ref, k)
            for d in range(3):
                ready_ref[h, pl.ds(((1 + d) * K + k) * A, A), :] = scaled(
                    vector[d * A : (d + 1) * A, :], wv2_ref, k
                )
        return carry

    lax.fori_loop(0, BX, mix, 0)

    def second(p, carry):
        own, other, bias = entry(list2_ref, p)
        row = rows_of(ext_ref, own + EX + 1)
        for r in range(0, A, ROWS):
            off, inv, taper, u, q = geometry(col_ref, other, row, r, 1.0, bias)

            def put(g, k, tile):
                wide_ref[pl.ds(r, ROWS), pl.ds((g * K + k) * A, A)] = tile

            store_tiles(put, off, inv, taper, q)
        total_ref[other] += dot(wide_ref[...], ready_ref[own])
        return carry

    lax.fori_loop(0, n2, second, 0)
    for x in range(EX):
        out_lo_ref[x] = total_ref[x].astype(BF16)
        out_mid_ref[x] = total_ref[EX + x]
        out_hi_ref[x] = total_ref[2 * EX + x].astype(BF16)


def slope_of(value):
    sigma = jax.nn.sigmoid(value)
    return sigma * (1.0 + value * (1.0 - sigma))


def middle_kernel(
    mid_ref, below_ref, above_ref, left_ref, right_ref, feat_ref, mix_ref, readout_ref,
    energy_ref, second_in_ref,
):
    for h in range(BX):
        msg = mid_ref[h + 1] + below_ref[h + 1].astype(F32) + above_ref[h + 1].astype(F32)
        if h == 0:
            msg = msg + left_ref[0].astype(F32)
        if h == BX - 1:
            msg = msg + right_ref[0].astype(F32)
        pre = dot((msg * 0.125).astype(BF16), mix_ref[...])
        sigma = jax.nn.sigmoid(pre)
        part = (feat_ref[h, 0:A, :].astype(F32) + pre * sigma) * readout_ref[...]
        energy_ref[h : h + 1, :] = jnp.sum(part.T, axis=0, keepdims=True)
        grad = (readout_ref[...] * (sigma * (1.0 + pre * (1.0 - sigma)))).astype(BF16)
        second_in_ref[h] = (dot_nt(grad, mix_ref[...]) * 0.125).astype(BF16)


def backward_kernel(
    lo_ref, mid_ref, hi_ref, in_lo_ref, in_mid_ref, in_hi_ref, feat_ref, pre_ref, table_ref,
    ws1_ref, wv1_ref, ws2_ref, wv2_ref, ms_ref, mv_ref, readout_ref,
    out_lo_ref, out_mid_ref, out_hi_ref,
    ext_ref, col_ref, init_ref, scaled_s_ref, scaled_v_ref, cot_s_ref, cot_v_ref, acc_ref, tile_ref,
    grad_ref, inward_ref, down_ref, across_ref, maskv_ref, masks_ref, list1_ref, list2_ref, sem,
):
    gather_ext(lo_ref, mid_ref, hi_ref, ext_ref)
    copy = send_masks(ext_ref, maskv_ref, masks_ref, sem)
    columns(ext_ref, col_ref, range(EX + 1, EX + 1 + BX), 3)
    embed_all(ext_ref, table_ref, init_ref, range(3 * EX))

    def scale_block(e, carry):
        for k in range(K):
            scaled_s_ref[e, pl.ds(k * A, A), :] = scaled(init_ref[e], ws1_ref, k)
            scaled_v_ref[e, pl.ds(k * A, A), :] = scaled(init_ref[e], wv1_ref, k)
        return carry

    lax.fori_loop(0, 3 * EX, scale_block, 0)
    for row, ref in enumerate((in_lo_ref, in_mid_ref, in_hi_ref)):

        def cot_block(x, carry, row=row, ref=ref):
            for k in range(K):
                cot_s_ref[row * EX + x, pl.ds(k * A, A), :] = scaled(ref[x], ws2_ref, k)
                cot_v_ref[row * EX + x, pl.ds(k * A, A), :] = scaled(ref[x], wv2_ref, k)
            return carry

        lax.fori_loop(0, EX, cot_block, 0)
    acc_ref[...] = jnp.zeros_like(acc_ref)
    down_ref[...] = jnp.zeros_like(down_ref)
    across_ref[...] = jnp.zeros_like(across_ref)
    copy.wait()
    n1 = make_list(HOME_PAIRS, masks_ref, list1_ref)
    n2 = make_list(FAR_PAIRS, masks_ref, list2_ref)

    def move(own, other, r, off, inv, taper, u, q, own_sign):
        def grads(g, k):
            return grad_ref[pl.ds(g * A + r, ROWS), pl.ds(k * A, A)]

        moved = pull_back(grads, off, inv, taper, u, q)
        for d in range(3):
            across_ref[own, d, pl.ds(r, ROWS), :] += own_sign * moved[d]
            part = moved[d][0:8]
            for i in range(8, ROWS, 8):
                part = part + moved[d][i : i + 8]
            down_ref[other, d] -= own_sign * part

    def second_back(p, carry):
        own, other, bias = entry(list2_ref, p)
        row = rows_of(ext_ref, other)
        grad_ref[0:A, :] = dot_nt(feat_ref[own, 0:A, :], cot_s_ref[other])
        grad_ref[A : 4 * A, :] = dot_nt(feat_ref[own, A : 4 * A, :], cot_v_ref[other])
        for r in range(0, A, ROWS):
            off, inv, taper, u, q = geometry(col_ref, own, row, r, -1.0, bias)

            def put(g, k, tile):
                tile_ref[pl.ds(g * A + r, ROWS), pl.ds(k * A, A)] = tile

            store_tiles(put, off, inv, taper, q)
            move(own, other, r, off, inv, taper, u, q, 1.0)
        acc_ref[own, 0:A, :] += dot(tile_ref[0:A, :], cot_s_ref[other])
        acc_ref[own, A : 4 * A, :] += dot(tile_ref[A : 4 * A, :], cot_v_ref[other])
        return carry

    lax.fori_loop(0, n2, second_back, 0)

    def inward(h, carry):
        slope = (readout_ref[...] + acc_ref[h, 0:A, :]) * slope_of(pre_ref[h])
        inward_ref[h, 0:A, :] = (dot_nt(slope.astype(BF16), ms_ref[...]) * 0.125).astype(BF16)
        inward_ref[h, A : 4 * A, :] = (
            dot_nt(acc_ref[h, A : 4 * A, :].astype(BF16), mv_ref[...]) * 0.125
        ).astype(BF16)
        return carry

    lax.fori_loop(0, BX, inward, 0)

    def first_back(p, carry):
        own, other, bias = entry(list1_ref, p)
        row = rows_of(ext_ref, other)
        grad_ref[0:A, :] = dot_nt(inward_ref[own, 0:A, :], scaled_s_ref[other])
        grad_ref[A : 4 * A, :] = dot_nt(inward_ref[own, A : 4 * A, :], scaled_v_ref[other])
        for r in range(0, A, ROWS):
            off, inv, taper, u, q = geometry(col_ref, own, row, r, 1.0, bias)
            move(own, other, r, off, inv, taper, u, q, -1.0)
        return carry

    lax.fori_loop(0, n1, first_back, 0)
    for row, ref in enumerate((out_lo_ref, out_mid_ref, out_hi_ref)):
        for x in range(EX):
            for d in range(3):
                line = jnp.sum(down_ref[row * EX + x, d], axis=0, keepdims=True)
                if row == 1 and 1 <= x <= BX:
                    line = line + jnp.sum(across_ref[x - 1, d].T, axis=0, keepdims=True)
                ref[x, d : d + 1, :] = line


VMEM = pl.BlockSpec(memory_space=pltpu.VMEM)
SMEM = pl.BlockSpec(memory_space=pltpu.SMEM)
PARAMS = pltpu.CompilerParams(vmem_limit_bytes=56 * 1024 * 1024)


def call(kernel, args, outs, scratch=(), in_specs=None):
    return pl.pallas_call(
        kernel,
        out_shape=[jax.ShapeDtypeStruct(s, d) for s, d in outs],
        in_specs=in_specs or [VMEM] * len(args),
        out_specs=[VMEM] * len(outs),
        scratch_shapes=list(scratch),
        compiler_params=PARAMS,
    )(*args)


def along(block, axis, step):
    size = lax.axis_size(axis)
    return lax.ppermute(block, axis, [(i, i + step) for i in range(size) if 0 <= i + step < size])


def halo(own):
    left = along(own[BX - 1 : BX], "gx", 1)
    right = along(own[0:1], "gx", -1)
    mid = jnp.concatenate([left, own, right], axis=0)
    return along(mid, "gy", 1), mid, along(mid, "gy", -1)


def fold(lo, mid, hi, dtype):
    above = along(lo, "gy", -1)
    below = along(hi, "gy", 1)
    edge = lambda x: (mid[x : x + 1] + below[x : x + 1] + above[x : x + 1]).astype(dtype)
    right = along(edge(0), "gx", -1)
    left = along(edge(EX - 1), "gx", 1)
    return mid, below, above, left, right


E = 3 * EX


def local(
    positions, species, pair_codes, pair_count, embed_table, ws1, wv1, ws2, wv2, ms, mv, m2, readout
):
    (packed,) = call(
        pack_kernel,
        (positions.reshape(BX, 3, A), species.reshape(BX, A), pair_codes.reshape(1, -1), pair_count),
        [((BX, 8, A), F32)],
        in_specs=[VMEM, VMEM, SMEM, SMEM],
    )
    ext = halo(packed)
    table = jnp.pad(embed_table, ((0, 128 - embed_table.shape[0]), (0, 0)))
    readout = readout.reshape(1, C)
    lists = [
        pltpu.VMEM((E, 128), jnp.int32),
        pltpu.SMEM((E, 128), jnp.int32),
        pltpu.SMEM((64,), jnp.int32),
        pltpu.SMEM((64,), jnp.int32),
        pltpu.SemaphoreType.DMA,
    ]
    pre, feat, lo, mid, hi = call(
        forward_kernel,
        (*ext, table, ws1, wv1, ws2, wv2, ms, mv),
        [
            ((BX, A, C), F32),
            ((BX, 4 * A, C), BF16),
            ((EX, A, C), BF16),
            ((EX, A, C), F32),
            ((EX, A, C), BF16),
        ],
        [
            pltpu.VMEM((E, 8, A), F32),
            pltpu.VMEM((E, 3, A, 128), F32),
            pltpu.VMEM((E, A, C), BF16),
            pltpu.VMEM((E, K * A, C), BF16),
            pltpu.VMEM((E, K * A, C), BF16),
            pltpu.VMEM((BX, 4 * A, C), F32),
            pltpu.VMEM((4 * A, K * A), BF16),
            pltpu.VMEM((A, 4 * K * A), BF16),
            pltpu.VMEM((BX, 4 * K * A, C), BF16),
            pltpu.VMEM((E, A, C), F32),
            *lists,
        ],
    )
    energy, second_in = call(
        middle_kernel,
        (*fold(lo, mid, hi, BF16), feat, m2, readout),
        [((BX, A), F32), ((BX, A, C), BF16)],
    )
    inner = halo(second_in)
    lo, mid, hi = call(
        backward_kernel,
        (*ext, *inner, feat, pre, table, ws1, wv1, ws2, wv2, ms, mv, readout),
        [((EX, 3, A), F32)] * 3,
        [
            pltpu.VMEM((E, 8, A), F32),
            pltpu.VMEM((BX, 3, A, 128), F32),
            pltpu.VMEM((E, A, C), BF16),
            pltpu.VMEM((E, K * A, C), BF16),
            pltpu.VMEM((E, K * A, C), BF16),
            pltpu.VMEM((E, K * A, C), BF16),
            pltpu.VMEM((E, K * A, C), BF16),
            pltpu.VMEM((BX, 4 * A, C), F32),
            pltpu.VMEM((4 * A, K * A), BF16),
            pltpu.VMEM((4 * A, K * A), F32),
            pltpu.VMEM((BX, 4 * A, C), BF16),
            pltpu.VMEM((E, 3, 8, A), F32),
            pltpu.VMEM((BX, 3, A, 128), F32),
            *lists,
        ],
    )
    mid, below, above, left, right = fold(lo, mid, hi, F32)
    total = mid[1 : BX + 1] + below[1 : BX + 1] + above[1 : BX + 1]
    total = total + jnp.concatenate([left, jnp.zeros((BX - 2, 3, A), F32), right], axis=0)
    return energy.reshape(BX, 1, A), -total.reshape(BX, 1, 3, A)


def solution(mesh):
    in_specs = (
        P("gx", "gy", None, None),
        P("gx", "gy", None),
        P("gx", "gy", None),
        P("gx", "gy"),
        *[P()] * 9,
    )
    out_specs = (P("gx", "gy", None), P("gx", "gy", None, None))
    return jax.shard_map(local, mesh=mesh, in_specs=in_specs, out_specs=out_specs, check_vma=False)
```

```python
import jax
import jax.numpy as jnp
from jax import lax
from jax.experimental import pallas as pl
from jax.experimental.pallas import tpu as pltpu
from jax.sharding import PartitionSpec as P

BX = 6
EX = 8
A = 128
C = 128
K = 4
ROWS = 32
F32 = jnp.float32
BF16 = jnp.bfloat16
SIGMA = 1.5
NT = (((1,), (1,)), ((), ()))
E = 3 * EX

HOME_PAIRS = [
    (h, (o % 3) * EX + h + o // 3, EX + 1 + h, o) for h in range(BX) for o in range(9)
]
FAR_PAIRS = [
    (f, (2 - o % 3) * EX + f + 2 - o // 3, (2 - o % 3) * EX + f + 2 - o // 3, o)
    for f in range(BX)
    for o in range(9)
]


def dot(a, b):
    return jnp.dot(a, b, preferred_element_type=F32)


def dot_nt(a, b):
    return lax.dot_general(a, b, NT, preferred_element_type=F32)


def pack_kernel(pos_ref, species_ref, codes_ref, count_ref, first_ref, out_ref, last_ref):
    block_id = lax.broadcasted_iota(jnp.int32, (8, 128), 0)
    mask = jnp.zeros((8, 128), jnp.int32)
    for p in range(codes_ref.shape[2]):
        code = codes_ref[0, 0, p]
        block = lax.shift_right_logical(code * 57, 9)
        bit = jnp.where(p < count_ref[0, 0], lax.shift_left(1, code - 9 * block), 0)
        mask = mask + jnp.where(block_id == block, bit, 0)
    mask = mask.astype(F32)
    for h in range(BX):
        places = [(out_ref, h)]
        if h == 0:
            places.append((first_ref, 0))
        if h == BX - 1:
            places.append((last_ref, 0))
        for ref, i in places:
            ref[i, 0:3, :] = pos_ref[h, 0]
            ref[i, 3:4, :] = species_ref[h].astype(F32)
            ref[i, 4:5, :] = mask[h : h + 1, :]
            ref[i, 5:8, :] = jnp.zeros((3, 128), F32)


def gather_ext(lo_ref, mid_ref, hi_ref, ext_ref):
    for row, ref in enumerate((lo_ref, mid_ref, hi_ref)):
        for x in range(EX):
            ext_ref[row * EX + x] = ref[x]
    ext_ref[E : E + 8] = jnp.full((8, 8, A), 1.0e4, F32)


def send_masks(ext_ref, maskv_ref, masks_ref, sem):
    for e in range(E):
        maskv_ref[e : e + 1, :] = ext_ref[e, 4:5, :].astype(jnp.int32)
    copy = pltpu.make_async_copy(maskv_ref, masks_ref, sem)
    copy.start()
    return copy


def make_list(pairs, masks_ref, list_ref):
    n = jnp.int32(0)
    for own, other, lister, o in pairs:
        list_ref[n] = own + other * 8 + (256 if o == 4 else 0)
        n = n + (lax.shift_right_logical(masks_ref[lister, 0], o) & 1)
    for i in range(3):
        list_ref[n + i] = E * 8
    return n


def entry(list_ref, p):
    code = list_ref[p]
    own = code & 7
    other = lax.shift_right_logical(code, 3) & 31
    bias = jnp.where(code >= 256, 0, 1024)
    return own, other, bias


def turned_blocks(ext_ref):
    return [ext_ref[0:16].reshape(128, A).T, ext_ref[16:32].reshape(128, A).T]


def spread_lane(turned, e, d):
    lane = 8 * (e % 16) + d
    return jnp.broadcast_to(turned[e // 16][:, lane : lane + 1], (A, 128))


def geometry(col_ref, i, row, r, sign, bias, rows=ROWS):
    off = [sign * (row[d] - col_ref[i, d, pl.ds(r, rows), :]) for d in range(3)]
    squared = off[0] * off[0] + off[1] * off[1] + off[2] * off[2]
    soft = squared + 0.25
    inv = lax.rsqrt(soft)
    s = soft * inv
    taper = jnp.maximum(1.0 - squared * (1.0 / 36.0), 0.0)
    at = lax.broadcasted_iota(jnp.int32, (rows, 128), 0) + (r + bias)
    lane = lax.broadcasted_iota(jnp.int32, (rows, 128), 1)
    taper = jnp.where(at == lane, 0.0, taper)
    u = jnp.minimum(s, 6.25) * (1.0 / SIGMA) - 0.5
    base = taper * jnp.exp(-u * u)
    step = jnp.exp(2.0 * u - 1.0)
    q = [base]
    for k in range(1, K):
        q.append(q[-1] * (step * EXPS[k]))
    return off, inv, taper, u, q


EXPS = [1.0, 1.0, 0.1353352832366127, 0.01831563888873418]


def store_tiles(put, off, inv, taper, q):
    direction = [o * inv for o in off]
    for k in range(K):
        radial = taper * q[k]
        put(0, k, radial.astype(BF16))
        for d in range(3):
            put(1 + d, k, (radial * direction[d]).astype(BF16))


def pull_back(grads, off, inv, taper, u, q):
    direction = [o * inv for o in off]
    s0 = s1 = turn = None
    dg = [None] * 3
    for k in range(K):
        radial = taper * q[k]
        tilted = [grads(1 + d, k) for d in range(3)]
        along = tilted[0] * direction[0] + tilted[1] * direction[1] + tilted[2] * direction[2]
        p = (grads(0, k) + along) * q[k]
        w = along * radial
        s0 = p if s0 is None else s0 + p
        if k:
            s1 = p * float(k) if s1 is None else s1 + p * float(k)
        turn = w if turn is None else turn + w
        for d in range(3):
            v = tilted[d] * radial
            dg[d] = v if dg[d] is None else dg[d] + v
    bend = (2.0 / SIGMA) * taper * (u * s0 - s1) + turn * inv
    weight = -(s0 * (1.0 / 9.0)) - inv * bend
    return [dg[d] * inv + weight * off[d] for d in range(3)]


def rows_of(ext_ref, e):
    return [ext_ref[e, d : d + 1, :] for d in range(3)]


def scaled(feature, weights_ref, k):
    return (feature.astype(F32) * weights_ref[k : k + 1, :]).astype(BF16)


def forward_kernel(
    lo_ref, mid_ref, hi_ref, table_ref, ws1_ref, wv1_ref, ws2_ref, wv2_ref, ms_ref, mv_ref,
    pre_ref, feat_ref, out_lo_ref, out_mid_ref, out_hi_ref, keep_s_ref, keep_v_ref,
    ext_ref, col_ref, init_ref, scaled_s_ref, scaled_v_ref, acc_ref, tile_a_ref, tile_b_ref,
    wide_a_ref, wide_b_ref, ready_ref, total_ref, maskv_ref, masks_ref, list1_ref, list2_ref, sem,
    sem_s, sem_v,
):
    gather_ext(lo_ref, mid_ref, hi_ref, ext_ref)
    copy = send_masks(ext_ref, maskv_ref, masks_ref, sem)
    turned = turned_blocks(ext_ref)
    lanes = lax.broadcasted_iota(jnp.int32, (A, 128), 1).astype(F32)
    for e in range(E):
        for d in range(3):
            col_ref[e, d] = spread_lane(turned, e, d)
        hot = (spread_lane(turned, e, 3) == lanes).astype(BF16)
        init_ref[e] = dot(hot, table_ref[...]).astype(BF16)
    col_ref[E] = jnp.full((3, A, 128), 1.0e4, F32)

    def scale_block(e, carry):
        for k in range(K):
            scaled_s_ref[e, pl.ds(k * A, A), :] = scaled(init_ref[e], ws1_ref, k)
            scaled_v_ref[e, pl.ds(k * A, A), :] = scaled(init_ref[e], wv1_ref, k)
        return carry

    lax.fori_loop(0, E, scale_block, 0)
    scaled_s_ref[E] = jnp.zeros((K * A, C), BF16)
    scaled_v_ref[E] = jnp.zeros((K * A, C), BF16)
    keep_s = pltpu.make_async_copy(scaled_s_ref.at[0:E], keep_s_ref, sem_s)
    keep_s.start()
    keep_v = pltpu.make_async_copy(scaled_v_ref.at[0:E], keep_v_ref, sem_v)
    keep_v.start()
    acc_ref[...] = jnp.zeros_like(acc_ref)
    total_ref[...] = jnp.zeros_like(total_ref)
    copy.wait()
    n1 = make_list(HOME_PAIRS, masks_ref, list1_ref)
    n2 = make_list(FAR_PAIRS, masks_ref, list2_ref)

    def first_tiles(p, tile_ref):
        own, other, bias = entry(list1_ref, p)
        row = rows_of(ext_ref, other)
        for r in range(0, A, ROWS):
            off, inv, taper, u, q = geometry(col_ref, own + EX + 1, row, r, 1.0, bias)

            def put(g, k, tile):
                tile_ref[pl.ds(g * A + r, ROWS), pl.ds(k * A, A)] = tile

            store_tiles(put, off, inv, taper, q)

    def first_sum(p, tile_ref):
        own, other, _ = entry(list1_ref, p)
        acc_ref[own, 0:A, :] += dot(tile_ref[0:A, :], scaled_s_ref[other])
        acc_ref[own, A : 4 * A, :] += dot(tile_ref[A : 4 * A, :], scaled_v_ref[other])

    def first(i, carry):
        p = 2 * i
        first_sum(p, tile_a_ref)
        first_tiles(p + 1, tile_b_ref)
        first_sum(p + 1, tile_b_ref)
        first_tiles(p + 2, tile_a_ref)
        return carry

    first_tiles(0, tile_a_ref)
    lax.fori_loop(0, lax.shift_right_logical(n1 + 1, 1), first, 0)

    def mix(h, carry):
        pre = dot((acc_ref[h, 0:A, :] * 0.125).astype(BF16), ms_ref[...])
        pre_ref[h] = pre
        scalar = (init_ref[h + EX + 1].astype(F32) + pre * jax.nn.sigmoid(pre)).astype(BF16)
        vector = dot((acc_ref[h, A : 4 * A, :] * 0.125).astype(BF16), mv_ref[...]).astype(BF16)
        feat_ref[h, 0:A, :] = scalar
        feat_ref[h, A : 4 * A, :] = vector
        for k in range(K):
            ready_ref[h, pl.ds(k * A, A), :] = scaled(scalar, ws2_ref, k)
            for d in range(3):
                ready_ref[h, pl.ds(((1 + d) * K + k) * A, A), :] = scaled(
                    vector[d * A : (d + 1) * A, :], wv2_ref, k
                )
        return carry

    lax.fori_loop(0, BX, mix, 0)

    def second_tiles(p, wide_ref):
        own, other, bias = entry(list2_ref, p)
        row = rows_of(ext_ref, own + EX + 1)
        for r in range(0, A, ROWS):
            off, inv, taper, u, q = geometry(col_ref, other, row, r, 1.0, bias)

            def put(g, k, tile):
                wide_ref[pl.ds(r, ROWS), pl.ds((g * K + k) * A, A)] = tile

            store_tiles(put, off, inv, taper, q)

    def second_sum(p, wide_ref):
        own, other, _ = entry(list2_ref, p)
        total_ref[other] += dot(wide_ref[...], ready_ref[own])

    def second(i, carry):
        p = 2 * i
        second_sum(p, wide_a_ref)
        second_tiles(p + 1, wide_b_ref)
        second_sum(p + 1, wide_b_ref)
        second_tiles(p + 2, wide_a_ref)
        return carry

    second_tiles(0, wide_a_ref)
    lax.fori_loop(0, lax.shift_right_logical(n2 + 1, 1), second, 0)
    for x in range(EX):
        out_lo_ref[x] = total_ref[x].astype(BF16)
        out_mid_ref[x] = total_ref[EX + x]
        out_hi_ref[x] = total_ref[2 * EX + x].astype(BF16)
    keep_s.wait()
    keep_v.wait()


def slope_of(value):
    sigma = jax.nn.sigmoid(value)
    return sigma * (1.0 + value * (1.0 - sigma))


def middle_kernel(
    mid_ref, below_ref, above_ref, left_ref, right_ref, feat_ref, mix_ref, readout_ref,
    energy_ref, second_in_ref, second_own_ref,
):
    for x in range(EX):
        msg = mid_ref[x] + below_ref[x].astype(F32) + above_ref[x].astype(F32)
        if x < 2:
            msg = msg + left_ref[x].astype(F32)
        if x >= EX - 2:
            msg = msg + right_ref[x - EX + 2].astype(F32)
        pre = dot((msg * 0.125).astype(BF16), mix_ref[...])
        sigma = jax.nn.sigmoid(pre)
        if 1 <= x <= BX:
            part = (feat_ref[x - 1, 0:A, :].astype(F32) + pre * sigma) * readout_ref[...]
            energy_ref[x - 1] = jnp.sum(part.T, axis=0, keepdims=True)
        grad = (readout_ref[...] * (sigma * (1.0 + pre * (1.0 - sigma)))).astype(BF16)
        second = dot_nt(grad, mix_ref[...]) * 0.125
        second_own_ref[x] = second
        second_in_ref[x] = second.astype(BF16)


def backward_kernel(
    lo_ref, mid_ref, hi_ref, in_lo_ref, in_mid_ref, in_hi_ref, feat_ref, pre_ref, keep_s_ref,
    keep_v_ref, ws2_ref, wv2_ref, ms_ref, mv_ref, readout_ref,
    out_lo_ref, out_mid_ref, out_hi_ref,
    ext_ref, col_ref, scaled_s_ref, scaled_v_ref, cot_s_ref, cot_v_ref, acc_ref, tile_a_ref,
    tile_b_ref, grad_a_ref, grad_b_ref, inward_ref, down_ref, across_ref, maskv_ref, masks_ref,
    list1_ref, list2_ref, sem, sem_s, sem_v,
):
    keep_s = pltpu.make_async_copy(keep_s_ref, scaled_s_ref.at[0:E], sem_s)
    keep_s.start()
    keep_v = pltpu.make_async_copy(keep_v_ref, scaled_v_ref.at[0:E], sem_v)
    keep_v.start()
    gather_ext(lo_ref, mid_ref, hi_ref, ext_ref)
    copy = send_masks(ext_ref, maskv_ref, masks_ref, sem)
    turned = turned_blocks(ext_ref)
    for h in range(BX):
        for d in range(3):
            col_ref[h, d] = spread_lane(turned, EX + 1 + h, d)
    for row, ref in enumerate((in_lo_ref, in_mid_ref, in_hi_ref)):

        def cot_block(x, carry, row=row, ref=ref):
            for k in range(K):
                cot_s_ref[row * EX + x, pl.ds(k * A, A), :] = scaled(ref[x], ws2_ref, k)
                cot_v_ref[row * EX + x, pl.ds(k * A, A), :] = scaled(ref[x], wv2_ref, k)
            return carry

        lax.fori_loop(0, EX, cot_block, 0)
    for ref in (cot_s_ref, cot_v_ref, scaled_s_ref, scaled_v_ref):
        ref[E] = jnp.zeros((K * A, C), BF16)
    tile_b_ref[...] = jnp.zeros_like(tile_b_ref)
    acc_ref[...] = jnp.zeros_like(acc_ref)
    down_ref[...] = jnp.zeros_like(down_ref)
    across_ref[...] = jnp.zeros_like(across_ref)
    copy.wait()
    n1 = make_list(HOME_PAIRS, masks_ref, list1_ref)
    n2 = make_list(FAR_PAIRS, masks_ref, list2_ref)

    def move(own, other, r, off, inv, taper, u, q, own_sign, grad_ref):
        def grads(g, k):
            return grad_ref[pl.ds(g * A + r, ROWS), pl.ds(k * A, A)]

        moved = pull_back(grads, off, inv, taper, u, q)
        parts = []
        for d in range(3):
            across_ref[own, d, pl.ds(r, ROWS), :] += own_sign * moved[d]
            part = moved[d][0:8]
            for i in range(8, ROWS, 8):
                part = part + moved[d][i : i + 8]
            parts.append(part)
        return parts

    def add_down(other, own_sign, sums):
        for d in range(3):
            down_ref[other, d] -= own_sign * sums[d]

    def plus(sums, parts):
        return parts if sums is None else [a + b for a, b in zip(sums, parts)]

    def second_grads(p, grad_ref):
        own, other, _ = entry(list2_ref, p)
        grad_ref[0:A, :] = dot_nt(feat_ref[own, 0:A, :], cot_s_ref[other])
        grad_ref[A : 4 * A, :] = dot_nt(feat_ref[own, A : 4 * A, :], cot_v_ref[other])

    def second_move(p, grad_ref, tile_ref):
        own, other, bias = entry(list2_ref, p)
        row = rows_of(ext_ref, other)
        sums = None
        for r in range(0, A, ROWS):
            off, inv, taper, u, q = geometry(col_ref, own, row, r, -1.0, bias)

            def put(g, k, tile):
                tile_ref[pl.ds(g * A + r, ROWS), pl.ds(k * A, A)] = tile

            store_tiles(put, off, inv, taper, q)
            sums = plus(sums, move(own, other, r, off, inv, taper, u, q, 1.0, grad_ref))
        add_down(other, 1.0, sums)

    def second_sum(own, other, tile_ref):
        acc_ref[own, 0:A, :] += dot(tile_ref[0:A, :], cot_s_ref[other])
        acc_ref[own, A : 4 * A, :] += dot(tile_ref[A : 4 * A, :], cot_v_ref[other])

    def second_back(i, carry):
        p = 2 * i
        own, other, _ = entry(list2_ref, p)
        second_sum(*carry, tile_b_ref)
        second_grads(p + 1, grad_b_ref)
        second_move(p, grad_a_ref, tile_a_ref)
        second_sum(own, other, tile_a_ref)
        second_grads(p + 2, grad_a_ref)
        second_move(p + 1, grad_b_ref, tile_b_ref)
        own, other, _ = entry(list2_ref, p + 1)
        return own, other

    second_grads(0, grad_a_ref)
    last = lax.fori_loop(
        0, lax.shift_right_logical(n2 + 1, 1), second_back, (jnp.int32(0), jnp.int32(E))
    )
    second_sum(*last, tile_b_ref)

    def inward(h, carry):
        slope = (readout_ref[...] + acc_ref[h, 0:A, :]) * slope_of(pre_ref[h])
        inward_ref[h, 0:A, :] = (dot_nt(slope.astype(BF16), ms_ref[...]) * 0.125).astype(BF16)
        inward_ref[h, A : 4 * A, :] = (
            dot_nt(acc_ref[h, A : 4 * A, :].astype(BF16), mv_ref[...]) * 0.125
        ).astype(BF16)
        return carry

    lax.fori_loop(0, BX, inward, 0)
    keep_s.wait()
    keep_v.wait()

    def first_grads(p, grad_ref):
        own, other, _ = entry(list1_ref, p)
        grad_ref[0:A, :] = dot_nt(inward_ref[own, 0:A, :], scaled_s_ref[other])
        grad_ref[A : 4 * A, :] = dot_nt(inward_ref[own, A : 4 * A, :], scaled_v_ref[other])

    def first_move(p, grad_ref):
        own, other, bias = entry(list1_ref, p)
        row = rows_of(ext_ref, other)
        sums = None
        for r in range(0, A, ROWS):
            off, inv, taper, u, q = geometry(col_ref, own, row, r, 1.0, bias)
            sums = plus(sums, move(own, other, r, off, inv, taper, u, q, -1.0, grad_ref))
        add_down(other, -1.0, sums)

    def first_back(i, carry):
        p = 2 * i
        first_grads(p + 1, grad_b_ref)
        first_move(p, grad_a_ref)
        first_grads(p + 2, grad_a_ref)
        first_move(p + 1, grad_b_ref)
        return carry

    first_grads(0, grad_a_ref)
    lax.fori_loop(0, lax.shift_right_logical(n1 + 1, 1), first_back, 0)
    for row, ref in enumerate((out_lo_ref, out_mid_ref, out_hi_ref)):
        for x in range(EX):
            for d in range(3):
                line = jnp.sum(down_ref[row * EX + x, d], axis=0, keepdims=True)
                if row == 1 and 1 <= x <= BX:
                    line = line + jnp.sum(across_ref[x - 1, d].T, axis=0, keepdims=True)
                ref[x, d : d + 1, :] = line


def final_kernel(mid_ref, below_ref, above_ref, left_ref, right_ref, out_ref):
    for h in range(BX):
        total = mid_ref[h + 1] + below_ref[h + 1] + above_ref[h + 1]
        if h == 0:
            total = total + left_ref[0]
        if h == BX - 1:
            total = total + right_ref[0]
        out_ref[h, 0] = -total


ANY = pl.BlockSpec(memory_space=pl.ANY)
VMEM = pl.BlockSpec(memory_space=pltpu.VMEM)
SMEM = pl.BlockSpec(memory_space=pltpu.SMEM)
PARAMS = pltpu.CompilerParams(vmem_limit_bytes=56 * 1024 * 1024)


def call(kernel, args, outs, scratch=(), in_specs=None, out_specs=None):
    return pl.pallas_call(
        kernel,
        out_shape=[jax.ShapeDtypeStruct(s, d) for s, d in outs],
        in_specs=in_specs or [VMEM] * len(args),
        out_specs=out_specs or [VMEM] * len(outs),
        scratch_shapes=list(scratch),
        compiler_params=PARAMS,
    )(*args)


def along(block, axis, step):
    size = lax.axis_size(axis)
    return lax.ppermute(block, axis, [(i, i + step) for i in range(size) if 0 <= i + step < size])


def both(lo, hi, axis, step=1):
    return along(lo, axis, step), along(hi, axis, -step)


def list_scratch():
    return [
        pltpu.VMEM((E, 128), jnp.int32),
        pltpu.SMEM((E, 128), jnp.int32),
        pltpu.SMEM((64,), jnp.int32),
        pltpu.SMEM((64,), jnp.int32),
        pltpu.SemaphoreType.DMA,
        pltpu.SemaphoreType.DMA,
        pltpu.SemaphoreType.DMA,
    ]


def forward_call(*args):
    return call(
        forward_kernel,
        args,
        [
            ((BX, A, C), F32),
            ((BX, 4 * A, C), BF16),
            ((EX, A, C), BF16),
            ((EX, A, C), F32),
            ((EX, A, C), BF16),
            ((E, K * A, C), BF16),
            ((E, K * A, C), BF16),
        ],
        [
            pltpu.VMEM((E + 8, 8, A), F32),
            pltpu.VMEM((E + 1, 3, A, 128), F32),
            pltpu.VMEM((E, A, C), BF16),
            pltpu.VMEM((E + 1, K * A, C), BF16),
            pltpu.VMEM((E + 1, K * A, C), BF16),
            pltpu.VMEM((BX, 4 * A, C), F32),
            pltpu.VMEM((4 * A, K * A), BF16),
            pltpu.VMEM((4 * A, K * A), BF16),
            pltpu.VMEM((A, 4 * K * A), BF16),
            pltpu.VMEM((A, 4 * K * A), BF16),
            pltpu.VMEM((BX, 4 * K * A, C), BF16),
            pltpu.VMEM((E + 1, A, C), F32),
            *list_scratch(),
        ],
        out_specs=[VMEM] * 5 + [ANY] * 2,
    )


def backward_call(*args):
    return call(
        backward_kernel,
        args,
        [((EX, 3, A), F32)] * 3,
        [
            pltpu.VMEM((E + 8, 8, A), F32),
            pltpu.VMEM((BX, 3, A, 128), F32),
            pltpu.VMEM((E + 1, K * A, C), BF16),
            pltpu.VMEM((E + 1, K * A, C), BF16),
            pltpu.VMEM((E + 1, K * A, C), BF16),
            pltpu.VMEM((E + 1, K * A, C), BF16),
            pltpu.VMEM((BX, 4 * A, C), F32),
            pltpu.VMEM((4 * A, K * A), BF16),
            pltpu.VMEM((4 * A, K * A), BF16),
            pltpu.VMEM((4 * A, K * A), F32),
            pltpu.VMEM((4 * A, K * A), F32),
            pltpu.VMEM((BX, 4 * A, C), BF16),
            pltpu.VMEM((E + 1, 3, 8, A), F32),
            pltpu.VMEM((BX, 3, A, 128), F32),
            *list_scratch(),
        ],
        in_specs=[VMEM] * 8 + [ANY] * 2 + [VMEM] * 5,
    )


def local(
    positions, species, pair_codes, pair_count, embed_table, ws1, wv1, ws2, wv2, ms, mv, m2, readout
):
    first, own, last = call(
        pack_kernel,
        (positions, species, pair_codes, pair_count),
        [((1, 8, A), F32), ((BX, 8, A), F32), ((1, 8, A), F32)],
        in_specs=[VMEM, VMEM, SMEM, SMEM],
    )
    left, right = both(last, first, "gx")
    mid = jnp.concatenate([left, own, right], axis=0)
    ext = both(mid, mid, "gy")
    ext = (ext[0], mid, ext[1])
    table = jnp.pad(embed_table, ((0, 128 - embed_table.shape[0]), (0, 0)))
    readout = readout.reshape(1, C)
    pre, feat, lo, mid, hi, keep_s, keep_v = forward_call(
        *ext, table, ws1, wv1, ws2, wv2, ms, mv
    )
    below, above = both(hi, lo, "gy")
    edge = lambda x: (mid[x : x + 2] + below[x : x + 2] + above[x : x + 2]).astype(BF16)
    left, right = both(edge(EX - 2), edge(0), "gx")
    energy, inner, inner_own = call(
        middle_kernel,
        (mid, below, above, left, right, feat, m2, readout),
        [((BX, 1, A), F32), ((EX, A, C), BF16), ((EX, A, C), F32)],
    )
    inner = both(inner, inner, "gy")
    lo, mid, hi = backward_call(
        *ext, inner[0], inner_own, inner[1], feat, pre, keep_s, keep_v, ws2, wv2, ms, mv, readout
    )
    below, above = both(hi, lo, "gy")
    edge = lambda x: mid[x : x + 1] + below[x : x + 1] + above[x : x + 1]
    left, right = both(edge(EX - 1), edge(0), "gx")
    (forces,) = call(final_kernel, (mid, below, above, left, right), [((BX, 1, 3, A), F32)])
    return energy, forces


def solution(mesh):
    in_specs = (
        P("gx", "gy", None, None),
        P("gx", "gy", None),
        P("gx", "gy", None),
        P("gx", "gy"),
        *[P()] * 9,
    )
    out_specs = (P("gx", "gy", None), P("gx", "gy", None, None))
    return jax.shard_map(local, mesh=mesh, in_specs=in_specs, out_specs=out_specs, check_vma=False)
```

```python
import jax
import jax.numpy as jnp
from jax import lax
from jax.experimental import pallas as pl
from jax.experimental.pallas import tpu as pltpu
from jax.sharding import PartitionSpec as P

BX = 6
EX = 8
A = 128
C = 128
K = 4
ROWS = 16
F32 = jnp.float32
BF16 = jnp.bfloat16
SIGMA = 1.5
NT = (((1,), (1,)), ((), ()))
E = 3 * EX

HOME_PAIRS = [
    [(h, (o % 3) * EX + h + o // 3, EX + 1 + h, o) for h in range(BX) for o in range(9) if (o % 3 == 1) == inner]
    for inner in (False, True)
]
FAR_PAIRS = [
    [
        (f, (2 - o % 3) * EX + f + 2 - o // 3, (2 - o % 3) * EX + f + 2 - o // 3, o)
        for f in range(BX)
        for o in range(9)
        if (o % 3 == 1) == inner
    ]
    for inner in (False, True)
]
MIDDLE, END = 62, 63


def dot(a, b):
    return jnp.dot(a, b, preferred_element_type=F32)


def dot_nt(a, b):
    return lax.dot_general(a, b, NT, preferred_element_type=F32)


def pack_kernel(pos_ref, species_ref, codes_ref, count_ref, first_ref, out_ref, last_ref):
    block_id = lax.broadcasted_iota(jnp.int32, (8, 128), 0)
    mask = jnp.zeros((8, 128), jnp.int32)
    for p in range(codes_ref.shape[2]):
        code = codes_ref[0, 0, p]
        block = lax.shift_right_logical(code * 57, 9)
        bit = jnp.where(p < count_ref[0, 0], lax.shift_left(1, code - 9 * block), 0)
        mask = mask + jnp.where(block_id == block, bit, 0)
    mask = mask.astype(F32)
    for h in range(BX):
        places = [(out_ref, h)]
        if h == 0:
            places.append((first_ref, 0))
        if h == BX - 1:
            places.append((last_ref, 0))
        for ref, i in places:
            for d in range(3):
                ref[i, d : d + 1, :] = pos_ref[h, d]
            ref[i, 3:4, :] = species_ref[h].astype(F32)
            ref[i, 4:5, :] = mask[h : h + 1, :]
            ref[i, 5:8, :] = jnp.zeros((3, 128), F32)


def gather_ext(lo_ref, mid_ref, hi_ref, ext_ref):
    for row, ref in enumerate((lo_ref, mid_ref, hi_ref)):
        for x in range(EX):
            ext_ref[row * EX + x] = ref[x]
    ext_ref[E : E + 8] = jnp.full((8, 8, A), 1.0e4, F32)


def send_masks(ext_ref, maskv_ref, masks_ref, sem):
    for e in range(E):
        maskv_ref[e : e + 1, :] = ext_ref[e, 4:5, :].astype(jnp.int32)
    copy = pltpu.make_async_copy(maskv_ref, masks_ref, sem)
    copy.start()
    return copy


def make_list(parts, masks_ref, list_ref):
    n = jnp.int32(0)
    for pairs, place in zip(parts, (MIDDLE, END)):
        held = None
        for own, other, lister, o in sorted(pairs, key=lambda pair: pair[2]):
            if lister != held:
                held, mask = lister, masks_ref[lister, 0]
            list_ref[n] = own + other * 8 + (256 if o == 4 else 0)
            n = n + (lax.shift_right_logical(mask, o) & 1)
        for i in range(3):
            list_ref[n + i] = E * 8
        n = n + (n & 1)
        list_ref[place] = n


def entry(list_ref, p):
    code = list_ref[p]
    own = code & 7
    other = lax.shift_right_logical(code, 3) & 31
    bias = jnp.where(code >= 256, 0, 1024)
    return own, other, bias


def turned_blocks(ext_ref):
    return [ext_ref[0:16].reshape(128, A).T, ext_ref[16:32].reshape(128, A).T]


def spread_lane(turned, e, d):
    lane = 8 * (e % 16) + d
    return jnp.broadcast_to(turned[e // 16][:, lane : lane + 1], (A, 128))


def geometry(col_ref, i, row, r, sign, bias, rows=ROWS):
    off = [sign * (row[d] - col_ref[i, d, pl.ds(r, rows), :]) for d in range(3)]
    squared = off[0] * off[0] + off[1] * off[1] + off[2] * off[2]
    soft = squared + 0.25
    inv = lax.rsqrt(soft)
    s = soft * inv
    taper = jnp.maximum(1.0 - squared * (1.0 / 36.0), 0.0)
    at = lax.broadcasted_iota(jnp.int32, (rows, 128), 0) + (r + bias)
    lane = lax.broadcasted_iota(jnp.int32, (rows, 128), 1)
    taper = jnp.where(at == lane, 0.0, taper)
    u = jnp.minimum(s, 6.25) * (1.0 / SIGMA) - 0.5
    base = taper * jnp.exp(-u * u)
    step = jnp.exp(2.0 * u - 1.0)
    q = [base]
    for k in range(1, K):
        q.append(q[-1] * (step * EXPS[k]))
    return off, inv, taper, u, q


EXPS = [1.0, 1.0, 0.1353352832366127, 0.01831563888873418]


def store_tiles(put, off, inv, taper, q):
    direction = [o * inv for o in off]
    for k in range(K):
        radial = taper * q[k]
        put(0, k, radial.astype(BF16))
        for d in range(3):
            put(1 + d, k, (radial * direction[d]).astype(BF16))


def pull_back(grads, off, inv, taper, u, q):
    direction = [o * inv for o in off]
    s0 = s1 = None
    dg = [None] * 3
    for k in reversed(range(K)):
        tilted = [grads(1 + d, k) for d in range(3)]
        along = tilted[0] * direction[0] + tilted[1] * direction[1] + tilted[2] * direction[2]
        p = (grads(0, k) + along) * q[k]
        s0 = p if s0 is None else s0 + p
        if k:
            s1 = s0 if s1 is None else s1 + s0
        for d in range(3):
            v = tilted[d] * q[k]
            dg[d] = v if dg[d] is None else dg[d] + v
    turn = dg[0] * direction[0] + dg[1] * direction[1] + dg[2] * direction[2]
    bend = (2.0 / SIGMA) * (u * s0 - s1) + turn * inv
    pull = taper * inv
    weight = s0 * (1.0 / 9.0) + pull * bend
    return [dg[d] * pull - weight * off[d] for d in range(3)]


def rows_of(ext_ref, e):
    return [ext_ref[e, d : d + 1, :] for d in range(3)]


def scaled(feature, weights_ref, k):
    return (feature.astype(F32) * weights_ref[k : k + 1, :]).astype(BF16)


def forward_kernel(
    lo_ref, mid_ref, hi_ref, radial_ref, square_ref,
    pre_ref, feat_ref, out_lo_ref, out_hi_ref, scaled_s_ref, scaled_v_ref, ready_ref, keep_col_ref,
    list1_ref, list2_ref,
    ext_ref, col_ref, init_ref, acc_ref, tile_a_ref, tile_b_ref, wide_a_ref, wide_b_ref, total_ref,
    maskv_ref, masks_ref, sem,
):
    ws1_ref, wv1_ref, ws2_ref, wv2_ref, _ = radial_parts(radial_ref)
    ms_ref, mv_ref, _, table_ref = square_parts(square_ref)
    gather_ext(lo_ref, mid_ref, hi_ref, ext_ref)
    copy = send_masks(ext_ref, maskv_ref, masks_ref, sem)
    turned = turned_blocks(ext_ref)
    lanes = lax.broadcasted_iota(jnp.int32, (A, 128), 1).astype(F32)
    for e in range(E):
        if e == 8:
            copy.wait()
            make_list(HOME_PAIRS, masks_ref, list1_ref)
            make_list(FAR_PAIRS, masks_ref, list2_ref)
        for d in range(3):
            column = spread_lane(turned, e, d)
            col_ref[e, d] = column
            if EX <= e < 2 * EX:
                keep_col_ref[e - EX, d] = column
        hot = (spread_lane(turned, e, 3) == lanes).astype(BF16)
        init_ref[e] = dot(hot, table_ref[...]).astype(BF16)
    col_ref[E] = jnp.full((3, A, 128), 1.0e4, F32)
    keep_col_ref[EX] = jnp.full((3, A, 128), 1.0e4, F32)

    def scale_block(e, carry):
        for k in range(K):
            scaled_s_ref[e, pl.ds(k * A, A), :] = scaled(init_ref[e], ws1_ref, k)
            scaled_v_ref[e, pl.ds(k * A, A), :] = scaled(init_ref[e], wv1_ref, k)
        return carry

    lax.fori_loop(0, E, scale_block, 0)
    scaled_s_ref[E] = jnp.zeros((K * A, C), BF16)
    scaled_v_ref[E] = jnp.zeros((K * A, C), BF16)
    acc_ref[...] = jnp.zeros_like(acc_ref)
    total_ref[...] = jnp.zeros_like(total_ref)

    def first_tiles(p, tile_ref, r):
        own, other, bias = entry(list1_ref, p)
        row = rows_of(ext_ref, other)
        off, inv, taper, u, q = geometry(col_ref, own + EX + 1, row, r, 1.0, bias)

        def put(g, k, tile):
            tile_ref[pl.ds(g * A + r, ROWS), pl.ds(k * A, A)] = tile

        store_tiles(put, off, inv, taper, q)

    def first_sum(p, tile_ref, g):
        own, other, _ = entry(list1_ref, p)
        part = pl.ds(g * A, A)
        acc_ref[own, part, :] += dot(tile_ref[part, :], (scaled_v_ref if g else scaled_s_ref)[other])

    def first_half(p, this_ref, next_ref):
        for g in range(4):
            first_sum(p, this_ref, g)
            for r in range(g * 32, g * 32 + 32, ROWS):
                first_tiles(p + 1, next_ref, r)

    def first(i, carry):
        first_half(2 * i, tile_a_ref, tile_b_ref)
        first_half(2 * i + 1, tile_b_ref, tile_a_ref)
        return carry

    for r in range(0, A, ROWS):
        first_tiles(0, tile_a_ref, r)
    lax.fori_loop(0, half(list1_ref[END]), first, 0)

    for h in range(BX):
        pre = dot((acc_ref[h, 0:A, :] * 0.125).astype(BF16), ms_ref[...])
        pre_ref[h] = pre
        scalar = (init_ref[h + EX + 1].astype(F32) + pre * jax.nn.sigmoid(pre)).astype(BF16)
        vector = dot((acc_ref[h, A : 4 * A, :] * 0.125).astype(BF16), mv_ref[...]).astype(BF16)
        feat_ref[h, 0:A, :] = scalar
        feat_ref[h, A : 4 * A, :] = vector
        for k in range(K):
            ready_ref[h, pl.ds(k * A, A), :] = scaled(scalar, ws2_ref, k)
            for d in range(3):
                ready_ref[h, pl.ds(((1 + d) * K + k) * A, A), :] = scaled(
                    vector[d * A : (d + 1) * A, :], wv2_ref, k
                )
    second_sums(
        0, list2_ref[MIDDLE], list2_ref, col_ref, 0, lambda own: rows_of(ext_ref, own + EX + 1),
        ready_ref, total_ref, wide_a_ref, wide_b_ref,
    )
    for x in range(EX):
        out_lo_ref[x] = total_ref[x].astype(BF16)
        out_hi_ref[x] = total_ref[2 * EX + x].astype(BF16)


def place(other, shift):
    return jnp.minimum(other - shift, EX) if shift else other


def second_sums(
    start, end, list_ref, col_ref, shift, rows, ready_ref, total_ref, wide_a_ref, wide_b_ref
):
    def second_tiles(p, wide_ref, r):
        own, other, bias = entry(list_ref, p)
        row = rows(own)
        off, inv, taper, u, q = geometry(col_ref, place(other, shift), row, r, 1.0, bias)

        def put(g, k, tile):
            wide_ref[pl.ds(r, ROWS), pl.ds((g * K + k) * A, A)] = tile

        store_tiles(put, off, inv, taper, q)

    def second_half(p, this_ref, next_ref):
        own, other, _ = entry(list_ref, p)
        for g in range(4):
            part = pl.ds(g * K * A, K * A)
            total_ref[place(other, shift)] += dot(this_ref[:, part], ready_ref[own, part, :])
            for r in range(g * 32, g * 32 + 32, ROWS):
                second_tiles(p + 1, next_ref, r)

    def second(i, carry):
        second_half(2 * i, wide_a_ref, wide_b_ref)
        second_half(2 * i + 1, wide_b_ref, wide_a_ref)
        return carry

    for r in range(0, A, ROWS):
        second_tiles(start, wide_a_ref, r)
    lax.fori_loop(half(start), half(end), second, 0)


def forward_inner_kernel(
    mid_ref, list2_ref, ready_ref, col_ref, out_ref, wide_a_ref, wide_b_ref, total_ref
):
    total_ref[...] = jnp.zeros_like(total_ref)
    second_sums(
        list2_ref[MIDDLE], list2_ref[END], list2_ref, col_ref, EX,
        lambda own: rows_of(mid_ref, own + 1), ready_ref, total_ref, wide_a_ref, wide_b_ref,
    )
    out_ref[...] = total_ref[0:EX]


def radial_parts(ref):
    return [ref.at[pl.ds(K * i, K if i < 4 else 1), :] for i in range(5)]


def square_parts(ref):
    return [ref.at[pl.ds(C * i, C), :] for i in range(4)]


def half(n):
    return lax.shift_right_logical(n, 1)


def slope_of(value):
    sigma = jax.nn.sigmoid(value)
    return sigma * (1.0 + value * (1.0 - sigma))


def middle_kernel(
    mid_ref, below_ref, above_ref, left_ref, right_ref, feat_ref, radial_ref, square_ref,
    energy_ref, second_in_ref, second_own_ref,
):
    readout_ref = radial_parts(radial_ref)[4]
    mix_ref = square_parts(square_ref)[2]
    for x in range(EX):
        msg = mid_ref[x] + below_ref[x].astype(F32) + above_ref[x].astype(F32)
        if x < 2:
            msg = msg + left_ref[x].astype(F32)
        if x >= EX - 2:
            msg = msg + right_ref[x - EX + 2].astype(F32)
        pre = dot((msg * 0.125).astype(BF16), mix_ref[...])
        sigma = jax.nn.sigmoid(pre)
        if 1 <= x <= BX:
            part = (feat_ref[x - 1, 0:A, :].astype(F32) + pre * sigma) * readout_ref[...]
            energy_ref[x - 1] = jnp.sum(part.T, axis=0, keepdims=True)
        grad = (readout_ref[...] * (sigma * (1.0 + pre * (1.0 - sigma)))).astype(BF16)
        second = dot_nt(grad, mix_ref[...]) * 0.125
        second_own_ref[x] = second
        second_in_ref[x] = second.astype(BF16)


def move(across_ref, own, r, near, own_sign, grad_ref):
    def grads(g, k):
        return grad_ref[pl.ds(g * A + r, ROWS), pl.ds(k * A, A)]

    parts = []
    for d, moved in enumerate(pull_back(grads, *near)):
        if own_sign > 0:
            across_ref[own, d, pl.ds(r, ROWS), :] += moved
        else:
            across_ref[own, d, pl.ds(r, ROWS), :] -= moved
        part = moved[0:8]
        for i in range(8, ROWS, 8):
            part = part + moved[i : i + 8]
        parts.append(part)
    return parts


def add_down(down_ref, other, own_sign, sums):
    for d in range(3):
        down_ref[other, d] -= own_sign * sums[d]


def plus(sums, parts):
    return parts if sums is None else [a + b for a, b in zip(sums, parts)]


def first_moves(
    start, end, list_ref, col_ref, shift, rows, inward_ref, scaled_s_ref, scaled_v_ref, across_ref,
    down_ref, grad_a_ref, grad_b_ref,
):
    def first_grads(p, grad_ref):
        own, other, _ = entry(list_ref, p)
        grad_ref[0:A, :] = dot_nt(inward_ref[own, 0:A, :], scaled_s_ref[other])
        grad_ref[A : 4 * A, :] = dot_nt(inward_ref[own, A : 4 * A, :], scaled_v_ref[other])

    def first_move(p, grad_ref):
        own, other, bias = entry(list_ref, p)
        row = rows(place(other, shift))
        sums = None
        for r in range(0, A, ROWS):
            near = geometry(col_ref, own + 1, row, r, 1.0, bias)
            sums = plus(sums, move(across_ref, own, r, near, -1.0, grad_ref))
        add_down(down_ref, place(other, shift), -1.0, sums)

    def first_back(i, carry):
        p = 2 * i
        first_grads(p + 1, grad_b_ref)
        first_move(p, grad_a_ref)
        first_grads(p + 2, grad_a_ref)
        first_move(p + 1, grad_b_ref)
        return carry

    first_grads(start, grad_a_ref)
    lax.fori_loop(half(start), half(end), first_back, 0)


def line_of(down_ref, across_ref, e, x, d):
    line = jnp.sum(down_ref[e, d], axis=0, keepdims=True)
    if x is not None and 1 <= x <= BX:
        line = line + jnp.sum(across_ref[x - 1, d].T, axis=0, keepdims=True)
    return line


def second_moves(
    start, end, list_ref, col_ref, shift, rows, feat_ref, cot_s_ref, cot_v_ref, acc_ref, across_ref,
    down_ref, tile_a_ref, tile_b_ref, grad_a_ref, grad_b_ref,
):
    def second_grads(p, grad_ref):
        own, other, _ = entry(list_ref, p)
        source = place(other, shift)
        grad_ref[0:A, :] = dot_nt(feat_ref[own, 0:A, :], cot_s_ref[source])
        grad_ref[A : 4 * A, :] = dot_nt(feat_ref[own, A : 4 * A, :], cot_v_ref[source])

    def second_move(p, grad_ref, tile_ref):
        own, other, bias = entry(list_ref, p)
        source = place(other, shift)
        row = rows(source)
        sums = None
        for r in range(0, A, ROWS):
            near = geometry(col_ref, own + 1, row, r, -1.0, bias)
            off, inv, taper, u, q = near

            def put(g, k, tile):
                tile_ref[pl.ds(g * A + r, ROWS), pl.ds(k * A, A)] = tile

            store_tiles(put, off, inv, taper, q)
            sums = plus(sums, move(across_ref, own, r, near, 1.0, grad_ref))
        add_down(down_ref, source, 1.0, sums)

    def second_sum(own, source, tile_ref):
        acc_ref[own, 0:A, :] += dot(tile_ref[0:A, :], cot_s_ref[source])
        acc_ref[own, A : 4 * A, :] += dot(tile_ref[A : 4 * A, :], cot_v_ref[source])

    def second_back(i, carry):
        p = 2 * i
        own, other, _ = entry(list_ref, p)
        second_sum(*carry, tile_b_ref)
        second_grads(p + 1, grad_b_ref)
        second_move(p, grad_a_ref, tile_a_ref)
        second_sum(own, place(other, shift), tile_a_ref)
        second_grads(p + 2, grad_a_ref)
        second_move(p + 1, grad_b_ref, tile_b_ref)
        own, other, _ = entry(list_ref, p + 1)
        return own, place(other, shift)

    empty = EX if shift else E
    for ref in (cot_s_ref, cot_v_ref):
        ref[empty] = jnp.zeros((K * A, C), BF16)
    tile_b_ref[...] = jnp.zeros_like(tile_b_ref)
    second_grads(start, grad_a_ref)
    last = lax.fori_loop(half(start), half(end), second_back, (jnp.int32(0), jnp.int32(empty)))
    second_sum(*last, tile_b_ref)


def cotangents(ref, cot_s_ref, cot_v_ref, first, ws2_ref, wv2_ref):
    def cot_block(x, carry):
        for k in range(K):
            cot_s_ref[first + x, pl.ds(k * A, A), :] = scaled(ref[x], ws2_ref, k)
            cot_v_ref[first + x, pl.ds(k * A, A), :] = scaled(ref[x], wv2_ref, k)
        return carry

    lax.fori_loop(0, EX, cot_block, 0)


def backward_inner_two_kernel(
    mid_ref, list2_ref, in_mid_ref, feat_ref, col_ref, radial_ref,
    acc_ref, across_ref, down_ref,
    ext_ref, cot_s_ref, cot_v_ref, tile_a_ref, tile_b_ref, grad_a_ref, grad_b_ref,
):
    _, _, ws2_ref, wv2_ref, _ = radial_parts(radial_ref)
    for x in range(EX):
        ext_ref[x] = mid_ref[x]
    ext_ref[EX] = jnp.full((8, A), 1.0e4, F32)
    acc_ref[...] = jnp.zeros_like(acc_ref)
    down_ref[...] = jnp.zeros_like(down_ref)
    across_ref[...] = jnp.zeros_like(across_ref)
    cotangents(in_mid_ref, cot_s_ref, cot_v_ref, 0, ws2_ref, wv2_ref)
    second_moves(
        list2_ref[MIDDLE], list2_ref[END], list2_ref, col_ref, EX, lambda e: rows_of(ext_ref, e),
        feat_ref, cot_s_ref, cot_v_ref, acc_ref, across_ref, down_ref, tile_a_ref, tile_b_ref,
        grad_a_ref, grad_b_ref,
    )


def backward_kernel(
    lo_ref, mid_ref, hi_ref, list1_ref, list2_ref, acc_in_ref, across_in_ref, down_in_ref, feat_ref,
    pre_ref, in_lo_ref, in_hi_ref, scaled_s_ref, scaled_v_ref, col_ref, radial_ref, square_ref,
    out_lo_ref, out_mid_ref, out_hi_ref, inward_ref,
    ext_ref, cot_s_ref, cot_v_ref, acc_ref, tile_a_ref, tile_b_ref, grad_a_ref, grad_b_ref,
    down_ref, across_ref,
):
    _, _, ws2_ref, wv2_ref, readout_ref = radial_parts(radial_ref)
    ms_ref, mv_ref, _, _ = square_parts(square_ref)
    gather_ext(lo_ref, mid_ref, hi_ref, ext_ref)
    acc_ref[...] = acc_in_ref[...]
    across_ref[...] = across_in_ref[...]
    down_ref[0:EX] = jnp.zeros((EX, 3, 8, A), F32)
    down_ref[EX : 2 * EX] = down_in_ref[0:EX]
    down_ref[2 * EX : E + 1] = jnp.zeros((EX + 1, 3, 8, A), F32)
    cotangents(in_lo_ref, cot_s_ref, cot_v_ref, 0, ws2_ref, wv2_ref)
    cotangents(in_hi_ref, cot_s_ref, cot_v_ref, 2 * EX, ws2_ref, wv2_ref)
    second_moves(
        0, list2_ref[MIDDLE], list2_ref, col_ref, 0, lambda e: rows_of(ext_ref, e), feat_ref,
        cot_s_ref, cot_v_ref, acc_ref, across_ref, down_ref, tile_a_ref, tile_b_ref, grad_a_ref,
        grad_b_ref,
    )
    for h in range(BX):
        slope = (readout_ref[...] + acc_ref[h, 0:A, :]) * slope_of(pre_ref[h])
        inward_ref[h, 0:A, :] = (dot_nt(slope.astype(BF16), ms_ref[...]) * 0.125).astype(BF16)
        inward_ref[h, A : 4 * A, :] = (
            dot_nt(acc_ref[h, A : 4 * A, :].astype(BF16), mv_ref[...]) * 0.125
        ).astype(BF16)
    first_moves(
        0, list1_ref[MIDDLE], list1_ref, col_ref, 0, lambda e: rows_of(ext_ref, e), inward_ref,
        scaled_s_ref, scaled_v_ref, across_ref, down_ref, grad_a_ref, grad_b_ref,
    )
    for row, ref in enumerate((out_lo_ref, out_mid_ref, out_hi_ref)):
        for x in range(EX):
            for d in range(3):
                line = line_of(down_ref, across_ref, row * EX + x, x if row == 1 else None, d)
                ref[x, d : d + 1, :] = line


def backward_inner_kernel(
    mid_ref, list1_ref, scaled_s_ref, scaled_v_ref, col_ref, inward_ref, out_ref,
    ext_ref, grad_a_ref, grad_b_ref, down_ref, across_ref,
):
    for x in range(EX):
        ext_ref[x] = mid_ref[x]
    ext_ref[EX] = jnp.full((8, A), 1.0e4, F32)
    down_ref[...] = jnp.zeros_like(down_ref)
    across_ref[...] = jnp.zeros_like(across_ref)
    first_moves(
        list1_ref[MIDDLE], list1_ref[END], list1_ref, col_ref, EX, lambda e: rows_of(ext_ref, e),
        inward_ref, scaled_s_ref, scaled_v_ref, across_ref, down_ref, grad_a_ref, grad_b_ref,
    )
    for x in range(EX):
        for d in range(3):
            out_ref[x, d : d + 1, :] = line_of(down_ref, across_ref, x, x, d)


ANY = pl.BlockSpec(memory_space=pl.ANY)
VMEM = pl.BlockSpec(memory_space=pltpu.VMEM)
SMEM = pl.BlockSpec(memory_space=pltpu.SMEM)
PARAMS = pltpu.CompilerParams(vmem_limit_bytes=24 * 1024 * 1024)


SEM = pltpu.SemaphoreType.DMA


def forward_call(*args):
    return call(
        forward_kernel,
        args,
        [
            ((BX, A, C), F32),
            ((BX, 4 * A, C), BF16),
            ((EX, A, C), BF16),
            ((EX, A, C), BF16),
            ((E + 1, K * A, C), BF16),
            ((E + 1, K * A, C), BF16),
            ((BX, 4 * K * A, C), BF16),
            ((EX + 1, 3, A, 128), F32),
            ((64,), jnp.int32),
            ((64,), jnp.int32),
        ],
        [
            pltpu.VMEM((E + 8, 8, A), F32),
            pltpu.VMEM((E + 1, 3, A, 128), F32),
            pltpu.VMEM((E, A, C), BF16),
            pltpu.VMEM((BX, 4 * A, C), F32),
            pltpu.VMEM((4 * A, K * A), BF16),
            pltpu.VMEM((4 * A, K * A), BF16),
            pltpu.VMEM((A, 4 * K * A), BF16),
            pltpu.VMEM((A, 4 * K * A), BF16),
            pltpu.VMEM((E + 1, A, C), F32),
            pltpu.VMEM((E, 128), jnp.int32),
            pltpu.SMEM((E, 128), jnp.int32),
            SEM,
        ],
        out_specs=[VMEM] * 8 + [SMEM] * 2,
    )


def forward_inner_call(*args):
    return call(
        forward_inner_kernel,
        args,
        [((EX, A, C), F32)],
        [
            pltpu.VMEM((A, 4 * K * A), BF16),
            pltpu.VMEM((A, 4 * K * A), BF16),
            pltpu.VMEM((EX + 1, A, C), F32),
        ],
        in_specs=[VMEM, SMEM, VMEM, VMEM],
        cost=pl.CostEstimate(flops=4 * 10**9, bytes_accessed=10**6, transcendentals=0),
    )


def backward_inner_two_call(*args):
    return call(
        backward_inner_two_kernel,
        args,
        [((BX, 4 * A, C), F32), ((BX, 3, A, 128), F32), ((EX + 1, 3, 8, A), F32)],
        [
            pltpu.VMEM((EX + 1, 8, A), F32),
            pltpu.VMEM((EX + 1, K * A, C), BF16),
            pltpu.VMEM((EX + 1, K * A, C), BF16),
            pltpu.VMEM((4 * A, K * A), BF16),
            pltpu.VMEM((4 * A, K * A), BF16),
            pltpu.VMEM((4 * A, K * A), F32),
            pltpu.VMEM((4 * A, K * A), F32),
        ],
        in_specs=[VMEM, SMEM, VMEM, VMEM, VMEM, VMEM],
        cost=pl.CostEstimate(flops=4 * 10**9, bytes_accessed=10**6, transcendentals=0),
    )


def backward_call(*args):
    return call(
        backward_kernel,
        args,
        [*[((EX, 3, A), F32)] * 3, ((BX, 4 * A, C), BF16)],
        [
            pltpu.VMEM((E + 8, 8, A), F32),
            pltpu.VMEM((E + 1, K * A, C), BF16),
            pltpu.VMEM((E + 1, K * A, C), BF16),
            pltpu.VMEM((BX, 4 * A, C), F32),
            pltpu.VMEM((4 * A, K * A), BF16),
            pltpu.VMEM((4 * A, K * A), BF16),
            pltpu.VMEM((4 * A, K * A), F32),
            pltpu.VMEM((4 * A, K * A), F32),
            pltpu.VMEM((E + 1, 3, 8, A), F32),
            pltpu.VMEM((BX, 3, A, 128), F32),
        ],
        in_specs=[VMEM] * 3 + [SMEM] * 2 + [VMEM] * 12,
    )


def backward_inner_call(*args):
    return call(
        backward_inner_kernel,
        args,
        [((EX, 3, A), F32)],
        [
            pltpu.VMEM((EX + 1, 8, A), F32),
            pltpu.VMEM((4 * A, K * A), F32),
            pltpu.VMEM((4 * A, K * A), F32),
            pltpu.VMEM((EX + 1, 3, 8, A), F32),
            pltpu.VMEM((BX, 3, A, 128), F32),
        ],
        in_specs=[VMEM, SMEM, VMEM, VMEM, VMEM, VMEM],
        cost=pl.CostEstimate(flops=4 * 10**9, bytes_accessed=10**6, transcendentals=0),
    )


def call(kernel, args, outs, scratch=(), in_specs=None, out_specs=None, cost=None, params=PARAMS):
    return pl.pallas_call(
        kernel,
        out_shape=[jax.ShapeDtypeStruct(s, d) for s, d in outs],
        in_specs=in_specs or [VMEM] * len(args),
        out_specs=out_specs or [VMEM] * len(outs),
        scratch_shapes=list(scratch),
        compiler_params=params,
        cost_estimate=cost,
    )(*args)


def along(block, axis, step):
    size = lax.axis_size(axis)
    return lax.ppermute(block, axis, [(i, i + step) for i in range(size) if 0 <= i + step < size])


def both(lo, hi, axis, step=1):
    return along(lo, axis, step), along(hi, axis, -step)


def local(
    positions, species, pair_codes, pair_count, embed_table, ws1, wv1, ws2, wv2, ms, mv, m2, readout
):
    first, own, last = call(
        pack_kernel,
        (positions.transpose(0, 2, 1, 3), species, pair_codes, pair_count),
        [((1, 8, A), F32), ((BX, 8, A), F32), ((1, 8, A), F32)],
        in_specs=[VMEM, VMEM, SMEM, SMEM],
        params=pltpu.CompilerParams(vmem_limit_bytes=60 * 1024 * 1024),
    )
    left, right = both(last, first, "gx")
    ext_mid = jnp.concatenate([left, own, right], axis=0)
    ext_lo, ext_hi = both(ext_mid, ext_mid, "gy")
    ext = (ext_lo, ext_mid, ext_hi)
    table = jnp.pad(embed_table, ((0, 128 - embed_table.shape[0]), (0, 0)))
    square = jnp.concatenate([ms, mv, m2, table], axis=0)
    radial = jnp.concatenate([ws1, wv1, ws2, wv2, readout.reshape(1, C), jnp.zeros((7, C), F32)], axis=0)
    pre, feat, lo, hi, keep_s, keep_v, keep_ready, keep_col, list1, list2 = forward_call(
        *ext, radial, square
    )
    below, above = both(hi, lo, "gy")
    (mid,) = forward_inner_call(ext_mid, list2, keep_ready, keep_col)
    edge = lambda x: (mid[x : x + 2] + below[x : x + 2] + above[x : x + 2]).astype(BF16)
    left, right = both(edge(EX - 2), edge(0), "gx")
    energy, inner, inner_own = call(
        middle_kernel,
        (mid, below, above, left, right, feat, radial, square),
        [((BX, 1, A), F32), ((EX, A, C), BF16), ((EX, A, C), F32)],
    )
    in_lo, in_hi = both(inner, inner, "gy")
    held = backward_inner_two_call(ext_mid, list2, inner_own, feat, keep_col, radial)
    lo, mid, hi, keep_inward = backward_call(
        *ext, list1, list2, *held, feat, pre, in_lo, in_hi, keep_s, keep_v, keep_col, radial, square
    )
    below, above = both(hi, lo, "gy")
    (more,) = backward_inner_call(ext_mid, list1, keep_s, keep_v, keep_col, keep_inward)
    total = mid + more + below + above
    left, right = both(total[EX - 1 :], total[:1], "gx")
    total = total[1 : BX + 1] + jnp.concatenate(
        [left, jnp.zeros((BX - 2, 3, A), F32), right], axis=0
    )
    return energy, -total.reshape(BX, 1, 3, A)


def solution(mesh):
    in_specs = (
        P("gx", "gy", None, None),
        P("gx", "gy", None),
        P("gx", "gy", None),
        P("gx", "gy"),
        *[P()] * 9,
    )
    out_specs = (P("gx", "gy", None), P("gx", "gy", None, None))
    return jax.shard_map(local, mesh=mesh, in_specs=in_specs, out_specs=out_specs, check_vma=False)
```

```python
import jax
import jax.numpy as jnp
from jax import lax
from jax.experimental import pallas as pl
from jax.experimental.pallas import tpu as pltpu
from jax.sharding import PartitionSpec as P

BX = 6
EX = 8
A = 128
C = 128
K = 4
ROWS = 16
F32 = jnp.float32
BF16 = jnp.bfloat16
SIGMA = 1.5
NT = (((1,), (1,)), ((), ()))
E = 3 * EX

HOME_PAIRS = [
    [
        (h, (o % 3) * EX + h + o // 3, EX + 1 + h, o)
        for h in range(BX)
        for o in range(9)
        if (o % 3 == 1 and 0 <= h + o // 3 - 1 < BX) == inner
    ]
    for inner in (False, True)
]


def far_part(e):
    return 0 if e // EX != 1 else 1 if 2 <= e % EX < EX - 2 else 2


FAR_PAIRS = [
    [
        (f, (2 - o % 3) * EX + f + 2 - o // 3, (2 - o % 3) * EX + f + 2 - o // 3, o)
        for f in range(BX)
        for o in range(9)
        if far_part((2 - o % 3) * EX + f + 2 - o // 3) == part
    ]
    for part in range(3)
]
MIDDLE, THIRD, END = 62, 61, 63
INNER = range(2, EX - 2)
OUTER = [0, 1, EX - 2, EX - 1]


def dot(a, b):
    return jnp.dot(a, b, preferred_element_type=F32)


def dot_nt(a, b):
    return lax.dot_general(a, b, NT, preferred_element_type=F32)


def pack_kernel(
    pos_ref, species_ref, codes_ref, count_ref, table_ref, ws1_ref, wv1_ref, ws2_ref, wv2_ref, ms_ref,
    mv_ref, m2_ref, readout_ref,
    first_ref, out_ref, last_ref, list_ref, radial_ref, square_ref,
    wide_ref,
):
    for i, ref in enumerate((ws1_ref, wv1_ref, ws2_ref, wv2_ref)):
        radial_ref[K * i : K * i + K, :] = ref[...]
    radial_ref[4 * K : 4 * K + 1, :] = readout_ref[...]
    for i, ref in enumerate((ms_ref, mv_ref, m2_ref)):
        square_ref[C * i : C * i + C, :] = ref[...]
    wide_ref[...] = jnp.zeros_like(wide_ref)
    wide_ref[0 : table_ref.shape[0], :] = table_ref[...].astype(F32)
    square_ref[3 * C : 4 * C, :] = wide_ref[...].astype(BF16)
    n = jnp.int32(0)
    block_id = lax.broadcasted_iota(jnp.int32, (8, 128), 0)
    mask = jnp.zeros((8, 128), jnp.int32)
    for p in range(codes_ref.shape[2]):
        code = codes_ref[0, 0, p]
        block = lax.shift_right_logical(code * 57, 9)
        offset = code - 9 * block
        bit = jnp.where(p < count_ref[0, 0], lax.shift_left(1, offset), 0)
        mask = mask + jnp.where(block_id == block, bit, 0)
        over = lax.shift_right_logical(offset * 11, 5)
        far = block + over - 1
        inside = (bit > 0) & (offset - 3 * over == 1) & (far >= 0) & (far < BX)
        list_ref[n] = block + (far + EX + 1) * 8 + jnp.where(offset == 4, 256, 0)
        n = n + jnp.where(inside, 1, 0)
    for i in range(3):
        list_ref[n + i] = E * 8
    list_ref[END] = n + (n & 1)
    mask = mask.astype(F32)
    for h in range(BX):
        places = [(out_ref, h)]
        if h == 0:
            places.append((first_ref, 0))
        if h == BX - 1:
            places.append((last_ref, 0))
        for ref, i in places:
            for d in range(3):
                ref[i, d : d + 1, :] = pos_ref[h, d]
            ref[i, 3:4, :] = species_ref[h].astype(F32)
            ref[i, 4:5, :] = mask[h : h + 1, :]
            ref[i, 5:8, :] = jnp.zeros((3, 128), F32)


def gather_ext(lo_ref, mid_ref, hi_ref, ext_ref):
    for row, ref in enumerate((lo_ref, mid_ref, hi_ref)):
        for x in range(EX):
            ext_ref[row * EX + x] = ref[x]
    ext_ref[E : E + 8] = jnp.full((8, 8, A), 1.0e4, F32)


def send_masks(ext_ref, maskv_ref, masks_ref, sem):
    for e in range(E):
        maskv_ref[e : e + 1, :] = ext_ref[e, 4:5, :].astype(jnp.int32)
    copy = pltpu.make_async_copy(maskv_ref, masks_ref, sem)
    copy.start()
    return copy


def make_list(parts, masks_ref, list_ref):
    n = jnp.int32(0)
    places = (MIDDLE, END) if len(parts) == 2 else (MIDDLE, THIRD, END)
    for pairs, place in zip(parts, places):
        held = None
        for own, other, lister, o in sorted(pairs, key=lambda pair: pair[2]):
            if lister != held:
                held, mask = lister, masks_ref[lister, 0]
            list_ref[n] = own + other * 8 + (256 if o == 4 else 0)
            n = n + (lax.shift_right_logical(mask, o) & 1)
        for i in range(3):
            list_ref[n + i] = E * 8
        n = n + (n & 1)
        list_ref[place] = n


def entry(list_ref, p):
    code = list_ref[p]
    own = code & 7
    other = lax.shift_right_logical(code, 3) & 31
    bias = jnp.where(code >= 256, 0, 1024)
    return own, other, bias


def turned_blocks(ext_ref):
    return [ext_ref[0:16].reshape(128, A).T, ext_ref[16:32].reshape(128, A).T]


def spread_lane(turned, e, d):
    lane = 8 * (e % 16) + d
    return jnp.broadcast_to(turned[e // 16][:, lane : lane + 1], (A, 128))


def geometry(col_ref, i, row, r, sign, bias, rows=ROWS):
    off = [sign * (row[d] - col_ref[i, d, pl.ds(r, rows), :]) for d in range(3)]
    squared = off[0] * off[0] + off[1] * off[1] + off[2] * off[2]
    soft = squared + 0.25
    inv = lax.rsqrt(soft)
    s = soft * inv
    taper = jnp.maximum(1.0 - squared * (1.0 / 36.0), 0.0)
    at = lax.broadcasted_iota(jnp.int32, (rows, 128), 0) + (r + bias)
    lane = lax.broadcasted_iota(jnp.int32, (rows, 128), 1)
    taper = jnp.where(at == lane, 0.0, taper)
    u = jnp.minimum(s, 6.25) * (1.0 / SIGMA) - 0.5
    base = taper * jnp.exp(-u * u)
    step = jnp.exp(2.0 * u - 1.0)
    q = [base]
    for k in range(1, K):
        q.append(q[-1] * (step * EXPS[k]))
    return off, inv, taper, u, q


EXPS = [1.0, 1.0, 0.1353352832366127, 0.01831563888873418]


def store_tiles(put, off, inv, taper, q):
    direction = [o * inv for o in off]
    for k in range(K):
        radial = taper * q[k]
        put(0, k, radial.astype(BF16))
        for d in range(3):
            put(1 + d, k, (radial * direction[d]).astype(BF16))


def pull_back(grads, off, inv, taper, u, q):
    direction = [o * inv for o in off]
    s0 = s1 = None
    dg = [None] * 3
    for k in reversed(range(K)):
        tilted = [grads(1 + d, k) for d in range(3)]
        along = tilted[0] * direction[0] + tilted[1] * direction[1] + tilted[2] * direction[2]
        p = (grads(0, k) + along) * q[k]
        s0 = p if s0 is None else s0 + p
        if k:
            s1 = s0 if s1 is None else s1 + s0
        for d in range(3):
            v = tilted[d] * q[k]
            dg[d] = v if dg[d] is None else dg[d] + v
    turn = dg[0] * direction[0] + dg[1] * direction[1] + dg[2] * direction[2]
    bend = (2.0 / SIGMA) * (u * s0 - s1) + turn * inv
    pull = taper * inv
    weight = s0 * (1.0 / 9.0) + pull * bend
    return [dg[d] * pull - weight * off[d] for d in range(3)]


def rows_of(ext_ref, e):
    return [ext_ref[e, d : d + 1, :] for d in range(3)]


def scaled(feature, weights_ref, k):
    return (feature.astype(F32) * weights_ref[k : k + 1, :]).astype(BF16)


def first_sums(
    end, list_ref, col_ref, near, rows, where, scaled_s_ref, scaled_v_ref, acc_ref, tile_a_ref,
    tile_b_ref,
):
    def first_tiles(p, tile_ref, r):
        own, other, bias = entry(list_ref, p)
        row = rows(where(other))
        off, inv, taper, u, q = geometry(col_ref, own + near, row, r, 1.0, bias)

        def put(g, k, tile):
            tile_ref[pl.ds(g * A + r, ROWS), pl.ds(k * A, A)] = tile

        store_tiles(put, off, inv, taper, q)

    def first_sum(p, tile_ref, g):
        own, other, _ = entry(list_ref, p)
        part = pl.ds(g * A, A)
        acc_ref[own, part, :] += dot(tile_ref[part, :], (scaled_v_ref if g else scaled_s_ref)[where(other)])

    def first_half(p, this_ref, next_ref):
        for g in range(4):
            first_sum(p, this_ref, g)
            for r in range(g * 32, g * 32 + 32, ROWS):
                first_tiles(p + 1, next_ref, r)

    def first(i, carry):
        first_half(2 * i, tile_a_ref, tile_b_ref)
        first_half(2 * i + 1, tile_b_ref, tile_a_ref)
        return carry

    for r in range(0, A, ROWS):
        first_tiles(0, tile_a_ref, r)
    lax.fori_loop(0, half(end), first, 0)


def own_kernel(
    own_ref, list_ref, radial_ref, square_ref,
    acc_ref,
    ext_ref, col_ref, scaled_s_ref, scaled_v_ref, tile_a_ref, tile_b_ref,
):
    ws1_ref, wv1_ref, _, _, _ = radial_parts(radial_ref)
    table = square_parts(square_ref)[3][...]
    for h in range(BX):
        ext_ref[h] = own_ref[h]
    ext_ref[BX] = jnp.full((8, A), 1.0e4, F32)
    for h in range(BX + 1, 16):
        ext_ref[h] = jnp.zeros((8, A), F32)
    turned = [ext_ref[0:16].reshape(128, A).T]
    lanes = lax.broadcasted_iota(jnp.int32, (A, 128), 1).astype(F32)
    acc_ref[...] = jnp.zeros_like(acc_ref)
    for h in range(BX):
        for d in range(3):
            col_ref[h, d] = spread_lane(turned, h, d)
        hot = (spread_lane(turned, h, 3) == lanes).astype(BF16)
        initial = dot(hot, table).astype(BF16)
        for k in range(K):
            scaled_s_ref[h, pl.ds(k * A, A), :] = scaled(initial, ws1_ref, k)
            scaled_v_ref[h, pl.ds(k * A, A), :] = scaled(initial, wv1_ref, k)
    scaled_s_ref[BX] = jnp.zeros((K * A, C), BF16)
    scaled_v_ref[BX] = jnp.zeros((K * A, C), BF16)
    first_sums(
        list_ref[END], list_ref, col_ref, 0, lambda e: rows_of(ext_ref, e),
        lambda e: jnp.minimum(e - EX - 1, BX), scaled_s_ref, scaled_v_ref, acc_ref, tile_a_ref,
        tile_b_ref,
    )


def forward_kernel(
    lo_ref, mid_ref, hi_ref, acc_own_ref, radial_ref, square_ref,
    pre_ref, feat_ref, out_lo_ref, out_hi_ref, scaled_s_ref, scaled_v_ref, ready_ref, keep_col_ref,
    list1_ref, list2_ref,
    ext_ref, col_ref, init_ref, acc_ref, tile_a_ref, tile_b_ref, wide_a_ref, wide_b_ref, total_ref,
    maskv_ref, masks_ref, sem,
):
    ws1_ref, wv1_ref, ws2_ref, wv2_ref, _ = radial_parts(radial_ref)
    ms_ref, mv_ref, _, table_ref = square_parts(square_ref)
    gather_ext(lo_ref, mid_ref, hi_ref, ext_ref)
    copy = send_masks(ext_ref, maskv_ref, masks_ref, sem)
    turned = turned_blocks(ext_ref)
    lanes = lax.broadcasted_iota(jnp.int32, (A, 128), 1).astype(F32)
    for e in range(E):
        if e == 8:
            copy.wait()
            make_list(HOME_PAIRS, masks_ref, list1_ref)
            make_list(FAR_PAIRS, masks_ref, list2_ref)
        for d in range(3):
            column = spread_lane(turned, e, d)
            col_ref[e, d] = column
            if EX <= e < 2 * EX:
                keep_col_ref[e - EX, d] = column
        hot = (spread_lane(turned, e, 3) == lanes).astype(BF16)
        init_ref[e] = dot(hot, table_ref[...]).astype(BF16)
    col_ref[E] = jnp.full((3, A, 128), 1.0e4, F32)
    keep_col_ref[EX] = jnp.full((3, A, 128), 1.0e4, F32)

    def scale_block(e, carry):
        for k in range(K):
            scaled_s_ref[e, pl.ds(k * A, A), :] = scaled(init_ref[e], ws1_ref, k)
            scaled_v_ref[e, pl.ds(k * A, A), :] = scaled(init_ref[e], wv1_ref, k)
        return carry

    lax.fori_loop(0, E, scale_block, 0)
    scaled_s_ref[E] = jnp.zeros((K * A, C), BF16)
    scaled_v_ref[E] = jnp.zeros((K * A, C), BF16)
    acc_ref[...] = acc_own_ref[...]
    total_ref[...] = jnp.zeros_like(total_ref)
    first_sums(
        list1_ref[MIDDLE], list1_ref, col_ref, EX + 1, lambda e: rows_of(ext_ref, e), lambda e: e,
        scaled_s_ref, scaled_v_ref, acc_ref, tile_a_ref, tile_b_ref,
    )
    for h in range(BX):
        pre = dot((acc_ref[h, 0:A, :] * 0.125).astype(BF16), ms_ref[...])
        pre_ref[h] = pre
        scalar = (init_ref[h + EX + 1].astype(F32) + pre * jax.nn.sigmoid(pre)).astype(BF16)
        vector = dot((acc_ref[h, A : 4 * A, :] * 0.125).astype(BF16), mv_ref[...]).astype(BF16)
        feat_ref[h, 0:A, :] = scalar
        feat_ref[h, A : 4 * A, :] = vector
        for k in range(K):
            ready_ref[h, pl.ds(k * A, A), :] = scaled(scalar, ws2_ref, k)
            for d in range(3):
                ready_ref[h, pl.ds(((1 + d) * K + k) * A, A), :] = scaled(
                    vector[d * A : (d + 1) * A, :], wv2_ref, k
                )
    second_sums(
        0, list2_ref[MIDDLE], list2_ref, col_ref, 0, lambda own: rows_of(ext_ref, own + EX + 1),
        ready_ref, total_ref, wide_a_ref, wide_b_ref,
    )
    for x in range(EX):
        out_lo_ref[x] = total_ref[x].astype(BF16)
        out_hi_ref[x] = total_ref[2 * EX + x].astype(BF16)


def place(other, shift):
    return jnp.minimum(other - shift, EX) if shift else other


def second_sums(
    start, end, list_ref, col_ref, shift, rows, ready_ref, total_ref, wide_a_ref, wide_b_ref
):
    def second_tiles(p, wide_ref, r):
        own, other, bias = entry(list_ref, p)
        row = rows(own)
        off, inv, taper, u, q = geometry(col_ref, place(other, shift), row, r, 1.0, bias)

        def put(g, k, tile):
            wide_ref[pl.ds(r, ROWS), pl.ds((g * K + k) * A, A)] = tile

        store_tiles(put, off, inv, taper, q)

    def second_half(p, this_ref, next_ref):
        own, other, _ = entry(list_ref, p)
        for g in range(4):
            part = pl.ds(g * K * A, K * A)
            total_ref[place(other, shift)] += dot(this_ref[:, part], ready_ref[own, part, :])
            for r in range(g * 32, g * 32 + 32, ROWS):
                second_tiles(p + 1, next_ref, r)

    def second(i, carry):
        second_half(2 * i, wide_a_ref, wide_b_ref)
        second_half(2 * i + 1, wide_b_ref, wide_a_ref)
        return carry

    for r in range(0, A, ROWS):
        second_tiles(start, wide_a_ref, r)
    lax.fori_loop(half(start), half(end), second, 0)


def forward_inner_kernel(
    mid_ref, list2_ref, ready_ref, col_ref, out_ref, wide_a_ref, wide_b_ref, total_ref
):
    total_ref[...] = jnp.zeros_like(total_ref)
    second_sums(
        list2_ref[MIDDLE], list2_ref[END], list2_ref, col_ref, EX,
        lambda own: rows_of(mid_ref, own + 1), ready_ref, total_ref, wide_a_ref, wide_b_ref,
    )
    out_ref[...] = total_ref[0:EX]


def radial_parts(ref):
    return [ref.at[pl.ds(K * i, K if i < 4 else 1), :] for i in range(5)]


def square_parts(ref):
    return [ref.at[pl.ds(C * i, C), :] for i in range(4)]


def half(n):
    return lax.shift_right_logical(n, 1)


def slope_of(value):
    sigma = jax.nn.sigmoid(value)
    return sigma * (1.0 + value * (1.0 - sigma))


def middle(msg, x, feat_ref, radial_ref, square_ref, energy_ref):
    readout = radial_parts(radial_ref)[4][...]
    mix_ref = square_parts(square_ref)[2]
    pre = dot((msg * 0.125).astype(BF16), mix_ref[...])
    sigma = jax.nn.sigmoid(pre)
    if 1 <= x <= BX:
        part = (feat_ref[x - 1, 0:A, :].astype(F32) + pre * sigma) * readout
        energy_ref[x - 1] = jnp.sum(part.T, axis=0, keepdims=True)
    grad = (readout * (sigma * (1.0 + pre * (1.0 - sigma)))).astype(BF16)
    return dot_nt(grad, mix_ref[...]) * 0.125


def message(mid_ref, below_ref, above_ref, x):
    return mid_ref[x] + below_ref[x].astype(F32) + above_ref[x].astype(F32)


def middle_inner_kernel(
    mid_ref, below_ref, above_ref, ext_mid_ref, list2_ref, feat_ref, col_ref, radial_ref, square_ref,
    energy_ref, second_in_ref, acc_ref, across_ref, down_ref,
    ext_ref, second_ref, cot_s_ref, cot_v_ref, tile_a_ref, tile_b_ref, grad_a_ref, grad_b_ref,
):
    _, _, ws2_ref, wv2_ref, _ = radial_parts(radial_ref)
    for x in range(EX):
        ext_ref[x] = ext_mid_ref[x]
    ext_ref[EX] = jnp.full((8, A), 1.0e4, F32)
    for x in INNER:
        second = middle(
            message(mid_ref, below_ref, above_ref, x), x, feat_ref, radial_ref, square_ref, energy_ref
        )
        second_ref[x] = second
        second_in_ref[x] = second.astype(BF16)
    acc_ref[...] = jnp.zeros_like(acc_ref)
    down_ref[...] = jnp.zeros_like(down_ref)
    across_ref[...] = jnp.zeros_like(across_ref)
    cotangents(second_ref, cot_s_ref, cot_v_ref, 0, ws2_ref, wv2_ref, INNER)
    second_moves(
        list2_ref[MIDDLE], list2_ref[THIRD], list2_ref, col_ref, EX, lambda e: rows_of(ext_ref, e),
        feat_ref, cot_s_ref, cot_v_ref, acc_ref, across_ref, down_ref, tile_a_ref, tile_b_ref,
        grad_a_ref, grad_b_ref,
    )


def middle_kernel(
    mid_ref, below_ref, above_ref, left_ref, right_ref, feat_ref, radial_ref, square_ref,
    energy_part_ref, second_part_ref,
    energy_ref, second_in_ref, second_own_ref,
):
    for x in OUTER:
        msg = message(mid_ref, below_ref, above_ref, x)
        if x < 2:
            msg = msg + left_ref[x].astype(F32)
        else:
            msg = msg + right_ref[x - EX + 2].astype(F32)
        second = middle(msg, x, feat_ref, radial_ref, square_ref, energy_ref)
        second_own_ref[x] = second
        second_in_ref[x] = second.astype(BF16)
    for x in INNER:
        energy_ref[x - 1] = energy_part_ref[x - 1]
        second_in_ref[x] = second_part_ref[x]
        second_own_ref[x] = jnp.zeros((A, C), F32)


def move(across_ref, own, r, near, own_sign, grad_ref):
    def grads(g, k):
        return grad_ref[pl.ds(g * A + r, ROWS), pl.ds(k * A, A)]

    parts = []
    for d, moved in enumerate(pull_back(grads, *near)):
        if own_sign > 0:
            across_ref[own, d, pl.ds(r, ROWS), :] += moved
        else:
            across_ref[own, d, pl.ds(r, ROWS), :] -= moved
        part = moved[0:8]
        for i in range(8, ROWS, 8):
            part = part + moved[i : i + 8]
        parts.append(part)
    return parts


def add_down(down_ref, other, own_sign, sums):
    for d in range(3):
        down_ref[other, d] -= own_sign * sums[d]


def plus(sums, parts):
    return parts if sums is None else [a + b for a, b in zip(sums, parts)]


def first_moves(
    start, end, list_ref, col_ref, shift, rows, inward_ref, scaled_s_ref, scaled_v_ref, across_ref,
    down_ref, grad_a_ref, grad_b_ref,
):
    def first_grads(p, grad_ref):
        own, other, _ = entry(list_ref, p)
        grad_ref[0:A, :] = dot_nt(inward_ref[own, 0:A, :], scaled_s_ref[other])
        grad_ref[A : 4 * A, :] = dot_nt(inward_ref[own, A : 4 * A, :], scaled_v_ref[other])

    def first_move(p, grad_ref):
        own, other, bias = entry(list_ref, p)
        row = rows(place(other, shift))
        sums = None
        for r in range(0, A, ROWS):
            near = geometry(col_ref, own + 1, row, r, 1.0, bias)
            sums = plus(sums, move(across_ref, own, r, near, -1.0, grad_ref))
        add_down(down_ref, place(other, shift), -1.0, sums)

    def first_back(i, carry):
        p = 2 * i
        first_grads(p + 1, grad_b_ref)
        first_move(p, grad_a_ref)
        first_grads(p + 2, grad_a_ref)
        first_move(p + 1, grad_b_ref)
        return carry

    first_grads(start, grad_a_ref)
    lax.fori_loop(half(start), half(end), first_back, 0)


def line_of(down_ref, across_ref, e, x, d):
    line = jnp.sum(down_ref[e, d], axis=0, keepdims=True)
    if x is not None and 1 <= x <= BX:
        line = line + jnp.sum(across_ref[x - 1, d].T, axis=0, keepdims=True)
    return line


def second_moves(
    start, end, list_ref, col_ref, shift, rows, feat_ref, cot_s_ref, cot_v_ref, acc_ref, across_ref,
    down_ref, tile_a_ref, tile_b_ref, grad_a_ref, grad_b_ref,
):
    def second_grads(p, grad_ref):
        own, other, _ = entry(list_ref, p)
        source = place(other, shift)
        grad_ref[0:A, :] = dot_nt(feat_ref[own, 0:A, :], cot_s_ref[source])
        grad_ref[A : 4 * A, :] = dot_nt(feat_ref[own, A : 4 * A, :], cot_v_ref[source])

    def second_move(p, grad_ref, tile_ref):
        own, other, bias = entry(list_ref, p)
        source = place(other, shift)
        row = rows(source)
        sums = None
        for r in range(0, A, ROWS):
            near = geometry(col_ref, own + 1, row, r, -1.0, bias)
            off, inv, taper, u, q = near

            def put(g, k, tile):
                tile_ref[pl.ds(g * A + r, ROWS), pl.ds(k * A, A)] = tile

            store_tiles(put, off, inv, taper, q)
            sums = plus(sums, move(across_ref, own, r, near, 1.0, grad_ref))
        add_down(down_ref, source, 1.0, sums)

    def second_sum(own, source, tile_ref):
        acc_ref[own, 0:A, :] += dot(tile_ref[0:A, :], cot_s_ref[source])
        acc_ref[own, A : 4 * A, :] += dot(tile_ref[A : 4 * A, :], cot_v_ref[source])

    def second_back(i, carry):
        p = 2 * i
        own, other, _ = entry(list_ref, p)
        second_sum(*carry, tile_b_ref)
        second_grads(p + 1, grad_b_ref)
        second_move(p, grad_a_ref, tile_a_ref)
        second_sum(own, place(other, shift), tile_a_ref)
        second_grads(p + 2, grad_a_ref)
        second_move(p + 1, grad_b_ref, tile_b_ref)
        own, other, _ = entry(list_ref, p + 1)
        return own, place(other, shift)

    empty = EX if shift else E
    for ref in (cot_s_ref, cot_v_ref):
        ref[empty] = jnp.zeros((K * A, C), BF16)
    tile_b_ref[...] = jnp.zeros_like(tile_b_ref)
    second_grads(start, grad_a_ref)
    last = lax.fori_loop(half(start), half(end), second_back, (jnp.int32(0), jnp.int32(empty)))
    second_sum(*last, tile_b_ref)


def cotangents(ref, cot_s_ref, cot_v_ref, first, ws2_ref, wv2_ref, blocks=range(EX)):
    for x in blocks:
        for k in range(K):
            cot_s_ref[first + x, pl.ds(k * A, A), :] = scaled(ref[x], ws2_ref, k)
            cot_v_ref[first + x, pl.ds(k * A, A), :] = scaled(ref[x], wv2_ref, k)


def backward_outer_two_kernel(
    mid_ref, list2_ref, in_mid_ref, feat_ref, col_ref, radial_ref, acc_in_ref, across_in_ref,
    down_in_ref,
    acc_ref, across_ref, down_ref,
    ext_ref, cot_s_ref, cot_v_ref, tile_a_ref, tile_b_ref, grad_a_ref, grad_b_ref,
):
    _, _, ws2_ref, wv2_ref, _ = radial_parts(radial_ref)
    for x in range(EX):
        ext_ref[x] = mid_ref[x]
    ext_ref[EX] = jnp.full((8, A), 1.0e4, F32)
    acc_ref[...] = acc_in_ref[...]
    down_ref[...] = down_in_ref[...]
    across_ref[...] = across_in_ref[...]
    cotangents(in_mid_ref, cot_s_ref, cot_v_ref, 0, ws2_ref, wv2_ref, OUTER)
    second_moves(
        list2_ref[THIRD], list2_ref[END], list2_ref, col_ref, EX, lambda e: rows_of(ext_ref, e),
        feat_ref, cot_s_ref, cot_v_ref, acc_ref, across_ref, down_ref, tile_a_ref, tile_b_ref,
        grad_a_ref, grad_b_ref,
    )


def backward_kernel(
    lo_ref, mid_ref, hi_ref, list1_ref, list2_ref, acc_in_ref, across_in_ref, down_in_ref, feat_ref,
    pre_ref, in_lo_ref, in_hi_ref, scaled_s_ref, scaled_v_ref, col_ref, radial_ref, square_ref,
    out_lo_ref, out_mid_ref, out_hi_ref, inward_ref,
    ext_ref, cot_s_ref, cot_v_ref, acc_ref, tile_a_ref, tile_b_ref, grad_a_ref, grad_b_ref,
    down_ref, across_ref,
):
    _, _, ws2_ref, wv2_ref, readout_ref = radial_parts(radial_ref)
    ms_ref, mv_ref, _, _ = square_parts(square_ref)
    gather_ext(lo_ref, mid_ref, hi_ref, ext_ref)
    acc_ref[...] = acc_in_ref[...]
    across_ref[...] = across_in_ref[...]
    down_ref[0:EX] = jnp.zeros((EX, 3, 8, A), F32)
    down_ref[EX : 2 * EX] = down_in_ref[0:EX]
    down_ref[2 * EX : E + 1] = jnp.zeros((EX + 1, 3, 8, A), F32)
    cotangents(in_lo_ref, cot_s_ref, cot_v_ref, 0, ws2_ref, wv2_ref)
    cotangents(in_hi_ref, cot_s_ref, cot_v_ref, 2 * EX, ws2_ref, wv2_ref)
    second_moves(
        0, list2_ref[MIDDLE], list2_ref, col_ref, 0, lambda e: rows_of(ext_ref, e), feat_ref,
        cot_s_ref, cot_v_ref, acc_ref, across_ref, down_ref, tile_a_ref, tile_b_ref, grad_a_ref,
        grad_b_ref,
    )
    for h in range(BX):
        slope = (readout_ref[...] + acc_ref[h, 0:A, :]) * slope_of(pre_ref[h])
        inward_ref[h, 0:A, :] = (dot_nt(slope.astype(BF16), ms_ref[...]) * 0.125).astype(BF16)
        inward_ref[h, A : 4 * A, :] = (
            dot_nt(acc_ref[h, A : 4 * A, :].astype(BF16), mv_ref[...]) * 0.125
        ).astype(BF16)
    first_moves(
        0, list1_ref[MIDDLE], list1_ref, col_ref, 0, lambda e: rows_of(ext_ref, e), inward_ref,
        scaled_s_ref, scaled_v_ref, across_ref, down_ref, grad_a_ref, grad_b_ref,
    )
    for row, ref in enumerate((out_lo_ref, out_mid_ref, out_hi_ref)):
        for x in range(EX):
            for d in range(3):
                line = line_of(down_ref, across_ref, row * EX + x, x if row == 1 else None, d)
                ref[x, d : d + 1, :] = line


def backward_inner_kernel(
    mid_ref, list1_ref, scaled_s_ref, scaled_v_ref, col_ref, inward_ref, out_ref,
    ext_ref, grad_a_ref, grad_b_ref, down_ref, across_ref,
):
    for x in range(EX):
        ext_ref[x] = mid_ref[x]
    ext_ref[EX] = jnp.full((8, A), 1.0e4, F32)
    down_ref[...] = jnp.zeros_like(down_ref)
    across_ref[...] = jnp.zeros_like(across_ref)
    first_moves(
        list1_ref[MIDDLE], list1_ref[END], list1_ref, col_ref, EX, lambda e: rows_of(ext_ref, e),
        inward_ref, scaled_s_ref, scaled_v_ref, across_ref, down_ref, grad_a_ref, grad_b_ref,
    )
    for x in range(EX):
        for d in range(3):
            out_ref[x, d : d + 1, :] = line_of(down_ref, across_ref, x, x, d)


VMEM = pl.BlockSpec(memory_space=pltpu.VMEM)
SMEM = pl.BlockSpec(memory_space=pltpu.SMEM)
PARAMS = pltpu.CompilerParams(vmem_limit_bytes=24 * 1024 * 1024)


SEM = pltpu.SemaphoreType.DMA


def forward_call(*args):
    return call(
        forward_kernel,
        args,
        [
            ((BX, A, C), F32),
            ((BX, 4 * A, C), BF16),
            ((EX, A, C), BF16),
            ((EX, A, C), BF16),
            ((E + 1, K * A, C), BF16),
            ((E + 1, K * A, C), BF16),
            ((BX, 4 * K * A, C), BF16),
            ((EX + 1, 3, A, 128), F32),
            ((64,), jnp.int32),
            ((64,), jnp.int32),
        ],
        [
            pltpu.VMEM((E + 8, 8, A), F32),
            pltpu.VMEM((E + 1, 3, A, 128), F32),
            pltpu.VMEM((E, A, C), BF16),
            pltpu.VMEM((BX, 4 * A, C), F32),
            pltpu.VMEM((4 * A, K * A), BF16),
            pltpu.VMEM((4 * A, K * A), BF16),
            pltpu.VMEM((A, 4 * K * A), BF16),
            pltpu.VMEM((A, 4 * K * A), BF16),
            pltpu.VMEM((E + 1, A, C), F32),
            pltpu.VMEM((E, 128), jnp.int32),
            pltpu.SMEM((E, 128), jnp.int32),
            SEM,
        ],
        out_specs=[VMEM] * 8 + [SMEM] * 2,
    )


def forward_inner_call(*args):
    return call(
        forward_inner_kernel,
        args,
        [((EX, A, C), F32)],
        [
            pltpu.VMEM((A, 4 * K * A), BF16),
            pltpu.VMEM((A, 4 * K * A), BF16),
            pltpu.VMEM((EX + 1, A, C), F32),
        ],
        in_specs=[VMEM, SMEM, VMEM, VMEM],
        cost=pl.CostEstimate(flops=4 * 10**9, bytes_accessed=10**6, transcendentals=0),
    )


LONG = pl.CostEstimate(flops=4 * 10**9, bytes_accessed=10**6, transcendentals=0)
HELD = [((BX, 4 * A, C), F32), ((BX, 3, A, 128), F32), ((EX + 1, 3, 8, A), F32)]
ROW_SCRATCH = [
    pltpu.VMEM((EX + 1, K * A, C), BF16),
    pltpu.VMEM((EX + 1, K * A, C), BF16),
    pltpu.VMEM((4 * A, K * A), BF16),
    pltpu.VMEM((4 * A, K * A), BF16),
    pltpu.VMEM((4 * A, K * A), F32),
    pltpu.VMEM((4 * A, K * A), F32),
]


def own_call(*args):
    return call(
        own_kernel,
        args,
        [((BX, 4 * A, C), F32)],
        [
            pltpu.VMEM((16, 8, A), F32),
            pltpu.VMEM((BX, 3, A, 128), F32),
            pltpu.VMEM((BX + 1, K * A, C), BF16),
            pltpu.VMEM((BX + 1, K * A, C), BF16),
            pltpu.VMEM((4 * A, K * A), BF16),
            pltpu.VMEM((4 * A, K * A), BF16),
        ],
        in_specs=[VMEM, SMEM, VMEM, VMEM],
        cost=LONG,
    )


def middle_inner_call(*args):
    return call(
        middle_inner_kernel,
        args,
        [((BX, 1, A), F32), ((EX, A, C), BF16), *HELD],
        [pltpu.VMEM((EX + 1, 8, A), F32), pltpu.VMEM((EX, A, C), F32), *ROW_SCRATCH],
        in_specs=[VMEM] * 4 + [SMEM] + [VMEM] * 4,
        cost=LONG,
    )


def backward_outer_two_call(*args):
    return call(
        backward_outer_two_kernel,
        args,
        HELD,
        [pltpu.VMEM((EX + 1, 8, A), F32), *ROW_SCRATCH],
        in_specs=[VMEM, SMEM] + [VMEM] * 7,
        cost=LONG,
    )


def backward_call(*args):
    return call(
        backward_kernel,
        args,
        [*[((EX, 3, A), F32)] * 3, ((BX, 4 * A, C), BF16)],
        [
            pltpu.VMEM((E + 8, 8, A), F32),
            pltpu.VMEM((E + 1, K * A, C), BF16),
            pltpu.VMEM((E + 1, K * A, C), BF16),
            pltpu.VMEM((BX, 4 * A, C), F32),
            pltpu.VMEM((4 * A, K * A), BF16),
            pltpu.VMEM((4 * A, K * A), BF16),
            pltpu.VMEM((4 * A, K * A), F32),
            pltpu.VMEM((4 * A, K * A), F32),
            pltpu.VMEM((E + 1, 3, 8, A), F32),
            pltpu.VMEM((BX, 3, A, 128), F32),
        ],
        in_specs=[VMEM] * 3 + [SMEM] * 2 + [VMEM] * 12,
    )


def backward_inner_call(*args):
    return call(
        backward_inner_kernel,
        args,
        [((EX, 3, A), F32)],
        [
            pltpu.VMEM((EX + 1, 8, A), F32),
            pltpu.VMEM((4 * A, K * A), F32),
            pltpu.VMEM((4 * A, K * A), F32),
            pltpu.VMEM((EX + 1, 3, 8, A), F32),
            pltpu.VMEM((BX, 3, A, 128), F32),
        ],
        in_specs=[VMEM, SMEM, VMEM, VMEM, VMEM, VMEM],
        cost=pl.CostEstimate(flops=4 * 10**9, bytes_accessed=10**6, transcendentals=0),
    )


def call(kernel, args, outs, scratch=(), in_specs=None, out_specs=None, cost=None, params=PARAMS):
    return pl.pallas_call(
        kernel,
        out_shape=[jax.ShapeDtypeStruct(s, d) for s, d in outs],
        in_specs=in_specs or [VMEM] * len(args),
        out_specs=out_specs or [VMEM] * len(outs),
        scratch_shapes=list(scratch),
        compiler_params=params,
        cost_estimate=cost,
    )(*args)


def along(block, axis, step):
    size = lax.axis_size(axis)
    return lax.ppermute(block, axis, [(i, i + step) for i in range(size) if 0 <= i + step < size])


def both(lo, hi, axis, step=1):
    return along(lo, axis, step), along(hi, axis, -step)


def local(
    positions, species, pair_codes, pair_count, embed_table, ws1, wv1, ws2, wv2, ms, mv, m2, readout
):
    first, own, last, own_list, radial, square = call(
        pack_kernel,
        (
            positions.transpose(0, 2, 1, 3), species, pair_codes, pair_count, embed_table, ws1, wv1,
            ws2, wv2, ms, mv, m2, readout.reshape(1, C),
        ),
        [
            ((1, 8, A), F32),
            ((BX, 8, A), F32),
            ((1, 8, A), F32),
            ((64,), jnp.int32),
            ((24, C), F32),
            ((4 * C, C), BF16),
        ],
        [pltpu.VMEM((C, C), F32)],
        in_specs=[VMEM] * 2 + [SMEM] * 2 + [VMEM] * 9,
        out_specs=[VMEM] * 3 + [SMEM] + [VMEM] * 2,
        params=pltpu.CompilerParams(vmem_limit_bytes=60 * 1024 * 1024),
    )
    left, right = both(last, first, "gx")
    (acc,) = own_call(own, own_list, radial, square)
    own, acc = lax.optimization_barrier((own, acc))
    ext_mid = jnp.concatenate([left, own, right], axis=0)
    ext_lo, ext_hi = both(ext_mid, ext_mid, "gy")
    ext = (ext_lo, ext_mid, ext_hi)
    pre, feat, lo, hi, scaled_s, scaled_v, ready, col, list1, list2 = forward_call(
        *ext, acc, radial, square
    )
    below, above = both(hi, lo, "gy")
    (mid,) = forward_inner_call(ext_mid, list2, ready, col)
    edge = lambda x: (mid[x : x + 2] + below[x : x + 2] + above[x : x + 2]).astype(BF16)
    left, right = both(edge(EX - 2), edge(0), "gx")
    energy, inner, *held = middle_inner_call(
        mid, below, above, ext_mid, list2, feat, col, radial, square
    )
    energy, inner, inner_own = call(
        middle_kernel,
        (mid, below, above, left, right, feat, radial, square, energy, inner),
        [((BX, 1, A), F32), ((EX, A, C), BF16), ((EX, A, C), F32)],
    )
    in_lo, in_hi = both(inner, inner, "gy")
    held = backward_outer_two_call(ext_mid, list2, inner_own, feat, col, radial, *held)
    lo, mid, hi, inward = backward_call(
        *ext, list1, list2, *held, feat, pre, in_lo, in_hi, scaled_s, scaled_v, col, radial, square
    )
    below, above = both(hi, lo, "gy")
    (more,) = backward_inner_call(ext_mid, list1, scaled_s, scaled_v, col, inward)
    total = mid + below + above
    left, right = both(total[EX - 1 :], total[:1], "gx")
    total = total[1 : BX + 1] + more[1 : BX + 1]
    total = total + jnp.concatenate([left, jnp.zeros((BX - 2, 3, A), F32), right], axis=0)
    return energy, -total.reshape(BX, 1, 3, A)


def solution(mesh):
    in_specs = (
        P("gx", "gy", None, None),
        P("gx", "gy", None),
        P("gx", "gy", None),
        P("gx", "gy"),
        *[P()] * 9,
    )
    out_specs = (P("gx", "gy", None), P("gx", "gy", None, None))
    return jax.shard_map(local, mesh=mesh, in_specs=in_specs, out_specs=out_specs, check_vma=False)
```

```python
import jax
import jax.numpy as jnp
from jax import lax
from jax.experimental import pallas as pl
from jax.experimental.pallas import tpu as pltpu
from jax.sharding import PartitionSpec as P

BX = 6
EX = 8
A = 128
C = 128
K = 4
ROWS = 16
F32 = jnp.float32
BF16 = jnp.bfloat16
SIGMA = 1.5
NT = (((1,), (1,)), ((), ()))
E = 3 * EX

def home_part(e):
    return 0 if e % EX in (0, EX - 1) else 1 if e // EX != 1 else 2


HOME_PAIRS = [
    [
        (h, (o % 3) * EX + h + o // 3, EX + 1 + h, o)
        for h in range(BX)
        for o in range(9)
        if home_part((o % 3) * EX + h + o // 3) == part
    ]
    for part in range(3)
]


def far_part(e):
    return 0 if e // EX != 1 else 1 if 2 <= e % EX < EX - 2 else 2


FAR_PAIRS = [
    [
        (f, (2 - o % 3) * EX + f + 2 - o // 3, (2 - o % 3) * EX + f + 2 - o // 3, o)
        for f in range(BX)
        for o in range(9)
        if far_part((2 - o % 3) * EX + f + 2 - o // 3) == part
    ]
    for part in range(3)
]
MIDDLE, THIRD, END = 62, 61, 63
INNER = range(2, EX - 2)
OUTER = [0, 1, EX - 2, EX - 1]


def dot(a, b):
    return jnp.dot(a, b, preferred_element_type=F32)


def dot_nt(a, b):
    return lax.dot_general(a, b, NT, preferred_element_type=F32)


def pack_kernel(
    pos_ref, species_ref, codes_ref, count_ref, table_ref, ws1_ref, wv1_ref, ws2_ref, wv2_ref, ms_ref,
    mv_ref, m2_ref, readout_ref,
    first_ref, out_ref, last_ref, list_ref, square_ref,
    wide_ref,
):
    for i, ref in enumerate((ws1_ref, wv1_ref, ws2_ref, wv2_ref)):
        out_ref[BX + i // 2, K * (i % 2) : K * (i % 2) + K, :] = ref[...]
    out_ref[BX + 2] = jnp.broadcast_to(readout_ref[...], (8, C))
    for i, ref in enumerate((ms_ref, mv_ref, m2_ref)):
        square_ref[C * i : C * i + C, :] = ref[...]
    wide_ref[...] = jnp.zeros_like(wide_ref)
    wide_ref[0 : table_ref.shape[0], :] = table_ref[...].astype(F32)
    square_ref[3 * C : 4 * C, :] = wide_ref[...].astype(BF16)
    n = jnp.int32(0)
    block_id = lax.broadcasted_iota(jnp.int32, (8, 128), 0)
    mask = jnp.zeros((8, 128), jnp.int32)
    for p in range(codes_ref.shape[2]):
        code = codes_ref[0, 0, p]
        block = lax.shift_right_logical(code * 57, 9)
        offset = code - 9 * block
        bit = jnp.where(p < count_ref[0, 0], lax.shift_left(1, offset), 0)
        mask = mask + jnp.where(block_id == block, bit, 0)
        over = lax.shift_right_logical(offset * 11, 5)
        far = block + over - 1
        inside = (bit > 0) & (offset - 3 * over == 1) & (far >= 0) & (far < BX)
        list_ref[n] = block + (far + EX + 1) * 8 + jnp.where(offset == 4, 256, 0)
        n = n + jnp.where(inside, 1, 0)
    for i in range(3):
        list_ref[n + i] = E * 8
    list_ref[END] = n + (n & 1)
    mask = mask.astype(F32)
    for h in range(BX):
        places = [(out_ref, h)]
        if h == 0:
            places.append((first_ref, 0))
        if h == BX - 1:
            places.append((last_ref, 0))
        for ref, i in places:
            for d in range(3):
                ref[i, d : d + 1, :] = pos_ref[h, d]
            ref[i, 3:4, :] = species_ref[h].astype(F32)
            ref[i, 4:5, :] = mask[h : h + 1, :]
            ref[i, 5:8, :] = jnp.zeros((3, 128), F32)


def gather_ext(lo_ref, mid_ref, hi_ref, ext_ref):
    for row, ref in enumerate((lo_ref, mid_ref, hi_ref)):
        for x in range(EX):
            ext_ref[row * EX + x] = ref[x]
    ext_ref[E : E + 8] = jnp.full((8, 8, A), 1.0e4, F32)


def send_masks(ext_ref, maskv_ref, masks_ref, sem):
    for e in range(E):
        maskv_ref[e : e + 1, :] = ext_ref[e, 4:5, :].astype(jnp.int32)
    copy = pltpu.make_async_copy(maskv_ref, masks_ref, sem)
    copy.start()
    return copy


def make_list(parts, masks_ref, list_ref):
    n = jnp.int32(0)
    for pairs, place in zip(parts, (MIDDLE, THIRD, END)):
        held = None
        for own, other, lister, o in sorted(pairs, key=lambda pair: pair[2]):
            if lister != held:
                held, mask = lister, masks_ref[lister, 0]
            list_ref[n] = own + other * 8 + (256 if o == 4 else 0)
            n = n + (lax.shift_right_logical(mask, o) & 1)
        for i in range(3):
            list_ref[n + i] = E * 8
        n = n + (n & 1)
        list_ref[place] = n


def entry(list_ref, p):
    code = list_ref[p]
    own = code & 7
    other = lax.shift_right_logical(code, 3) & 31
    bias = jnp.where(code >= 256, 0, 1024)
    return own, other, bias


def turned_blocks(ext_ref):
    return [ext_ref[0:16].reshape(128, A).T, ext_ref[16:32].reshape(128, A).T]


def spread_lane(turned, e, d):
    lane = 8 * (e % 16) + d
    return jnp.broadcast_to(turned[e // 16][:, lane : lane + 1], (A, 128))


def geometry(col_ref, i, row, r, sign, bias, rows=ROWS):
    off = [sign * (row[d] - col_ref[i, d, pl.ds(r, rows), :]) for d in range(3)]
    squared = off[0] * off[0] + off[1] * off[1] + off[2] * off[2]
    soft = squared + 0.25
    inv = lax.rsqrt(soft)
    s = soft * inv
    taper = jnp.maximum(1.0 - squared * (1.0 / 36.0), 0.0)
    at = lax.broadcasted_iota(jnp.int32, (rows, 128), 0) + (r + bias)
    lane = lax.broadcasted_iota(jnp.int32, (rows, 128), 1)
    taper = jnp.where(at == lane, 0.0, taper)
    u = jnp.minimum(s, 6.25) * (1.0 / SIGMA) - 0.5
    base = taper * jnp.exp(-u * u)
    step = jnp.exp(2.0 * u - 1.0)
    q = [base]
    for k in range(1, K):
        q.append(q[-1] * (step * EXPS[k]))
    return off, inv, taper, u, q


EXPS = [1.0, 1.0, 0.1353352832366127, 0.01831563888873418]


def store_tiles(put, off, inv, taper, q):
    direction = [o * inv for o in off]
    for k in range(K):
        radial = taper * q[k]
        put(0, k, radial.astype(BF16))
        for d in range(3):
            put(1 + d, k, (radial * direction[d]).astype(BF16))


def pull_back(grads, off, inv, taper, u, q):
    direction = [o * inv for o in off]
    s0 = s1 = None
    dg = [None] * 3
    for k in reversed(range(K)):
        tilted = [grads(1 + d, k) for d in range(3)]
        along = tilted[0] * direction[0] + tilted[1] * direction[1] + tilted[2] * direction[2]
        p = (grads(0, k) + along) * q[k]
        s0 = p if s0 is None else s0 + p
        if k:
            s1 = s0 if s1 is None else s1 + s0
        for d in range(3):
            v = tilted[d] * q[k]
            dg[d] = v if dg[d] is None else dg[d] + v
    turn = dg[0] * direction[0] + dg[1] * direction[1] + dg[2] * direction[2]
    bend = (2.0 / SIGMA) * (u * s0 - s1) + turn * inv
    pull = taper * inv
    weight = s0 * (1.0 / 9.0) + pull * bend
    return [dg[d] * pull - weight * off[d] for d in range(3)]


def rows_of(ext_ref, e):
    return [ext_ref[e, d : d + 1, :] for d in range(3)]


def scaled(feature, weights_ref, k):
    return (feature.astype(F32) * weights_ref[k : k + 1, :]).astype(BF16)


def first_sums(
    end, list_ref, col_ref, near, rows, where, scaled_s_ref, scaled_v_ref, acc_ref, tile_a_ref,
    tile_b_ref,
):
    def first_tiles(p, tile_ref, r):
        own, other, bias = entry(list_ref, p)
        row = rows(where(other))
        off, inv, taper, u, q = geometry(col_ref, own + near, row, r, 1.0, bias)

        def put(g, k, tile):
            tile_ref[pl.ds(g * A + r, ROWS), pl.ds(k * A, A)] = tile

        store_tiles(put, off, inv, taper, q)

    def first_sum(p, tile_ref, g):
        own, other, _ = entry(list_ref, p)
        part = pl.ds(g * A, A)
        acc_ref[own, part, :] += dot(tile_ref[part, :], (scaled_v_ref if g else scaled_s_ref)[where(other)])

    def first_half(p, this_ref, next_ref):
        for g in range(4):
            first_sum(p, this_ref, g)
            for r in range(g * 32, g * 32 + 32, ROWS):
                first_tiles(p + 1, next_ref, r)

    def first(i, carry):
        first_half(2 * i, tile_a_ref, tile_b_ref)
        first_half(2 * i + 1, tile_b_ref, tile_a_ref)
        return carry

    for r in range(0, A, ROWS):
        first_tiles(0, tile_a_ref, r)
    lax.fori_loop(0, half(end), first, 0)


def own_kernel(
    own_ref, list_ref, square_ref,
    acc_ref,
    ext_ref, col_ref, scaled_s_ref, scaled_v_ref, tile_a_ref, tile_b_ref,
):
    ws1_ref, wv1_ref, _, _, _ = radial_parts(own_ref)
    table = square_parts(square_ref)[3][...]
    for h in range(BX):
        ext_ref[h] = own_ref[h]
    ext_ref[BX] = jnp.full((8, A), 1.0e4, F32)
    for h in range(BX + 1, 16):
        ext_ref[h] = jnp.zeros((8, A), F32)
    turned = [ext_ref[0:16].reshape(128, A).T]
    lanes = lax.broadcasted_iota(jnp.int32, (A, 128), 1).astype(F32)
    acc_ref[...] = jnp.zeros_like(acc_ref)
    for h in range(BX):
        for d in range(3):
            col_ref[h, d] = spread_lane(turned, h, d)
        hot = (spread_lane(turned, h, 3) == lanes).astype(BF16)
        initial = dot(hot, table).astype(BF16)
        for k in range(K):
            scaled_s_ref[h, pl.ds(k * A, A), :] = scaled(initial, ws1_ref, k)
            scaled_v_ref[h, pl.ds(k * A, A), :] = scaled(initial, wv1_ref, k)
    scaled_s_ref[BX] = jnp.zeros((K * A, C), BF16)
    scaled_v_ref[BX] = jnp.zeros((K * A, C), BF16)
    first_sums(
        list_ref[END], list_ref, col_ref, 0, lambda e: rows_of(ext_ref, e),
        lambda e: jnp.minimum(e - EX - 1, BX), scaled_s_ref, scaled_v_ref, acc_ref, tile_a_ref,
        tile_b_ref,
    )


def forward_kernel(
    lo_ref, mid_ref, hi_ref, acc_own_ref, radial_ref, square_ref,
    pre_ref, feat_ref, out_lo_ref, out_hi_ref, scaled_s_ref, scaled_v_ref, ready_ref, keep_col_ref,
    list1_ref, list2_ref,
    ext_ref, col_ref, init_ref, acc_ref, tile_a_ref, tile_b_ref, wide_a_ref, wide_b_ref, total_ref,
    maskv_ref, masks_ref, sem,
):
    ws1_ref, wv1_ref, ws2_ref, wv2_ref, _ = radial_parts(radial_ref)
    ms_ref, mv_ref, _, table_ref = square_parts(square_ref)
    gather_ext(lo_ref, mid_ref, hi_ref, ext_ref)
    copy = send_masks(ext_ref, maskv_ref, masks_ref, sem)
    turned = turned_blocks(ext_ref)
    lanes = lax.broadcasted_iota(jnp.int32, (A, 128), 1).astype(F32)
    for e in range(E):
        if e == 8:
            copy.wait()
            make_list(HOME_PAIRS, masks_ref, list1_ref)
            make_list(FAR_PAIRS, masks_ref, list2_ref)
        for d in range(3):
            column = spread_lane(turned, e, d)
            col_ref[e, d] = column
            if EX <= e < 2 * EX:
                keep_col_ref[e - EX, d] = column
        hot = (spread_lane(turned, e, 3) == lanes).astype(BF16)
        init_ref[e] = dot(hot, table_ref[...]).astype(BF16)
    col_ref[E] = jnp.full((3, A, 128), 1.0e4, F32)
    keep_col_ref[EX] = jnp.full((3, A, 128), 1.0e4, F32)

    def scale_block(e, carry):
        for k in range(K):
            scaled_s_ref[e, pl.ds(k * A, A), :] = scaled(init_ref[e], ws1_ref, k)
            scaled_v_ref[e, pl.ds(k * A, A), :] = scaled(init_ref[e], wv1_ref, k)
        return carry

    lax.fori_loop(0, E, scale_block, 0)
    scaled_s_ref[E] = jnp.zeros((K * A, C), BF16)
    scaled_v_ref[E] = jnp.zeros((K * A, C), BF16)
    acc_ref[...] = acc_own_ref[...]
    total_ref[...] = jnp.zeros_like(total_ref)
    first_sums(
        list1_ref[THIRD], list1_ref, col_ref, EX + 1, lambda e: rows_of(ext_ref, e), lambda e: e,
        scaled_s_ref, scaled_v_ref, acc_ref, tile_a_ref, tile_b_ref,
    )
    for h in range(BX):
        pre = dot((acc_ref[h, 0:A, :] * 0.125).astype(BF16), ms_ref[...])
        pre_ref[h] = pre
        scalar = (init_ref[h + EX + 1].astype(F32) + pre * jax.nn.sigmoid(pre)).astype(BF16)
        vector = dot((acc_ref[h, A : 4 * A, :] * 0.125).astype(BF16), mv_ref[...]).astype(BF16)
        feat_ref[h, 0:A, :] = scalar
        feat_ref[h, A : 4 * A, :] = vector
        for k in range(K):
            ready_ref[h, pl.ds(k * A, A), :] = scaled(scalar, ws2_ref, k)
            for d in range(3):
                ready_ref[h, pl.ds(((1 + d) * K + k) * A, A), :] = scaled(
                    vector[d * A : (d + 1) * A, :], wv2_ref, k
                )
    second_sums(
        0, list2_ref[MIDDLE], list2_ref, col_ref, 0, lambda own: rows_of(ext_ref, own + EX + 1),
        ready_ref, total_ref, wide_a_ref, wide_b_ref,
    )
    for x in range(EX):
        out_lo_ref[x] = total_ref[x].astype(BF16)
        out_hi_ref[x] = total_ref[2 * EX + x].astype(BF16)


def place(other, shift):
    return jnp.minimum(other - shift, EX) if shift else other


def second_sums(
    start, end, list_ref, col_ref, shift, rows, ready_ref, total_ref, wide_a_ref, wide_b_ref
):
    def second_tiles(p, wide_ref, r):
        own, other, bias = entry(list_ref, p)
        row = rows(own)
        off, inv, taper, u, q = geometry(col_ref, place(other, shift), row, r, 1.0, bias)

        def put(g, k, tile):
            wide_ref[pl.ds(r, ROWS), pl.ds((g * K + k) * A, A)] = tile

        store_tiles(put, off, inv, taper, q)

    def second_half(p, this_ref, next_ref):
        own, other, _ = entry(list_ref, p)
        for g in range(4):
            part = pl.ds(g * K * A, K * A)
            total_ref[place(other, shift)] += dot(this_ref[:, part], ready_ref[own, part, :])
            for r in range(g * 32, g * 32 + 32, ROWS):
                second_tiles(p + 1, next_ref, r)

    def second(i, carry):
        second_half(2 * i, wide_a_ref, wide_b_ref)
        second_half(2 * i + 1, wide_b_ref, wide_a_ref)
        return carry

    for r in range(0, A, ROWS):
        second_tiles(start, wide_a_ref, r)
    lax.fori_loop(half(start), half(end), second, 0)


def forward_inner_kernel(
    mid_ref, list2_ref, ready_ref, col_ref, out_ref, wide_a_ref, wide_b_ref, total_ref
):
    total_ref[...] = jnp.zeros_like(total_ref)
    second_sums(
        list2_ref[MIDDLE], list2_ref[END], list2_ref, col_ref, EX,
        lambda own: rows_of(mid_ref, own + 1), ready_ref, total_ref, wide_a_ref, wide_b_ref,
    )
    out_ref[...] = total_ref[0:EX]


def radial_parts(ref):
    return [ref.at[BX + i // 2, pl.ds(K * (i % 2), K if i < 4 else 1), :] for i in range(5)]


def square_parts(ref):
    return [ref.at[pl.ds(C * i, C), :] for i in range(4)]


def half(n):
    return lax.shift_right_logical(n, 1)


def slope_of(value):
    sigma = jax.nn.sigmoid(value)
    return sigma * (1.0 + value * (1.0 - sigma))


def middle(msg, x, feat_ref, radial_ref, square_ref, energy_ref):
    readout = radial_parts(radial_ref)[4][...]
    mix_ref = square_parts(square_ref)[2]
    pre = dot((msg * 0.125).astype(BF16), mix_ref[...])
    sigma = jax.nn.sigmoid(pre)
    if 1 <= x <= BX:
        part = (feat_ref[x - 1, 0:A, :].astype(F32) + pre * sigma) * readout
        energy_ref[x - 1] = jnp.sum(part.T, axis=0, keepdims=True)
    grad = (readout * (sigma * (1.0 + pre * (1.0 - sigma)))).astype(BF16)
    return dot_nt(grad, mix_ref[...]) * 0.125


def message(mid_ref, below_ref, above_ref, x):
    return mid_ref[x] + below_ref[x].astype(F32) + above_ref[x].astype(F32)


def middle_inner_kernel(
    mid_ref, below_ref, above_ref, ext_mid_ref, list2_ref, feat_ref, col_ref, radial_ref, square_ref,
    energy_ref, second_in_ref, acc_ref, across_ref, down_ref,
    ext_ref, second_ref, cot_s_ref, cot_v_ref, tile_a_ref, tile_b_ref, grad_a_ref, grad_b_ref,
):
    _, _, ws2_ref, wv2_ref, _ = radial_parts(radial_ref)
    for x in range(EX):
        ext_ref[x] = ext_mid_ref[x]
    ext_ref[EX] = jnp.full((8, A), 1.0e4, F32)
    for x in INNER:
        second = middle(
            message(mid_ref, below_ref, above_ref, x), x, feat_ref, radial_ref, square_ref, energy_ref
        )
        second_ref[x] = second
        second_in_ref[x] = second.astype(BF16)
    acc_ref[...] = jnp.zeros_like(acc_ref)
    down_ref[...] = jnp.zeros_like(down_ref)
    across_ref[...] = jnp.zeros_like(across_ref)
    cotangents(second_ref, cot_s_ref, cot_v_ref, 0, ws2_ref, wv2_ref, INNER)
    second_moves(
        list2_ref[MIDDLE], list2_ref[THIRD], list2_ref, col_ref, EX, lambda e: rows_of(ext_ref, e),
        feat_ref, cot_s_ref, cot_v_ref, acc_ref, across_ref, down_ref, tile_a_ref, tile_b_ref,
        grad_a_ref, grad_b_ref,
    )


def middle_kernel(
    mid_ref, below_ref, above_ref, left_ref, right_ref, feat_ref, radial_ref, square_ref,
    energy_part_ref, second_part_ref,
    energy_ref, second_in_ref, second_own_ref,
):
    for x in OUTER:
        msg = message(mid_ref, below_ref, above_ref, x)
        if x < 2:
            msg = msg + left_ref[x].astype(F32)
        else:
            msg = msg + right_ref[x - EX + 2].astype(F32)
        second = middle(msg, x, feat_ref, radial_ref, square_ref, energy_ref)
        second_own_ref[x] = second
        second_in_ref[x] = second.astype(BF16)
    for x in INNER:
        energy_ref[x - 1] = energy_part_ref[x - 1]
        second_in_ref[x] = second_part_ref[x]
        second_own_ref[x] = jnp.zeros((A, C), F32)


def move(across_ref, own, r, near, own_sign, grad_ref):
    def grads(g, k):
        return grad_ref[pl.ds(g * A + r, ROWS), pl.ds(k * A, A)]

    parts = []
    for d, moved in enumerate(pull_back(grads, *near)):
        if own_sign > 0:
            across_ref[own, d, pl.ds(r, ROWS), :] += moved
        else:
            across_ref[own, d, pl.ds(r, ROWS), :] -= moved
        part = moved[0:8]
        for i in range(8, ROWS, 8):
            part = part + moved[i : i + 8]
        parts.append(part)
    return parts


def add_down(down_ref, other, own_sign, sums):
    for d in range(3):
        down_ref[other, d] -= own_sign * sums[d]


def plus(sums, parts):
    return parts if sums is None else [a + b for a, b in zip(sums, parts)]


def first_moves(
    start, end, list_ref, col_ref, shift, rows, inward_ref, scaled_s_ref, scaled_v_ref, across_ref,
    down_ref, grad_a_ref, grad_b_ref,
):
    def first_grads(p, grad_ref):
        own, other, _ = entry(list_ref, p)
        grad_ref[0:A, :] = dot_nt(inward_ref[own, 0:A, :], scaled_s_ref[other])
        grad_ref[A : 4 * A, :] = dot_nt(inward_ref[own, A : 4 * A, :], scaled_v_ref[other])

    def first_move(p, grad_ref):
        own, other, bias = entry(list_ref, p)
        row = rows(place(other, shift))
        sums = None
        for r in range(0, A, ROWS):
            near = geometry(col_ref, own + 1, row, r, 1.0, bias)
            sums = plus(sums, move(across_ref, own, r, near, -1.0, grad_ref))
        add_down(down_ref, place(other, shift), -1.0, sums)

    def first_back(i, carry):
        p = 2 * i
        first_grads(p + 1, grad_b_ref)
        first_move(p, grad_a_ref)
        first_grads(p + 2, grad_a_ref)
        first_move(p + 1, grad_b_ref)
        return carry

    first_grads(start, grad_a_ref)
    lax.fori_loop(half(start), half(end), first_back, 0)


def line_of(down_ref, across_ref, e, x, d):
    line = jnp.sum(down_ref[e, d], axis=0, keepdims=True)
    if x is not None and 1 <= x <= BX:
        line = line + jnp.sum(across_ref[x - 1, d].T, axis=0, keepdims=True)
    return line


def second_moves(
    start, end, list_ref, col_ref, shift, rows, feat_ref, cot_s_ref, cot_v_ref, acc_ref, across_ref,
    down_ref, tile_a_ref, tile_b_ref, grad_a_ref, grad_b_ref,
):
    def second_grads(p, grad_ref):
        own, other, _ = entry(list_ref, p)
        source = place(other, shift)
        grad_ref[0:A, :] = dot_nt(feat_ref[own, 0:A, :], cot_s_ref[source])
        grad_ref[A : 4 * A, :] = dot_nt(feat_ref[own, A : 4 * A, :], cot_v_ref[source])

    def second_move(p, grad_ref, tile_ref):
        own, other, bias = entry(list_ref, p)
        source = place(other, shift)
        row = rows(source)
        sums = None
        for r in range(0, A, ROWS):
            near = geometry(col_ref, own + 1, row, r, -1.0, bias)
            off, inv, taper, u, q = near

            def put(g, k, tile):
                tile_ref[pl.ds(g * A + r, ROWS), pl.ds(k * A, A)] = tile

            store_tiles(put, off, inv, taper, q)
            sums = plus(sums, move(across_ref, own, r, near, 1.0, grad_ref))
        add_down(down_ref, source, 1.0, sums)

    def second_sum(own, source, tile_ref):
        acc_ref[own, 0:A, :] += dot(tile_ref[0:A, :], cot_s_ref[source])
        acc_ref[own, A : 4 * A, :] += dot(tile_ref[A : 4 * A, :], cot_v_ref[source])

    def second_back(i, carry):
        p = 2 * i
        own, other, _ = entry(list_ref, p)
        second_sum(*carry, tile_b_ref)
        second_grads(p + 1, grad_b_ref)
        second_move(p, grad_a_ref, tile_a_ref)
        second_sum(own, place(other, shift), tile_a_ref)
        second_grads(p + 2, grad_a_ref)
        second_move(p + 1, grad_b_ref, tile_b_ref)
        own, other, _ = entry(list_ref, p + 1)
        return own, place(other, shift)

    empty = EX if shift else E
    for ref in (cot_s_ref, cot_v_ref):
        ref[empty] = jnp.zeros((K * A, C), BF16)
    tile_b_ref[...] = jnp.zeros_like(tile_b_ref)
    second_grads(start, grad_a_ref)
    last = lax.fori_loop(half(start), half(end), second_back, (jnp.int32(0), jnp.int32(empty)))
    second_sum(*last, tile_b_ref)


def cotangents(ref, cot_s_ref, cot_v_ref, first, ws2_ref, wv2_ref, blocks=range(EX)):
    for x in blocks:
        for k in range(K):
            cot_s_ref[first + x, pl.ds(k * A, A), :] = scaled(ref[x], ws2_ref, k)
            cot_v_ref[first + x, pl.ds(k * A, A), :] = scaled(ref[x], wv2_ref, k)


def backward_outer_two_kernel(
    mid_ref, list2_ref, in_mid_ref, feat_ref, col_ref, radial_ref, acc_in_ref, across_in_ref,
    down_in_ref,
    acc_ref, across_ref, down_ref,
    ext_ref, cot_s_ref, cot_v_ref, tile_a_ref, tile_b_ref, grad_a_ref, grad_b_ref,
):
    _, _, ws2_ref, wv2_ref, _ = radial_parts(radial_ref)
    for x in range(EX):
        ext_ref[x] = mid_ref[x]
    ext_ref[EX] = jnp.full((8, A), 1.0e4, F32)
    acc_ref[...] = acc_in_ref[...]
    down_ref[...] = down_in_ref[...]
    across_ref[...] = across_in_ref[...]
    cotangents(in_mid_ref, cot_s_ref, cot_v_ref, 0, ws2_ref, wv2_ref, OUTER)
    second_moves(
        list2_ref[THIRD], list2_ref[END], list2_ref, col_ref, EX, lambda e: rows_of(ext_ref, e),
        feat_ref, cot_s_ref, cot_v_ref, acc_ref, across_ref, down_ref, tile_a_ref, tile_b_ref,
        grad_a_ref, grad_b_ref,
    )


def backward_kernel(
    lo_ref, mid_ref, hi_ref, list1_ref, list2_ref, acc_in_ref, across_in_ref, down_in_ref, feat_ref,
    pre_ref, in_lo_ref, in_hi_ref, scaled_s_ref, scaled_v_ref, col_ref, radial_ref, square_ref,
    out_left_ref, out_right_ref, inward_ref, down_ref, across_ref,
    ext_ref, cot_s_ref, cot_v_ref, acc_ref, tile_a_ref, tile_b_ref, grad_a_ref, grad_b_ref,
):
    _, _, ws2_ref, wv2_ref, readout_ref = radial_parts(radial_ref)
    ms_ref, mv_ref, _, _ = square_parts(square_ref)
    gather_ext(lo_ref, mid_ref, hi_ref, ext_ref)
    acc_ref[...] = acc_in_ref[...]
    across_ref[...] = across_in_ref[...]
    down_ref[0:EX] = jnp.zeros((EX, 3, 8, A), F32)
    down_ref[EX : 2 * EX] = down_in_ref[0:EX]
    down_ref[2 * EX : E + 1] = jnp.zeros((EX + 1, 3, 8, A), F32)
    cotangents(in_lo_ref, cot_s_ref, cot_v_ref, 0, ws2_ref, wv2_ref)
    cotangents(in_hi_ref, cot_s_ref, cot_v_ref, 2 * EX, ws2_ref, wv2_ref)
    second_moves(
        0, list2_ref[MIDDLE], list2_ref, col_ref, 0, lambda e: rows_of(ext_ref, e), feat_ref,
        cot_s_ref, cot_v_ref, acc_ref, across_ref, down_ref, tile_a_ref, tile_b_ref, grad_a_ref,
        grad_b_ref,
    )
    for h in range(BX):
        slope = (readout_ref[...] + acc_ref[h, 0:A, :]) * slope_of(pre_ref[h])
        inward_ref[h, 0:A, :] = (dot_nt(slope.astype(BF16), ms_ref[...]) * 0.125).astype(BF16)
        inward_ref[h, A : 4 * A, :] = (
            dot_nt(acc_ref[h, A : 4 * A, :].astype(BF16), mv_ref[...]) * 0.125
        ).astype(BF16)
    first_moves(
        0, list1_ref[MIDDLE], list1_ref, col_ref, 0, lambda e: rows_of(ext_ref, e), inward_ref,
        scaled_s_ref, scaled_v_ref, across_ref, down_ref, grad_a_ref, grad_b_ref,
    )
    for row in range(3):
        for d in range(3):
            out_left_ref[row, d : d + 1, :] = line_of(down_ref, None, row * EX, None, d)
            out_right_ref[row, d : d + 1, :] = line_of(down_ref, None, row * EX + EX - 1, None, d)


def backward_rows_kernel(
    lo_ref, mid_ref, hi_ref, list1_ref, scaled_s_ref, scaled_v_ref, col_ref, inward_ref, down_in_ref,
    across_in_ref,
    out_lo_ref, out_mid_ref, out_hi_ref,
    ext_ref, grad_a_ref, grad_b_ref, down_ref, across_ref,
):
    gather_ext(lo_ref, mid_ref, hi_ref, ext_ref)
    down_ref[...] = down_in_ref[...]
    across_ref[...] = across_in_ref[...]
    first_moves(
        list1_ref[MIDDLE], list1_ref[THIRD], list1_ref, col_ref, 0, lambda e: rows_of(ext_ref, e),
        inward_ref, scaled_s_ref, scaled_v_ref, across_ref, down_ref, grad_a_ref, grad_b_ref,
    )
    for row, ref in enumerate((out_lo_ref, out_mid_ref, out_hi_ref)):
        for h in range(BX):
            for d in range(3):
                line = line_of(down_ref, across_ref, row * EX + h + 1, h + 1 if row == 1 else None, d)
                ref[h, d : d + 1, :] = line


def backward_inner_kernel(
    mid_ref, list1_ref, scaled_s_ref, scaled_v_ref, col_ref, inward_ref, out_ref,
    ext_ref, grad_a_ref, grad_b_ref, down_ref, across_ref,
):
    for x in range(EX):
        ext_ref[x] = mid_ref[x]
    ext_ref[EX] = jnp.full((8, A), 1.0e4, F32)
    down_ref[...] = jnp.zeros_like(down_ref)
    across_ref[...] = jnp.zeros_like(across_ref)
    first_moves(
        list1_ref[THIRD], list1_ref[END], list1_ref, col_ref, EX, lambda e: rows_of(ext_ref, e),
        inward_ref, scaled_s_ref, scaled_v_ref, across_ref, down_ref, grad_a_ref, grad_b_ref,
    )
    for x in range(EX):
        for d in range(3):
            out_ref[x, d : d + 1, :] = line_of(down_ref, across_ref, x, x, d)


VMEM = pl.BlockSpec(memory_space=pltpu.VMEM)
SMEM = pl.BlockSpec(memory_space=pltpu.SMEM)
PARAMS = pltpu.CompilerParams(vmem_limit_bytes=24 * 1024 * 1024)


SEM = pltpu.SemaphoreType.DMA


def forward_call(*args):
    return call(
        forward_kernel,
        args,
        [
            ((BX, A, C), F32),
            ((BX, 4 * A, C), BF16),
            ((EX, A, C), BF16),
            ((EX, A, C), BF16),
            ((E + 1, K * A, C), BF16),
            ((E + 1, K * A, C), BF16),
            ((BX, 4 * K * A, C), BF16),
            ((EX + 1, 3, A, 128), F32),
            ((64,), jnp.int32),
            ((64,), jnp.int32),
        ],
        [
            pltpu.VMEM((E + 8, 8, A), F32),
            pltpu.VMEM((E + 1, 3, A, 128), F32),
            pltpu.VMEM((E, A, C), BF16),
            pltpu.VMEM((BX, 4 * A, C), F32),
            pltpu.VMEM((4 * A, K * A), BF16),
            pltpu.VMEM((4 * A, K * A), BF16),
            pltpu.VMEM((A, 4 * K * A), BF16),
            pltpu.VMEM((A, 4 * K * A), BF16),
            pltpu.VMEM((E + 1, A, C), F32),
            pltpu.VMEM((E, 128), jnp.int32),
            pltpu.SMEM((E, 128), jnp.int32),
            SEM,
        ],
        out_specs=[VMEM] * 8 + [SMEM] * 2,
    )


def forward_inner_call(*args):
    return call(
        forward_inner_kernel,
        args,
        [((EX, A, C), F32)],
        [
            pltpu.VMEM((A, 4 * K * A), BF16),
            pltpu.VMEM((A, 4 * K * A), BF16),
            pltpu.VMEM((EX + 1, A, C), F32),
        ],
        in_specs=[VMEM, SMEM, VMEM, VMEM],
        cost=pl.CostEstimate(flops=4 * 10**9, bytes_accessed=10**6, transcendentals=0),
    )


LONG = pl.CostEstimate(flops=4 * 10**9, bytes_accessed=10**6, transcendentals=0)
HELD = [((BX, 4 * A, C), F32), ((BX, 3, A, 128), F32), ((EX + 1, 3, 8, A), F32)]
ROW_SCRATCH = [
    pltpu.VMEM((EX + 1, K * A, C), BF16),
    pltpu.VMEM((EX + 1, K * A, C), BF16),
    pltpu.VMEM((4 * A, K * A), BF16),
    pltpu.VMEM((4 * A, K * A), BF16),
    pltpu.VMEM((4 * A, K * A), F32),
    pltpu.VMEM((4 * A, K * A), F32),
]


def own_call(*args):
    return call(
        own_kernel,
        args,
        [((BX, 4 * A, C), F32)],
        [
            pltpu.VMEM((16, 8, A), F32),
            pltpu.VMEM((BX, 3, A, 128), F32),
            pltpu.VMEM((BX + 1, K * A, C), BF16),
            pltpu.VMEM((BX + 1, K * A, C), BF16),
            pltpu.VMEM((4 * A, K * A), BF16),
            pltpu.VMEM((4 * A, K * A), BF16),
        ],
        in_specs=[VMEM, SMEM, VMEM],
        cost=LONG,
    )


def middle_inner_call(*args):
    return call(
        middle_inner_kernel,
        args,
        [((BX, 1, A), F32), ((EX, A, C), BF16), *HELD],
        [pltpu.VMEM((EX + 1, 8, A), F32), pltpu.VMEM((EX, A, C), F32), *ROW_SCRATCH],
        in_specs=[VMEM] * 4 + [SMEM] + [VMEM] * 4,
        cost=LONG,
    )


def backward_outer_two_call(*args):
    return call(
        backward_outer_two_kernel,
        args,
        HELD,
        [pltpu.VMEM((EX + 1, 8, A), F32), *ROW_SCRATCH],
        in_specs=[VMEM, SMEM] + [VMEM] * 7,
        cost=LONG,
    )


def backward_call(*args):
    return call(
        backward_kernel,
        args,
        [
            ((3, 3, A), F32),
            ((3, 3, A), F32),
            ((BX, 4 * A, C), BF16),
            ((E + 1, 3, 8, A), F32),
            ((BX, 3, A, 128), F32),
        ],
        [
            pltpu.VMEM((E + 8, 8, A), F32),
            pltpu.VMEM((E + 1, K * A, C), BF16),
            pltpu.VMEM((E + 1, K * A, C), BF16),
            pltpu.VMEM((BX, 4 * A, C), F32),
            pltpu.VMEM((4 * A, K * A), BF16),
            pltpu.VMEM((4 * A, K * A), BF16),
            pltpu.VMEM((4 * A, K * A), F32),
            pltpu.VMEM((4 * A, K * A), F32),
        ],
        in_specs=[VMEM] * 3 + [SMEM] * 2 + [VMEM] * 12,
    )


def backward_rows_call(*args):
    return call(
        backward_rows_kernel,
        args,
        [((BX, 3, A), F32)] * 3,
        [
            pltpu.VMEM((E + 8, 8, A), F32),
            pltpu.VMEM((4 * A, K * A), F32),
            pltpu.VMEM((4 * A, K * A), F32),
            pltpu.VMEM((E + 1, 3, 8, A), F32),
            pltpu.VMEM((BX, 3, A, 128), F32),
        ],
        in_specs=[VMEM] * 3 + [SMEM] + [VMEM] * 6,
        cost=LONG,
    )


def backward_inner_call(*args):
    return call(
        backward_inner_kernel,
        args,
        [((EX, 3, A), F32)],
        [
            pltpu.VMEM((EX + 1, 8, A), F32),
            pltpu.VMEM((4 * A, K * A), F32),
            pltpu.VMEM((4 * A, K * A), F32),
            pltpu.VMEM((EX + 1, 3, 8, A), F32),
            pltpu.VMEM((BX, 3, A, 128), F32),
        ],
        in_specs=[VMEM, SMEM, VMEM, VMEM, VMEM, VMEM],
        cost=pl.CostEstimate(flops=4 * 10**9, bytes_accessed=10**6, transcendentals=0),
    )


def call(kernel, args, outs, scratch=(), in_specs=None, out_specs=None, cost=None, params=PARAMS):
    return pl.pallas_call(
        kernel,
        out_shape=[jax.ShapeDtypeStruct(s, d) for s, d in outs],
        in_specs=in_specs or [VMEM] * len(args),
        out_specs=out_specs or [VMEM] * len(outs),
        scratch_shapes=list(scratch),
        compiler_params=params,
        cost_estimate=cost,
    )(*args)


def along(block, axis, step):
    size = lax.axis_size(axis)
    return lax.ppermute(block, axis, [(i, i + step) for i in range(size) if 0 <= i + step < size])


def both(lo, hi, axis, step=1):
    return along(lo, axis, step), along(hi, axis, -step)


def local(
    positions, species, pair_codes, pair_count, embed_table, ws1, wv1, ws2, wv2, ms, mv, m2, readout
):
    first, radial, last, own_list, square = call(
        pack_kernel,
        (
            positions.transpose(0, 2, 1, 3), species, pair_codes, pair_count, embed_table, ws1, wv1,
            ws2, wv2, ms, mv, m2, readout.reshape(1, C),
        ),
        [
            ((1, 8, A), F32),
            ((BX + 3, 8, A), F32),
            ((1, 8, A), F32),
            ((64,), jnp.int32),
            ((4 * C, C), BF16),
        ],
        [pltpu.VMEM((C, C), F32)],
        in_specs=[VMEM] * 2 + [SMEM] * 2 + [VMEM] * 9,
        out_specs=[VMEM] * 3 + [SMEM, VMEM],
        params=pltpu.CompilerParams(vmem_limit_bytes=60 * 1024 * 1024),
    )
    left, right = both(last, first, "gx")
    (acc,) = own_call(radial, own_list, square)
    radial, acc = lax.optimization_barrier((radial, acc))
    ext_mid = jnp.concatenate([left, radial[:BX], right], axis=0)
    ext_lo, ext_hi = both(ext_mid, ext_mid, "gy")
    ext = (ext_lo, ext_mid, ext_hi)
    pre, feat, lo, hi, scaled_s, scaled_v, ready, col, list1, list2 = forward_call(
        *ext, acc, radial, square
    )
    below, above = both(hi, lo, "gy")
    (mid,) = forward_inner_call(ext_mid, list2, ready, col)
    edge = lambda x: (mid[x : x + 2] + below[x : x + 2] + above[x : x + 2]).astype(BF16)
    left, right = both(edge(EX - 2), edge(0), "gx")
    energy, inner, *held = middle_inner_call(
        mid, below, above, ext_mid, list2, feat, col, radial, square
    )
    energy, inner, inner_own = call(
        middle_kernel,
        (mid, below, above, left, right, feat, radial, square, energy, inner),
        [((BX, 1, A), F32), ((EX, A, C), BF16), ((EX, A, C), F32)],
    )
    in_lo, in_hi = both(inner, inner, "gy")
    held = backward_outer_two_call(ext_mid, list2, inner_own, feat, col, radial, *held)
    left, right, inward, down, across = backward_call(
        *ext, list1, list2, *held, feat, pre, in_lo, in_hi, scaled_s, scaled_v, col, radial, square
    )
    left, right = both(right, left, "gx")
    lo, mid, hi = backward_rows_call(
        *ext, list1, scaled_s, scaled_v, col, inward, down, across
    )
    pad = lambda row: jnp.concatenate(
        [left[row : row + 1], jnp.zeros((BX - 2, 3, A), F32), right[row : row + 1]], axis=0
    )
    lo, hi = lo + pad(0), hi + pad(2)
    below, above = both(hi, lo, "gy")
    (more,) = backward_inner_call(ext_mid, list1, scaled_s, scaled_v, col, inward)
    total = mid + pad(1) + below + above + more[1 : BX + 1]
    return energy, -total.reshape(BX, 1, 3, A)


def solution(mesh):
    in_specs = (
        P("gx", "gy", None, None),
        P("gx", "gy", None),
        P("gx", "gy", None),
        P("gx", "gy"),
        *[P()] * 9,
    )
    out_specs = (P("gx", "gy", None), P("gx", "gy", None, None))
    return jax.shard_map(local, mesh=mesh, in_specs=in_specs, out_specs=out_specs, check_vma=False)
```

```python
import jax
import jax.numpy as jnp
from jax import lax
from jax.experimental import pallas as pl
from jax.experimental.pallas import tpu as pltpu
from jax.sharding import PartitionSpec as P

BX = 6
EX = 8
A = 128
C = 128
K = 4
ROWS = 16
F32 = jnp.float32
BF16 = jnp.bfloat16
SIGMA = 1.5
NT = (((1,), (1,)), ((), ()))
E = 3 * EX

def home_part(e):
    return 0 if e % EX in (0, EX - 1) else 1 if e // EX != 1 else 2


HOME_PAIRS = [
    [
        (h, (o % 3) * EX + h + o // 3, EX + 1 + h, o)
        for h in range(BX)
        for o in range(9)
        if home_part((o % 3) * EX + h + o // 3) == part
    ]
    for part in range(3)
]


EARLY = range(2, EX - 3)
LATE = [0, 1, EX - 3, EX - 2, EX - 1]


def far_part(e):
    return 0 if e // EX != 1 else 1 if e % EX in EARLY else 2


FAR_PAIRS = [
    [
        (f, (2 - o % 3) * EX + f + 2 - o // 3, (2 - o % 3) * EX + f + 2 - o // 3, o)
        for f in range(BX)
        for o in range(9)
        if far_part((2 - o % 3) * EX + f + 2 - o // 3) == part
    ]
    for part in range(3)
]
MIDDLE, THIRD, END = 62, 61, 63
INNER = range(2, EX - 2)
OUTER = [0, 1, EX - 2, EX - 1]


def dot(a, b):
    return jnp.dot(a, b, preferred_element_type=F32)


def dot_nt(a, b):
    return lax.dot_general(a, b, NT, preferred_element_type=F32)


def pack_kernel(
    pos_ref, species_ref, codes_ref, count_ref, table_ref, ws1_ref, wv1_ref, ws2_ref, wv2_ref, ms_ref,
    mv_ref, m2_ref, readout_ref,
    first_ref, out_ref, last_ref, list_ref, square_ref,
    wide_ref,
):
    for i, ref in enumerate((ws1_ref, wv1_ref, ws2_ref, wv2_ref)):
        out_ref[BX + i // 2, K * (i % 2) : K * (i % 2) + K, :] = ref[...]
    out_ref[BX + 2] = jnp.broadcast_to(readout_ref[...], (8, C))
    for i, ref in enumerate((ms_ref, mv_ref, m2_ref)):
        square_ref[C * i : C * i + C, :] = ref[...]
    wide_ref[...] = jnp.zeros_like(wide_ref)
    wide_ref[0 : table_ref.shape[0], :] = table_ref[...].astype(F32)
    out_ref[BX + 3 : BX + 3 + C // 8] = wide_ref[...].reshape(C // 8, 8, C)
    n = jnp.int32(0)
    block_id = lax.broadcasted_iota(jnp.int32, (8, 128), 0)
    mask = jnp.zeros((8, 128), jnp.int32)
    for p in range(codes_ref.shape[2]):
        code = codes_ref[0, 0, p]
        block = lax.shift_right_logical(code * 57, 9)
        offset = code - 9 * block
        bit = jnp.where(p < count_ref[0, 0], lax.shift_left(1, offset), 0)
        mask = mask + jnp.where(block_id == block, bit, 0)
        over = lax.shift_right_logical(offset * 11, 5)
        far = block + over - 1
        inside = (bit > 0) & (offset - 3 * over == 1) & (far >= 0) & (far < BX)
        list_ref[n] = block + (far + EX + 1) * 8 + jnp.where(offset == 4, 256, 0)
        n = n + jnp.where(inside, 1, 0)
    for i in range(3):
        list_ref[n + i] = E * 8
    list_ref[END] = n + (n & 1)
    mask = mask.astype(F32)
    for h in range(BX):
        places = [(out_ref, h)]
        if h == 0:
            places.append((first_ref, 0))
        if h == BX - 1:
            places.append((last_ref, 0))
        for ref, i in places:
            for d in range(3):
                ref[i, d : d + 1, :] = pos_ref[h, d]
            ref[i, 3:4, :] = species_ref[h].astype(F32)
            ref[i, 4:5, :] = mask[h : h + 1, :]
            ref[i, 5:8, :] = jnp.zeros((3, 128), F32)


def gather_ext(lo_ref, mid_ref, hi_ref, ext_ref):
    for row, ref in enumerate((lo_ref, mid_ref, hi_ref)):
        for x in range(EX):
            ext_ref[row * EX + x] = ref[x]
    ext_ref[E : E + 8] = jnp.full((8, 8, A), 1.0e4, F32)


def send_masks(ext_ref, maskv_ref, masks_ref, sem):
    for e in range(E):
        maskv_ref[e : e + 1, :] = ext_ref[e, 4:5, :].astype(jnp.int32)
    copy = pltpu.make_async_copy(maskv_ref, masks_ref, sem)
    copy.start()
    return copy


def make_list(parts, masks_ref, list_ref):
    n = jnp.int32(0)
    for pairs, place in zip(parts, (MIDDLE, THIRD, END)):
        held = None
        for own, other, lister, o in sorted(pairs, key=lambda pair: pair[2]):
            if lister != held:
                held, mask = lister, masks_ref[lister, 0]
            list_ref[n] = own + other * 8 + (256 if o == 4 else 0)
            n = n + (lax.shift_right_logical(mask, o) & 1)
        for i in range(3):
            list_ref[n + i] = E * 8
        n = n + (n & 1)
        list_ref[place] = n


def entry(list_ref, p):
    code = list_ref[p]
    own = code & 7
    other = lax.shift_right_logical(code, 3) & 31
    bias = jnp.where(code >= 256, 0, 1024)
    return own, other, bias


def turned_blocks(ext_ref):
    return [ext_ref[0:16].reshape(128, A).T, ext_ref[16:32].reshape(128, A).T]


def spread_lane(turned, e, d):
    lane = 8 * (e % 16) + d
    return jnp.broadcast_to(turned[e // 16][:, lane : lane + 1], (A, 128))


def geometry(col_ref, i, row, r, sign, bias, rows=ROWS):
    off = [sign * (row[d] - col_ref[i, d, pl.ds(r, rows), :]) for d in range(3)]
    squared = off[0] * off[0] + off[1] * off[1] + off[2] * off[2]
    soft = squared + 0.25
    inv = lax.rsqrt(soft)
    s = soft * inv
    taper = jnp.maximum(1.0 - squared * (1.0 / 36.0), 0.0)
    at = lax.broadcasted_iota(jnp.int32, (rows, 128), 0) + (r + bias)
    lane = lax.broadcasted_iota(jnp.int32, (rows, 128), 1)
    taper = jnp.where(at == lane, 0.0, taper)
    u = jnp.minimum(s, 6.25) * (1.0 / SIGMA) - 0.5
    base = taper * jnp.exp(-u * u)
    step = jnp.exp(2.0 * u - 1.0)
    q = [base]
    for k in range(1, K):
        q.append(q[-1] * (step * EXPS[k]))
    return off, inv, taper, u, q


EXPS = [1.0, 1.0, 0.1353352832366127, 0.01831563888873418]


def store_tiles(put, off, inv, taper, q):
    direction = [o * inv for o in off]
    for k in range(K):
        radial = taper * q[k]
        put(0, k, radial.astype(BF16))
        for d in range(3):
            put(1 + d, k, (radial * direction[d]).astype(BF16))


def pull_back(grads, off, inv, taper, u, q):
    direction = [o * inv for o in off]
    s0 = s1 = None
    dg = [None] * 3
    for k in reversed(range(K)):
        tilted = [grads(1 + d, k) for d in range(3)]
        along = tilted[0] * direction[0] + tilted[1] * direction[1] + tilted[2] * direction[2]
        p = (grads(0, k) + along) * q[k]
        s0 = p if s0 is None else s0 + p
        if k:
            s1 = s0 if s1 is None else s1 + s0
        for d in range(3):
            v = tilted[d] * q[k]
            dg[d] = v if dg[d] is None else dg[d] + v
    turn = dg[0] * direction[0] + dg[1] * direction[1] + dg[2] * direction[2]
    bend = (2.0 / SIGMA) * (u * s0 - s1) + turn * inv
    pull = taper * inv
    weight = s0 * (1.0 / 9.0) + pull * bend
    return [dg[d] * pull - weight * off[d] for d in range(3)]


def rows_of(ext_ref, e):
    return [ext_ref[e, d : d + 1, :] for d in range(3)]


def scaled(feature, weights_ref, k):
    return (feature.astype(F32) * weights_ref[k : k + 1, :]).astype(BF16)


def first_sums(
    end, list_ref, col_ref, near, rows, where, scaled_s_ref, scaled_v_ref, acc_ref, tile_a_ref,
    tile_b_ref,
):
    def first_tiles(p, tile_ref, r):
        own, other, bias = entry(list_ref, p)
        row = rows(where(other))
        off, inv, taper, u, q = geometry(col_ref, own + near, row, r, 1.0, bias)

        def put(g, k, tile):
            tile_ref[pl.ds(g * A + r, ROWS), pl.ds(k * A, A)] = tile

        store_tiles(put, off, inv, taper, q)

    def first_sum(p, tile_ref, g):
        own, other, _ = entry(list_ref, p)
        part = pl.ds(g * A, A)
        acc_ref[own, part, :] += dot(tile_ref[part, :], (scaled_v_ref if g else scaled_s_ref)[where(other)])

    def first_half(p, this_ref, next_ref):
        for g in range(4):
            first_sum(p, this_ref, g)
            for r in range(g * 32, g * 32 + 32, ROWS):
                first_tiles(p + 1, next_ref, r)

    def first(i, carry):
        first_half(2 * i, tile_a_ref, tile_b_ref)
        first_half(2 * i + 1, tile_b_ref, tile_a_ref)
        return carry

    for r in range(0, A, ROWS):
        first_tiles(0, tile_a_ref, r)
    lax.fori_loop(0, half(end), first, 0)


def own_kernel(
    own_ref, list_ref,
    acc_ref,
    ext_ref, col_ref, scaled_s_ref, scaled_v_ref, tile_a_ref, tile_b_ref,
):
    ws1_ref, wv1_ref, _, _, _ = radial_parts(own_ref)
    table = table_part(own_ref)
    for h in range(BX):
        ext_ref[h] = own_ref[h]
    ext_ref[BX] = jnp.full((8, A), 1.0e4, F32)
    for h in range(BX + 1, 16):
        ext_ref[h] = jnp.zeros((8, A), F32)
    turned = [ext_ref[0:16].reshape(128, A).T]
    lanes = lax.broadcasted_iota(jnp.int32, (A, 128), 1).astype(F32)
    acc_ref[...] = jnp.zeros_like(acc_ref)
    for h in range(BX):
        for d in range(3):
            col_ref[h, d] = spread_lane(turned, h, d)
        hot = (spread_lane(turned, h, 3) == lanes).astype(BF16)
        initial = dot(hot, table).astype(BF16)
        for k in range(K):
            scaled_s_ref[h, pl.ds(k * A, A), :] = scaled(initial, ws1_ref, k)
            scaled_v_ref[h, pl.ds(k * A, A), :] = scaled(initial, wv1_ref, k)
    scaled_s_ref[BX] = jnp.zeros((K * A, C), BF16)
    scaled_v_ref[BX] = jnp.zeros((K * A, C), BF16)
    first_sums(
        list_ref[END], list_ref, col_ref, 0, lambda e: rows_of(ext_ref, e),
        lambda e: jnp.minimum(e - EX - 1, BX), scaled_s_ref, scaled_v_ref, acc_ref, tile_a_ref,
        tile_b_ref,
    )


def forward_kernel(
    lo_ref, mid_ref, hi_ref, acc_own_ref, radial_ref, square_ref,
    pre_ref, feat_ref, out_lo_ref, out_hi_ref, scaled_s_ref, scaled_v_ref, ready_ref, keep_col_ref,
    list1_ref, list2_ref,
    ext_ref, col_ref, init_ref, acc_ref, tile_a_ref, tile_b_ref, wide_a_ref, wide_b_ref, total_ref,
    maskv_ref, masks_ref, sem,
):
    ws1_ref, wv1_ref, ws2_ref, wv2_ref, _ = radial_parts(radial_ref)
    ms_ref, mv_ref, _ = square_parts(square_ref)
    table = table_part(radial_ref)
    gather_ext(lo_ref, mid_ref, hi_ref, ext_ref)
    copy = send_masks(ext_ref, maskv_ref, masks_ref, sem)
    turned = turned_blocks(ext_ref)
    lanes = lax.broadcasted_iota(jnp.int32, (A, 128), 1).astype(F32)
    for e in range(E):
        if e == 8:
            copy.wait()
            make_list(HOME_PAIRS, masks_ref, list1_ref)
            make_list(FAR_PAIRS, masks_ref, list2_ref)
        for d in range(3):
            column = spread_lane(turned, e, d)
            col_ref[e, d] = column
            if EX <= e < 2 * EX:
                keep_col_ref[e - EX, d] = column
        hot = (spread_lane(turned, e, 3) == lanes).astype(BF16)
        initial = dot(hot, table).astype(BF16)
        if EX < e <= EX + BX:
            init_ref[e] = initial
        for k in range(K):
            scaled_s_ref[e, pl.ds(k * A, A), :] = scaled(initial, ws1_ref, k)
            scaled_v_ref[e, pl.ds(k * A, A), :] = scaled(initial, wv1_ref, k)
    col_ref[E] = jnp.full((3, A, 128), 1.0e4, F32)
    keep_col_ref[EX] = jnp.full((3, A, 128), 1.0e4, F32)
    scaled_s_ref[E] = jnp.zeros((K * A, C), BF16)
    scaled_v_ref[E] = jnp.zeros((K * A, C), BF16)
    acc_ref[...] = acc_own_ref[...]
    total_ref[...] = jnp.zeros_like(total_ref)
    first_sums(
        list1_ref[THIRD], list1_ref, col_ref, EX + 1, lambda e: rows_of(ext_ref, e), lambda e: e,
        scaled_s_ref, scaled_v_ref, acc_ref, tile_a_ref, tile_b_ref,
    )
    for h in range(BX):
        pre = dot((acc_ref[h, 0:A, :] * 0.125).astype(BF16), ms_ref[...])
        pre_ref[h] = pre
        scalar = (init_ref[h + EX + 1].astype(F32) + pre * jax.nn.sigmoid(pre)).astype(BF16)
        vector = dot((acc_ref[h, A : 4 * A, :] * 0.125).astype(BF16), mv_ref[...]).astype(BF16)
        feat_ref[h, 0:A, :] = scalar
        feat_ref[h, A : 4 * A, :] = vector
        for k in range(K):
            ready_ref[h, pl.ds(k * A, A), :] = scaled(scalar, ws2_ref, k)
            for d in range(3):
                ready_ref[h, pl.ds(((1 + d) * K + k) * A, A), :] = scaled(
                    vector[d * A : (d + 1) * A, :], wv2_ref, k
                )
    second_sums(
        0, list2_ref[MIDDLE], list2_ref, col_ref, 0, lambda own: rows_of(ext_ref, own + EX + 1),
        ready_ref, total_ref, wide_a_ref, wide_b_ref,
    )
    for x in range(EX):
        out_lo_ref[x] = total_ref[x].astype(BF16)
        out_hi_ref[x] = total_ref[2 * EX + x].astype(BF16)


def place(other, shift):
    return jnp.minimum(other - shift, EX) if shift else other


def second_sums(
    start, end, list_ref, col_ref, shift, rows, ready_ref, total_ref, wide_a_ref, wide_b_ref
):
    def second_tiles(p, wide_ref, r):
        own, other, bias = entry(list_ref, p)
        row = rows(own)
        off, inv, taper, u, q = geometry(col_ref, place(other, shift), row, r, 1.0, bias)

        def put(g, k, tile):
            wide_ref[pl.ds(r, ROWS), pl.ds((g * K + k) * A, A)] = tile

        store_tiles(put, off, inv, taper, q)

    def second_half(p, this_ref, next_ref):
        own, other, _ = entry(list_ref, p)
        for g in range(4):
            part = pl.ds(g * K * A, K * A)
            total_ref[place(other, shift)] += dot(this_ref[:, part], ready_ref[own, part, :])
            for r in range(g * 32, g * 32 + 32, ROWS):
                second_tiles(p + 1, next_ref, r)

    def second(i, carry):
        second_half(2 * i, wide_a_ref, wide_b_ref)
        second_half(2 * i + 1, wide_b_ref, wide_a_ref)
        return carry

    for r in range(0, A, ROWS):
        second_tiles(start, wide_a_ref, r)
    lax.fori_loop(half(start), half(end), second, 0)


def forward_inner_kernel(
    mid_ref, list2_ref, ready_ref, col_ref, out_ref, wide_a_ref, wide_b_ref, total_ref
):
    total_ref[...] = jnp.zeros_like(total_ref)
    second_sums(
        list2_ref[MIDDLE], list2_ref[END], list2_ref, col_ref, EX,
        lambda own: rows_of(mid_ref, own + 1), ready_ref, total_ref, wide_a_ref, wide_b_ref,
    )
    out_ref[...] = total_ref[0:EX]


def radial_parts(ref):
    return [ref.at[BX + i // 2, pl.ds(K * (i % 2), K if i < 4 else 1), :] for i in range(5)]


def square_parts(ref):
    return [ref.at[pl.ds(C * i, C), :] for i in range(3)]


def table_part(ref):
    return ref[BX + 3 : BX + 3 + C // 8].reshape(C, C).astype(BF16)


def half(n):
    return lax.shift_right_logical(n, 1)


def slope_of(value):
    sigma = jax.nn.sigmoid(value)
    return sigma * (1.0 + value * (1.0 - sigma))


def middle(msg, x, feat_ref, radial_ref, square_ref, energy_ref):
    readout = radial_parts(radial_ref)[4][...]
    mix_ref = square_parts(square_ref)[2]
    pre = dot((msg * 0.125).astype(BF16), mix_ref[...])
    sigma = jax.nn.sigmoid(pre)
    if 1 <= x <= BX:
        part = (feat_ref[x - 1, 0:A, :].astype(F32) + pre * sigma) * readout
        energy_ref[x - 1] = jnp.sum(part.T, axis=0, keepdims=True)
    grad = (readout * (sigma * (1.0 + pre * (1.0 - sigma)))).astype(BF16)
    return dot_nt(grad, mix_ref[...]) * 0.125


def message(mid_ref, below_ref, above_ref, x):
    return mid_ref[x] + below_ref[x].astype(F32) + above_ref[x].astype(F32)


def middle_inner_kernel(
    mid_ref, below_ref, above_ref, ext_mid_ref, list2_ref, feat_ref, col_ref, radial_ref, square_ref,
    energy_ref, second_in_ref, acc_ref, across_ref, down_ref,
    ext_ref, second_ref, cot_s_ref, cot_v_ref, tile_a_ref, tile_b_ref, grad_a_ref, grad_b_ref,
):
    _, _, ws2_ref, wv2_ref, _ = radial_parts(radial_ref)
    for x in range(EX):
        ext_ref[x] = ext_mid_ref[x]
    ext_ref[EX] = jnp.full((8, A), 1.0e4, F32)
    for x in INNER:
        second = middle(
            message(mid_ref, below_ref, above_ref, x), x, feat_ref, radial_ref, square_ref, energy_ref
        )
        second_ref[x] = second
        second_in_ref[x] = second.astype(BF16)
    acc_ref[...] = jnp.zeros_like(acc_ref)
    down_ref[...] = jnp.zeros_like(down_ref)
    across_ref[...] = jnp.zeros_like(across_ref)
    cotangents(second_ref, cot_s_ref, cot_v_ref, 0, ws2_ref, wv2_ref, EARLY)
    second_moves(
        list2_ref[MIDDLE], list2_ref[THIRD], list2_ref, col_ref, EX, lambda e: rows_of(ext_ref, e),
        feat_ref, cot_s_ref, cot_v_ref, acc_ref, across_ref, down_ref, tile_a_ref, tile_b_ref,
        grad_a_ref, grad_b_ref,
    )


def middle_kernel(
    mid_ref, below_ref, above_ref, left_ref, right_ref, feat_ref, radial_ref, square_ref,
    energy_part_ref, second_part_ref,
    energy_ref, second_in_ref, second_own_ref,
):
    for x in OUTER:
        msg = message(mid_ref, below_ref, above_ref, x)
        if x < 2:
            msg = msg + left_ref[x].astype(F32)
        else:
            msg = msg + right_ref[x - EX + 2].astype(F32)
        second = middle(msg, x, feat_ref, radial_ref, square_ref, energy_ref)
        second_own_ref[x] = second
        second_in_ref[x] = second.astype(BF16)
    for x in INNER:
        energy_ref[x - 1] = energy_part_ref[x - 1]
        second_in_ref[x] = second_part_ref[x]
        second_own_ref[x] = second_part_ref[x].astype(F32)


def move(across_ref, own, r, near, own_sign, grad_ref):
    def grads(g, k):
        return grad_ref[pl.ds(g * A + r, ROWS), pl.ds(k * A, A)]

    parts = []
    for d, moved in enumerate(pull_back(grads, *near)):
        if own_sign > 0:
            across_ref[own, d, pl.ds(r, ROWS), :] += moved
        else:
            across_ref[own, d, pl.ds(r, ROWS), :] -= moved
        part = moved[0:8]
        for i in range(8, ROWS, 8):
            part = part + moved[i : i + 8]
        parts.append(part)
    return parts


def add_down(down_ref, other, own_sign, sums):
    for d in range(3):
        down_ref[other, d] -= own_sign * sums[d]


def plus(sums, parts):
    return parts if sums is None else [a + b for a, b in zip(sums, parts)]


def first_moves(
    start, end, list_ref, col_ref, shift, rows, inward_ref, scaled_s_ref, scaled_v_ref, across_ref,
    down_ref, grad_a_ref, grad_b_ref,
):
    def first_grads(p, grad_ref):
        own, other, _ = entry(list_ref, p)
        grad_ref[0:A, :] = dot_nt(inward_ref[own, 0:A, :], scaled_s_ref[other])
        grad_ref[A : 4 * A, :] = dot_nt(inward_ref[own, A : 4 * A, :], scaled_v_ref[other])

    def first_move(p, grad_ref):
        own, other, bias = entry(list_ref, p)
        row = rows(place(other, shift))
        sums = None
        for r in range(0, A, ROWS):
            near = geometry(col_ref, own + 1, row, r, 1.0, bias)
            sums = plus(sums, move(across_ref, own, r, near, -1.0, grad_ref))
        add_down(down_ref, place(other, shift), -1.0, sums)

    def first_back(i, carry):
        p = 2 * i
        first_grads(p + 1, grad_b_ref)
        first_move(p, grad_a_ref)
        first_grads(p + 2, grad_a_ref)
        first_move(p + 1, grad_b_ref)
        return carry

    first_grads(start, grad_a_ref)
    lax.fori_loop(half(start), half(end), first_back, 0)


def line_of(down_ref, across_ref, e, x, d):
    line = jnp.sum(down_ref[e, d], axis=0, keepdims=True)
    if x is not None and 1 <= x <= BX:
        line = line + jnp.sum(across_ref[x - 1, d].T, axis=0, keepdims=True)
    return line


def second_moves(
    start, end, list_ref, col_ref, shift, rows, feat_ref, cot_s_ref, cot_v_ref, acc_ref, across_ref,
    down_ref, tile_a_ref, tile_b_ref, grad_a_ref, grad_b_ref,
):
    def second_grads(p, grad_ref):
        own, other, _ = entry(list_ref, p)
        source = place(other, shift)
        grad_ref[0:A, :] = dot_nt(feat_ref[own, 0:A, :], cot_s_ref[source])
        grad_ref[A : 4 * A, :] = dot_nt(feat_ref[own, A : 4 * A, :], cot_v_ref[source])

    def second_move(p, grad_ref, tile_ref):
        own, other, bias = entry(list_ref, p)
        source = place(other, shift)
        row = rows(source)
        sums = None
        for r in range(0, A, ROWS):
            near = geometry(col_ref, own + 1, row, r, -1.0, bias)
            off, inv, taper, u, q = near

            def put(g, k, tile):
                tile_ref[pl.ds(g * A + r, ROWS), pl.ds(k * A, A)] = tile

            store_tiles(put, off, inv, taper, q)
            sums = plus(sums, move(across_ref, own, r, near, 1.0, grad_ref))
        add_down(down_ref, source, 1.0, sums)

    def second_sum(own, source, tile_ref):
        acc_ref[own, 0:A, :] += dot(tile_ref[0:A, :], cot_s_ref[source])
        acc_ref[own, A : 4 * A, :] += dot(tile_ref[A : 4 * A, :], cot_v_ref[source])

    def second_back(i, carry):
        p = 2 * i
        own, other, _ = entry(list_ref, p)
        second_sum(*carry, tile_b_ref)
        second_grads(p + 1, grad_b_ref)
        second_move(p, grad_a_ref, tile_a_ref)
        second_sum(own, place(other, shift), tile_a_ref)
        second_grads(p + 2, grad_a_ref)
        second_move(p + 1, grad_b_ref, tile_b_ref)
        own, other, _ = entry(list_ref, p + 1)
        return own, place(other, shift)

    empty = EX if shift else E
    for ref in (cot_s_ref, cot_v_ref):
        ref[empty] = jnp.zeros((K * A, C), BF16)
    tile_b_ref[...] = jnp.zeros_like(tile_b_ref)
    second_grads(start, grad_a_ref)
    last = lax.fori_loop(half(start), half(end), second_back, (jnp.int32(0), jnp.int32(empty)))
    second_sum(*last, tile_b_ref)


def cotangents(ref, cot_s_ref, cot_v_ref, first, ws2_ref, wv2_ref, blocks=range(EX)):
    for x in blocks:
        for k in range(K):
            cot_s_ref[first + x, pl.ds(k * A, A), :] = scaled(ref[x], ws2_ref, k)
            cot_v_ref[first + x, pl.ds(k * A, A), :] = scaled(ref[x], wv2_ref, k)


def backward_outer_two_kernel(
    mid_ref, list2_ref, in_mid_ref, feat_ref, col_ref, radial_ref, acc_in_ref, across_in_ref,
    down_in_ref,
    acc_ref, across_ref, down_ref,
    ext_ref, cot_s_ref, cot_v_ref, tile_a_ref, tile_b_ref, grad_a_ref, grad_b_ref,
):
    _, _, ws2_ref, wv2_ref, _ = radial_parts(radial_ref)
    for x in range(EX):
        ext_ref[x] = mid_ref[x]
    ext_ref[EX] = jnp.full((8, A), 1.0e4, F32)
    acc_ref[...] = acc_in_ref[...]
    down_ref[...] = down_in_ref[...]
    across_ref[...] = across_in_ref[...]
    cotangents(in_mid_ref, cot_s_ref, cot_v_ref, 0, ws2_ref, wv2_ref, LATE)
    second_moves(
        list2_ref[THIRD], list2_ref[END], list2_ref, col_ref, EX, lambda e: rows_of(ext_ref, e),
        feat_ref, cot_s_ref, cot_v_ref, acc_ref, across_ref, down_ref, tile_a_ref, tile_b_ref,
        grad_a_ref, grad_b_ref,
    )


def backward_kernel(
    lo_ref, mid_ref, hi_ref, list1_ref, list2_ref, acc_in_ref, across_in_ref, down_in_ref, feat_ref,
    pre_ref, in_lo_ref, in_hi_ref, scaled_s_ref, scaled_v_ref, col_ref, radial_ref, square_ref,
    out_left_ref, out_right_ref, inward_ref, down_ref, across_ref,
    ext_ref, cot_s_ref, cot_v_ref, acc_ref, tile_a_ref, tile_b_ref, grad_a_ref, grad_b_ref,
):
    _, _, ws2_ref, wv2_ref, readout_ref = radial_parts(radial_ref)
    ms_ref, mv_ref, _ = square_parts(square_ref)
    gather_ext(lo_ref, mid_ref, hi_ref, ext_ref)
    acc_ref[...] = acc_in_ref[...]
    across_ref[...] = across_in_ref[...]
    down_ref[0:EX] = jnp.zeros((EX, 3, 8, A), F32)
    down_ref[EX : 2 * EX] = down_in_ref[0:EX]
    down_ref[2 * EX : E + 1] = jnp.zeros((EX + 1, 3, 8, A), F32)
    cotangents(in_lo_ref, cot_s_ref, cot_v_ref, 0, ws2_ref, wv2_ref)
    cotangents(in_hi_ref, cot_s_ref, cot_v_ref, 2 * EX, ws2_ref, wv2_ref)
    second_moves(
        0, list2_ref[MIDDLE], list2_ref, col_ref, 0, lambda e: rows_of(ext_ref, e), feat_ref,
        cot_s_ref, cot_v_ref, acc_ref, across_ref, down_ref, tile_a_ref, tile_b_ref, grad_a_ref,
        grad_b_ref,
    )
    for h in range(BX):
        slope = (readout_ref[...] + acc_ref[h, 0:A, :]) * slope_of(pre_ref[h])
        inward_ref[h, 0:A, :] = (dot_nt(slope.astype(BF16), ms_ref[...]) * 0.125).astype(BF16)
        inward_ref[h, A : 4 * A, :] = (
            dot_nt(acc_ref[h, A : 4 * A, :].astype(BF16), mv_ref[...]) * 0.125
        ).astype(BF16)
    first_moves(
        0, list1_ref[MIDDLE], list1_ref, col_ref, 0, lambda e: rows_of(ext_ref, e), inward_ref,
        scaled_s_ref, scaled_v_ref, across_ref, down_ref, grad_a_ref, grad_b_ref,
    )
    for row in range(3):
        for d in range(3):
            out_left_ref[row, d : d + 1, :] = line_of(down_ref, None, row * EX, None, d)
            out_right_ref[row, d : d + 1, :] = line_of(down_ref, None, row * EX + EX - 1, None, d)


def backward_rows_kernel(
    lo_ref, mid_ref, hi_ref, list1_ref, scaled_s_ref, scaled_v_ref, col_ref, inward_ref, down_in_ref,
    across_in_ref,
    out_lo_ref, out_mid_ref, out_hi_ref,
    ext_ref, grad_a_ref, grad_b_ref, down_ref, across_ref,
):
    gather_ext(lo_ref, mid_ref, hi_ref, ext_ref)
    down_ref[...] = down_in_ref[...]
    across_ref[...] = across_in_ref[...]
    first_moves(
        list1_ref[MIDDLE], list1_ref[THIRD], list1_ref, col_ref, 0, lambda e: rows_of(ext_ref, e),
        inward_ref, scaled_s_ref, scaled_v_ref, across_ref, down_ref, grad_a_ref, grad_b_ref,
    )
    for row, ref in enumerate((out_lo_ref, out_mid_ref, out_hi_ref)):
        for h in range(BX):
            for d in range(3):
                line = line_of(down_ref, across_ref, row * EX + h + 1, h + 1 if row == 1 else None, d)
                ref[h, d : d + 1, :] = line


def backward_inner_kernel(
    mid_ref, list1_ref, scaled_s_ref, scaled_v_ref, col_ref, inward_ref, out_ref,
    ext_ref, grad_a_ref, grad_b_ref, down_ref, across_ref,
):
    for x in range(EX):
        ext_ref[x] = mid_ref[x]
    ext_ref[EX] = jnp.full((8, A), 1.0e4, F32)
    down_ref[...] = jnp.zeros_like(down_ref)
    across_ref[...] = jnp.zeros_like(across_ref)
    first_moves(
        list1_ref[THIRD], list1_ref[END], list1_ref, col_ref, EX, lambda e: rows_of(ext_ref, e),
        inward_ref, scaled_s_ref, scaled_v_ref, across_ref, down_ref, grad_a_ref, grad_b_ref,
    )
    for x in range(EX):
        for d in range(3):
            out_ref[x, d : d + 1, :] = line_of(down_ref, across_ref, x, x, d)


VMEM = pl.BlockSpec(memory_space=pltpu.VMEM)
SMEM = pl.BlockSpec(memory_space=pltpu.SMEM)
PARAMS = pltpu.CompilerParams(vmem_limit_bytes=28 * 1024 * 1024)


SEM = pltpu.SemaphoreType.DMA


def forward_call(*args):
    return call(
        forward_kernel,
        args,
        [
            ((BX, A, C), F32),
            ((BX, 4 * A, C), BF16),
            ((EX, A, C), BF16),
            ((EX, A, C), BF16),
            ((E + 1, K * A, C), BF16),
            ((E + 1, K * A, C), BF16),
            ((BX, 4 * K * A, C), BF16),
            ((EX + 1, 3, A, 128), F32),
            ((64,), jnp.int32),
            ((64,), jnp.int32),
        ],
        [
            pltpu.VMEM((E + 8, 8, A), F32),
            pltpu.VMEM((E + 1, 3, A, 128), F32),
            pltpu.VMEM((E, A, C), BF16),
            pltpu.VMEM((BX, 4 * A, C), F32),
            pltpu.VMEM((4 * A, K * A), BF16),
            pltpu.VMEM((4 * A, K * A), BF16),
            pltpu.VMEM((A, 4 * K * A), BF16),
            pltpu.VMEM((A, 4 * K * A), BF16),
            pltpu.VMEM((E + 1, A, C), F32),
            pltpu.VMEM((E, 128), jnp.int32),
            pltpu.SMEM((E, 128), jnp.int32),
            SEM,
        ],
        out_specs=[VMEM] * 8 + [SMEM] * 2,
    )


def forward_inner_call(*args):
    return call(
        forward_inner_kernel,
        args,
        [((EX, A, C), F32)],
        [
            pltpu.VMEM((A, 4 * K * A), BF16),
            pltpu.VMEM((A, 4 * K * A), BF16),
            pltpu.VMEM((EX + 1, A, C), F32),
        ],
        in_specs=[VMEM, SMEM, VMEM, VMEM],
        cost=pl.CostEstimate(flops=4 * 10**9, bytes_accessed=10**6, transcendentals=0),
    )


LONG = pl.CostEstimate(flops=4 * 10**9, bytes_accessed=10**6, transcendentals=0)
HELD = [((BX, 4 * A, C), F32), ((BX, 3, A, 128), F32), ((EX + 1, 3, 8, A), F32)]
ROW_SCRATCH = [
    pltpu.VMEM((EX + 1, K * A, C), BF16),
    pltpu.VMEM((EX + 1, K * A, C), BF16),
    pltpu.VMEM((4 * A, K * A), BF16),
    pltpu.VMEM((4 * A, K * A), BF16),
    pltpu.VMEM((4 * A, K * A), F32),
    pltpu.VMEM((4 * A, K * A), F32),
]


def own_call(*args):
    return call(
        own_kernel,
        args,
        [((BX, 4 * A, C), F32)],
        [
            pltpu.VMEM((16, 8, A), F32),
            pltpu.VMEM((BX, 3, A, 128), F32),
            pltpu.VMEM((BX + 1, K * A, C), BF16),
            pltpu.VMEM((BX + 1, K * A, C), BF16),
            pltpu.VMEM((4 * A, K * A), BF16),
            pltpu.VMEM((4 * A, K * A), BF16),
        ],
        in_specs=[VMEM, SMEM],
        cost=LONG,
    )


def middle_inner_call(*args):
    return call(
        middle_inner_kernel,
        args,
        [((BX, 1, A), F32), ((EX, A, C), BF16), *HELD],
        [pltpu.VMEM((EX + 1, 8, A), F32), pltpu.VMEM((EX, A, C), F32), *ROW_SCRATCH],
        in_specs=[VMEM] * 4 + [SMEM] + [VMEM] * 4,
        cost=LONG,
    )


def backward_outer_two_call(*args):
    return call(
        backward_outer_two_kernel,
        args,
        HELD,
        [pltpu.VMEM((EX + 1, 8, A), F32), *ROW_SCRATCH],
        in_specs=[VMEM, SMEM] + [VMEM] * 7,
        cost=LONG,
    )


def backward_call(*args):
    return call(
        backward_kernel,
        args,
        [
            ((3, 3, A), F32),
            ((3, 3, A), F32),
            ((BX, 4 * A, C), BF16),
            ((E + 1, 3, 8, A), F32),
            ((BX, 3, A, 128), F32),
        ],
        [
            pltpu.VMEM((E + 8, 8, A), F32),
            pltpu.VMEM((E + 1, K * A, C), BF16),
            pltpu.VMEM((E + 1, K * A, C), BF16),
            pltpu.VMEM((BX, 4 * A, C), F32),
            pltpu.VMEM((4 * A, K * A), BF16),
            pltpu.VMEM((4 * A, K * A), BF16),
            pltpu.VMEM((4 * A, K * A), F32),
            pltpu.VMEM((4 * A, K * A), F32),
        ],
        in_specs=[VMEM] * 3 + [SMEM] * 2 + [VMEM] * 12,
    )


def backward_rows_call(*args):
    return call(
        backward_rows_kernel,
        args,
        [((BX, 3, A), F32)] * 3,
        [
            pltpu.VMEM((E + 8, 8, A), F32),
            pltpu.VMEM((4 * A, K * A), F32),
            pltpu.VMEM((4 * A, K * A), F32),
            pltpu.VMEM((E + 1, 3, 8, A), F32),
            pltpu.VMEM((BX, 3, A, 128), F32),
        ],
        in_specs=[VMEM] * 3 + [SMEM] + [VMEM] * 6,
        cost=LONG,
    )


def backward_inner_call(*args):
    return call(
        backward_inner_kernel,
        args,
        [((EX, 3, A), F32)],
        [
            pltpu.VMEM((EX + 1, 8, A), F32),
            pltpu.VMEM((4 * A, K * A), F32),
            pltpu.VMEM((4 * A, K * A), F32),
            pltpu.VMEM((EX + 1, 3, 8, A), F32),
            pltpu.VMEM((BX, 3, A, 128), F32),
        ],
        in_specs=[VMEM, SMEM, VMEM, VMEM, VMEM, VMEM],
        cost=pl.CostEstimate(flops=4 * 10**9, bytes_accessed=10**6, transcendentals=0),
    )


def call(kernel, args, outs, scratch=(), in_specs=None, out_specs=None, cost=None, params=PARAMS):
    return pl.pallas_call(
        kernel,
        out_shape=[jax.ShapeDtypeStruct(s, d) for s, d in outs],
        in_specs=in_specs or [VMEM] * len(args),
        out_specs=out_specs or [VMEM] * len(outs),
        scratch_shapes=list(scratch),
        compiler_params=params,
        cost_estimate=cost,
    )(*args)


def along(block, axis, step):
    size = lax.axis_size(axis)
    return lax.ppermute(block, axis, [(i, i + step) for i in range(size) if 0 <= i + step < size])


def both(lo, hi, axis, step=1):
    return along(lo, axis, step), along(hi, axis, -step)


def local(
    positions, species, pair_codes, pair_count, embed_table, ws1, wv1, ws2, wv2, ms, mv, m2, readout
):
    first, radial, last, own_list, square = call(
        pack_kernel,
        (
            positions.transpose(0, 2, 1, 3), species, pair_codes, pair_count, embed_table, ws1, wv1,
            ws2, wv2, ms, mv, m2, readout.reshape(1, C),
        ),
        [
            ((1, 8, A), F32),
            ((BX + 3 + C // 8, 8, A), F32),
            ((1, 8, A), F32),
            ((64,), jnp.int32),
            ((3 * C, C), BF16),
        ],
        [pltpu.VMEM((C, C), F32)],
        in_specs=[VMEM] * 2 + [SMEM] * 2 + [VMEM] * 9,
        out_specs=[VMEM] * 3 + [SMEM, VMEM],
        params=pltpu.CompilerParams(vmem_limit_bytes=60 * 1024 * 1024),
    )
    left, right = both(last, first, "gx")
    (acc,) = own_call(radial, own_list)
    radial, acc = lax.optimization_barrier((radial, acc))
    ext_mid = jnp.concatenate([left, radial[:BX], right], axis=0)
    ext_lo, ext_hi = both(ext_mid, ext_mid, "gy")
    ext = (ext_lo, ext_mid, ext_hi)
    pre, feat, lo, hi, scaled_s, scaled_v, ready, col, list1, list2 = forward_call(
        *ext, acc, radial, square
    )
    below, above = both(hi, lo, "gy")
    (mid,) = forward_inner_call(ext_mid, list2, ready, col)
    edge = lambda x: (mid[x : x + 2] + below[x : x + 2] + above[x : x + 2]).astype(BF16)
    left, right = both(edge(EX - 2), edge(0), "gx")
    energy, inner, *held = middle_inner_call(
        mid, below, above, ext_mid, list2, feat, col, radial, square
    )
    energy, inner, inner_own = call(
        middle_kernel,
        (mid, below, above, left, right, feat, radial, square, energy, inner),
        [((BX, 1, A), F32), ((EX, A, C), BF16), ((EX, A, C), F32)],
    )
    in_lo, in_hi = both(inner, inner, "gy")
    held = backward_outer_two_call(ext_mid, list2, inner_own, feat, col, radial, *held)
    left, right, inward, down, across = backward_call(
        *ext, list1, list2, *held, feat, pre, in_lo, in_hi, scaled_s, scaled_v, col, radial, square
    )
    left, right = both(right, left, "gx")
    lo, mid, hi = backward_rows_call(
        *ext, list1, scaled_s, scaled_v, col, inward, down, across
    )
    pad = lambda row: jnp.concatenate(
        [left[row : row + 1], jnp.zeros((BX - 2, 3, A), F32), right[row : row + 1]], axis=0
    )
    lo, hi = lo + pad(0), hi + pad(2)
    below, above = both(hi, lo, "gy")
    (more,) = backward_inner_call(ext_mid, list1, scaled_s, scaled_v, col, inward)
    total = mid + pad(1) + below + above + more[1 : BX + 1]
    return energy, -total.reshape(BX, 1, 3, A)


def solution(mesh):
    in_specs = (
        P("gx", "gy", None, None),
        P("gx", "gy", None),
        P("gx", "gy", None),
        P("gx", "gy"),
        *[P()] * 9,
    )
    out_specs = (P("gx", "gy", None), P("gx", "gy", None, None))
    return jax.shard_map(local, mesh=mesh, in_specs=in_specs, out_specs=out_specs, check_vma=False)
```
